32 devices in a mesh: section: 2 (over core), dp: 4 (over z), mp: 4 (over y, x).
Axes of the slice: x: 2, y: 2, z: 4, core: 2. Of those that a mesh axis runs over, the one named last changes fastest.
Arguments:
- events: bfloat16 [32, 1024, 512], P(('section', 'dp', 'mp')), may hold values from -6 to 6
- hist_len: int32 [32], P(('section', 'dp', 'mp')), may hold values from 256 to 1024, as said below
- sess_len: int32 [32, 32], P(('section', 'dp', 'mp')), may hold values from 1 to 64, 1024 in all within a row
- w_uvqk: bfloat16 [512, 2048], P('dp'), may hold values from -0.25 to 0.25
- w_out: bfloat16 [512, 512], P('dp'), may hold values from -0.25 to 0.25
- attn_gain: float32 [512], replicated, may hold values from 0.1 to 1.9
- w_in: bfloat16 [512, 4096], P(None, ('section', 'mp')), may hold values from -2 to 2
- ffn_gain: bfloat16 [1, 4096], P(None, ('section', 'mp')), may hold values from 0.099609375 to 1.8984375
- w_up: bfloat16 [4096, 8192], P('section', 'mp'), may hold values from -0.09375 to 0.09375
- w_down: bfloat16 [8192, 4096], P('mp', 'section'), may hold values from -0.0625 to 0.0625
Outputs:
- pooled: bfloat16 [1024, 512], P(('section', 'dp', 'mp'))
- cross_out: bfloat16 [256, 4096], P(('section', 'dp', 'mp'))
The draws below stay inside these ranges and needn't reach their ends.
Inputs may be any that keep to these rules, and one draw needn't show every extreme that they name: `hist_len`: some user has all 1024 events valid. `sess_len`: a user's 32 sessions cover all 1024 positions; some session has exactly 64 events.
All inputs are finite; a program needn't handle non-finite values.
Results may differ from the reference program's by a relative error of at most 0.015.
Values may be sent and summed in bfloat16 or wider, within the bound.
No kernel may reach another device: no remote copies, remote signals or barrier semaphores. Data moves between devices by JAX's collectives and lax.ppermute only.
A program may use at most 64 MiB of HBM per device.

```python
import math
import jax
import jax.numpy as jnp
import numpy as np
from jax import lax

E = 512
HEADS = 4
DM = 4096
FF = 8192
SESS = 32
MICRO = 4
SESS_MAX = 64
L = 1024
USERS = 32


def draw_hist_len(key, part):
    drawn = jax.random.randint(key, (USERS,), L // 4, L + 1, dtype=jnp.int32)
    return drawn.at[0].set(L).at[1].set(L // 4)


def draw_w_in(key, part):
    key_base, key_col = jax.random.split(jax.random.fold_in(key, 7), 2)
    columns = jnp.arange(DM, dtype=jnp.float32)
    jitter = jax.random.uniform(key_col, (DM,), jnp.float32, 0.0, 1.0)
    col_scale = 10.0 ** ((columns + DM * 0.125 * jitter) / (DM * 1.125))
    base_draw = jnp.clip(jax.random.normal(key_base, (E, DM), jnp.float32), -4.0, 4.0)
    scaled = base_draw * col_scale[None, :] * E ** (-0.5)
    return jnp.clip(scaled, -2.0, 2.0).astype(jnp.bfloat16)


def level_of(own_key, dims, cuts, low, high):
    level = 1.0
    for axis_at, blocks in cuts:
        draws = jax.random.uniform(jax.random.fold_in(jax.random.fold_in(own_key, 6), axis_at), (blocks,), jnp.float32, low / len(cuts), high / len(cuts))
        level = level * jnp.repeat(jnp.exp(draws), dims[axis_at] // blocks).reshape((-1,) + (1,) * (len(dims) - 1 - axis_at))
    return level


def split_up(number_of, total, most, skew):
    loads = [(1 << 20) // math.isqrt(rank ** skew) + 1 for rank in range(2, number_of + 1)]
    spare, given = total - most - (number_of - 1), [1] * (number_of - 1)
    while spare > 0:
        candidates = [i for i in range(number_of - 1) if given[i] < most]
        mass, left = sum([loads[i] for i in candidates]), spare
        for i in candidates:
            more = min(most - given[i], max(1, left * loads[i] // mass), spare)
            given[i] = given[i] + more
            spare = spare - more
    return np.array([most] + given)


def ragged_sizes(rng, number_of, total, bound, skew):
    if number_of == 2:
        one = jax.random.randint(rng, (), max(1, total - bound), min(bound, total - 1) + 1)
        return jnp.stack([one, total - one])
    lengths = jnp.asarray(split_up(number_of, total, bound, skew), jnp.int32)
    twos = (number_of - 1) // 2
    donor, sink = lengths[1:1 + 2 * twos:2], lengths[2:2 + 2 * twos:2]
    margin = jnp.minimum(donor - 1, bound - sink)
    shifted = jax.random.randint(jax.random.fold_in(rng, 1), (twos,), 0, 1 << 20) % (margin + 1)
    lengths = lengths.at[1:1 + 2 * twos:2].set(donor - shifted).at[2:2 + 2 * twos:2].set(sink + shifted)
    return lengths[jax.random.permutation(jax.random.fold_in(rng, 2), number_of)]


def gaussian(key, extent, deviation, bound, cuts=(), kind=jnp.bfloat16):
    entries = jax.random.normal(key, extent, jnp.float32) * deviation
    if len(cuts) > 0:
        entries = level_of(key, extent, cuts, -0.22, 0.18) * entries
    return jnp.clip(entries, min=-bound, max=bound).astype(kind)


def setup_inputs(seed: int = 0) -> dict:
    keys = jax.random.split(jax.random.key(seed), 11)
    return {
        "events": gaussian(keys[0], (USERS, L, E), 1.0, 6.0, ((0, 32),)),
        "hist_len": draw_hist_len(jax.random.fold_in(keys[10], 71), 0),
        "sess_len": jax.vmap(lambda own: ragged_sizes(own, SESS, SESS * 32, SESS_MAX, 1))(jax.random.split(keys[2], USERS)).reshape((USERS, SESS)).astype(jnp.int32),
        "w_uvqk": gaussian(keys[3], (E, 4 * E), E ** -0.5, 0.25, ((0, 4),)),
        "w_out": gaussian(keys[4], (E, E), E ** -0.5, 0.25, ((0, 4),)),
        "attn_gain": jnp.clip(1.0 + 0.18 * jax.random.normal(keys[5], (E,), jnp.float32), 0.1, 1.9),
        "w_in": draw_w_in(jax.random.fold_in(keys[10], 71), 0),
        "ffn_gain": jnp.clip(1.0 + 0.18 * jax.random.normal(keys[7], (1, DM), jnp.float32), 0.099609375, 1.8984375).astype(jnp.bfloat16),
        "w_up": gaussian(keys[8], (DM, FF), DM ** -0.5, 0.09375, ((0, 2), (1, 4))),
        "w_down": gaussian(keys[9], (FF, DM), FF ** -0.5, 0.0625, ((0, 4), (1, 2))),
    }


EPSILON = 1e-06

def encode_user(tokens, valid_len, w_uvqk, w_out, norm_gain):
    length, model_width = tokens.shape
    head_dim = model_width // HEADS
    projected = jnp.dot(tokens, w_uvqk, preferred_element_type=jnp.float32)
    activated = jax.nn.silu(projected)
    gate_part = activated[:, :model_width]
    values = activated[:, model_width:2 * model_width].astype(jnp.bfloat16)
    queries = activated[:, 2 * model_width:3 * model_width].astype(jnp.bfloat16)
    key_vecs = activated[:, 3 * model_width:].astype(jnp.bfloat16)
    values, queries, key_vecs = lax.optimization_barrier((values, queries, key_vecs))
    key_heads = key_vecs.reshape(length, HEADS, head_dim).astype(jnp.float32)
    value_heads = values.reshape(length, HEADS, head_dim).astype(jnp.float32)
    block_rows = min(length, 512)
    columns = jnp.arange(length, dtype=jnp.int32)
    outputs = []
    for block_index in range(length // block_rows):
        query_heads = queries[block_index * block_rows:(block_index + 1) * block_rows]
        query_heads = query_heads.reshape(block_rows, HEADS, head_dim).astype(jnp.float32)
        scores = jnp.einsum('ihd,jhd->hij', query_heads, key_heads) * head_dim ** (-0.5)
        rows_at = block_index * block_rows + jnp.arange(block_rows, dtype=jnp.int32)
        visible = (columns[None, :] <= rows_at[:, None]) & (columns[None, :] < valid_len)
        weights = jnp.where(visible[None], jax.nn.silu(scores), 0.0).astype(jnp.bfloat16)
        weights = lax.optimization_barrier(weights)
        mixed_heads = jnp.einsum('hij,jhd->ihd', weights.astype(jnp.float32), value_heads)
        outputs.append(mixed_heads.reshape(block_rows, model_width))
    attended = jnp.concatenate(outputs, axis=0)
    inv_rms = lax.rsqrt(lax.optimization_barrier(jnp.mean(attended * attended, axis=1, keepdims=True)) + EPSILON)
    gated_out = (attended * inv_rms * norm_gain.astype(jnp.float32) * gate_part).astype(jnp.bfloat16)
    return tokens.astype(jnp.float32) + jnp.dot(gated_out, w_out, preferred_element_type=jnp.float32)

def pool_sessions(enc_state, valid_len, sess_lens):
    length = enc_state.shape[0]
    sess_ends = jnp.cumsum(sess_lens).astype(jnp.int32)
    sess_starts = sess_ends - sess_lens.astype(jnp.int32)
    positions = jnp.arange(length, dtype=jnp.int32)
    membership = ((positions[None, :] >= sess_starts[:, None]) & (positions[None, :] < sess_ends[:, None]) & (positions[None, :] < valid_len)).astype(jnp.float32)
    sess_sums = jnp.dot(membership, enc_state, precision=lax.Precision.HIGHEST)
    sess_counts = lax.optimization_barrier(jnp.sum(membership, axis=1, keepdims=True))
    return (sess_sums / jnp.maximum(sess_counts, 1.0)).astype(jnp.bfloat16)

def reference(events, hist_len, sess_len, w_uvqk, w_out, attn_gain, w_in, ffn_gain, w_up, w_down):

    def one_user(user_items):
        tokens, valid_len, sess_lens = user_items
        enc_state = encode_user(tokens, valid_len, w_uvqk, w_out, attn_gain)
        return pool_sessions(enc_state, valid_len, sess_lens)
    pooled = lax.map(one_user, (events, hist_len, sess_len))
    micro_count = SESS // MICRO
    micro_rows = pooled[:, :micro_count].reshape(USERS * micro_count, E)
    hidden_in = jnp.dot(micro_rows, w_in, preferred_element_type=jnp.float32)
    inv_rms = lax.rsqrt(lax.optimization_barrier(jnp.mean(hidden_in * hidden_in, axis=1, keepdims=True)) + EPSILON)
    normed = (hidden_in * inv_rms * ffn_gain.astype(jnp.float32)).astype(jnp.bfloat16)
    up_proj = jnp.dot(normed, w_up, preferred_element_type=jnp.float32)
    hidden = jax.nn.gelu(up_proj, approximate=True).astype(jnp.bfloat16)
    cross_out = (hidden_in + jnp.dot(hidden, w_down, preferred_element_type=jnp.float32)).astype(jnp.bfloat16)
    return (pooled.reshape(USERS * SESS, E), cross_out)
```

```python
import functools

import jax
import jax.numpy as jnp
from jax import lax
from jax.experimental import pallas as pl
from jax.experimental.pallas import tpu as pltpu
from jax.sharding import PartitionSpec as P

HEADS = 4
DM = 4096
MICRO = 4
SESS_MAX = 64
EPSILON = 1e-06
F32 = jnp.float32
BF16 = jnp.bfloat16

VMEM = pl.BlockSpec(memory_space=pltpu.VMEM)
SMEM = pl.BlockSpec(memory_space=pltpu.SMEM)
ANY = pl.BlockSpec(memory_space=pl.ANY)


def params(mib):
    return pltpu.CompilerParams(vmem_limit_bytes=mib * 1024 * 1024)


def swap(x, axis, size, flip):
    return lax.ppermute(x, axis, [(i, i ^ flip) for i in range(size)])


def silu_half(h):
    return h + h * jnp.tanh(h)


def encoder_rows(place, counts, row0, first_out, *refs):
    refs = list(refs)
    hist_ref, sess_ref, ev_ref, gain_ref = refs[:4]
    refs = refs[4:]
    n_w, n_wout, n_kv = counts
    w_in_refs, refs = refs[:n_w], refs[n_w:]
    wout_in_refs, refs = refs[:n_wout], refs[n_wout:]
    kv_refs, refs = refs[:n_kv], refs[n_kv:]
    if n_kv:
        sums_ref, refs = refs[0], refs[1:]
    pooled_ref, kv_out, sums_out = refs[:3]
    w_ref, wout_ref, q_ref, gate_ref, att_ref, sems = refs[3:]
    rows, width = ev_ref.shape
    head = width // HEADS
    hist = hist_ref[0]
    copies = place(w_in_refs, wout_in_refs, w_ref, wout_ref, sems)
    for c in copies:
        c.start()

    sess = sess_ref.shape[1]
    lens = jnp.broadcast_to(sess_ref[...], (sess, sess))
    at_row = lax.broadcasted_iota(jnp.int32, (sess, sess), 0)
    at_col = lax.broadcasted_iota(jnp.int32, (sess, sess), 1)
    ends = jnp.sum(jnp.where(at_col <= at_row, lens, 0).astype(F32), axis=1, keepdims=True)
    starts = jnp.sum(jnp.where(at_col < at_row, lens, 0).astype(F32), axis=1, keepdims=True)
    ends = jnp.minimum(ends, hist.astype(F32))
    pos = (lax.broadcasted_iota(jnp.int32, (sess, rows), 1) + row0).astype(F32)
    member = jnp.where((pos >= starts) & (pos < ends), 1.0, 0.0).astype(BF16)
    n_valid = jnp.maximum(ends - starts, 0.0)

    for c in copies:
        c.wait()

    step = min(rows, 256)
    for r in range(0, rows, step):
        x = ev_ref[r : r + step, :]
        at = slice(r, r + step)
        row_pos = lax.broadcasted_iota(jnp.int32, (step, 1), 0) + (row0 + r)

        def act(n):
            part = jnp.dot(x, w_ref[:, n * width : (n + 1) * width], preferred_element_type=F32)
            return silu_half(part * 0.5)

        gate_ref[at, :] = act(0)
        kv_out[at, :width] = jnp.where(row_pos < hist, act(1), 0.0).astype(BF16)
        q_ref[at, :] = act(2).astype(BF16)
        kv_out[at, width:] = act(3).astype(BF16)

    blocks = []
    for ref in list(kv_refs) + [kv_out]:
        for r in range(0, ref.shape[0], step):
            blocks.append((ref, r))
    tri = lax.broadcasted_iota(jnp.int32, (step, step), 1) <= lax.broadcasted_iota(
        jnp.int32, (step, step), 0
    )
    before = len(blocks) - rows // step
    for i in range(rows // step):
        at = slice(i * step, (i + 1) * step)
        for h in range(HEADS):
            q = q_ref[at, h * head : (h + 1) * head]
            total = None
            for j in range(before + i + 1):
                ref, r = blocks[j]
                k = ref[r : r + step, width + h * head : width + (h + 1) * head]
                v = ref[r : r + step, h * head : (h + 1) * head]
                s = lax.dot_general(q, k, (((1,), (1,)), ((), ())), preferred_element_type=F32)
                wts = silu_half(s * (0.5 * head**-0.5))
                if j == before + i:
                    wts = jnp.where(tri, wts, 0.0)
                mixed = jnp.dot(wts.astype(BF16), v, preferred_element_type=F32)
                total = mixed if total is None else total + mixed
            att_ref[at, h * head : (h + 1) * head] = total

    sums_ev = jnp.dot(member, ev_ref[...], preferred_element_type=F32)
    att = att_ref[...]
    inv = lax.rsqrt(jnp.mean(att * att, axis=1, keepdims=True) + EPSILON)
    gated = (att * inv * gain_ref[...] * gate_ref[...]).astype(BF16)
    sums_g = jnp.dot(member, gated, preferred_element_type=F32)
    if n_kv:
        sums_ev = sums_ev + sums_ref[:, :width]
        sums_g = sums_g + sums_ref[:, width:]
    sums_out[:, :width] = sums_ev
    sums_out[:, width:] = sums_g

    hi = sums_g.astype(BF16)
    rest = sums_g - hi.astype(F32)
    mid = rest.astype(BF16)
    low = (rest - mid.astype(F32)).astype(BF16)
    terms = jnp.dot(jnp.concatenate([low, mid, hi], axis=0), wout_ref[...], preferred_element_type=F32)
    out = terms[:sess] + terms[sess : 2 * sess] + terms[2 * sess :] + sums_ev
    out = out / jnp.maximum(n_valid, 1.0)
    out = out.astype(BF16).astype(pooled_ref.dtype)
    pooled_ref[...] = out[:first_out]


def encoder_call(events, hist_len, sess_len, gain, place, weights, wouts, kvs, sums, row0, rows, take, dtype):
    width = events.shape[1]
    sess = sess_len.shape[1]
    block = row0 // rows
    prior = list(kvs) + ([sums] if kvs else [])
    specs = (
        [SMEM, VMEM, pl.BlockSpec((rows, width), lambda i: (block, 0)), VMEM]
        + [ANY] * (len(weights) + len(wouts))
        + [VMEM] * len(prior)
    )
    n_sems = 64
    return pl.pallas_call(
        functools.partial(encoder_rows, place, (len(weights), len(wouts), len(kvs)), row0, take),
        grid=(1,),
        in_specs=specs,
        out_specs=[VMEM, VMEM, VMEM],
        out_shape=[
            jax.ShapeDtypeStruct((take, width), dtype),
            jax.ShapeDtypeStruct((rows, 2 * width), BF16),
            jax.ShapeDtypeStruct((sess, 2 * width), F32),
        ],
        scratch_shapes=[
            pltpu.VMEM((width, 4 * width), BF16),
            pltpu.VMEM((width, width), BF16),
            pltpu.VMEM((rows, width), BF16),
            pltpu.VMEM((rows, width), F32),
            pltpu.VMEM((rows, width), F32),
            pltpu.SemaphoreType.DMA((n_sems,)),
        ],
        compiler_params=params(40),
        cost_estimate=pl.CostEstimate(
            flops=2 * rows * width * 4 * width + 4 * rows * (row0 + rows) * width,
            bytes_accessed=6 * 1024 * 1024,
            transcendentals=4 * rows * width + HEADS * rows * (row0 + rows),
        ),
        name=f"encode_rows_{row0}",
    )(hist_len, sess_len, events, gain, *weights, *wouts, *prior)


def gather_weights(w_uvqk, w_out, sections, dps, mps):
    depth, wide = w_uvqk.shape
    peers = sections * mps
    piece = wide // peers
    if wide % (128 * peers) or depth % 16:
        full = lax.all_gather(w_uvqk, "dp", axis=0, tiled=True)
        full_out = lax.all_gather(w_out, "dp", axis=0, tiled=True)

        def place_whole(ws, wouts, w_ref, wout_ref, sems):
            return [
                pltpu.make_async_copy(ws[0], w_ref, sems.at[0]),
                pltpu.make_async_copy(wouts[0], wout_ref, sems.at[1]),
            ]

        return [full], [full_out], place_whole

    s, m = lax.axis_index("section"), lax.axis_index("mp")
    mine = lax.dynamic_slice_in_dim(w_uvqk, (s * mps + m) * piece, piece, 1)
    got = jnp.stack([swap(mine, "dp", dps, k) for k in range(1, dps)])
    plane = [got] + [swap(got, "mp", mps, k) for k in range(1, mps)]
    across = [swap(p, "section", sections, 1) for p in plane] if sections == 2 else []
    wouts = [w_out] + [swap(w_out, "dp", dps, k) for k in range(1, dps)]

    def place(ws, wouts, w_ref, wout_ref, sems):
        z = lax.axis_index("dp")
        sec, col = lax.axis_index("section"), lax.axis_index("mp")
        copies = [pltpu.make_async_copy(ws[0], w_ref.at[pl.ds(pl.multiple_of(z * depth, depth), depth)], sems.at[0])]
        for a, half in enumerate(ws[1 : 1 + mps] and [ws[1 : 1 + mps], ws[1 + mps :]]):
            for j, ref in enumerate(half):
                spot = ((sec ^ a) * mps + (col ^ j)) * piece
                for k in range(1, dps):
                    dst = w_ref.at[
                        pl.ds(pl.multiple_of((z ^ k) * depth, depth), depth),
                        pl.ds(pl.multiple_of(spot, piece), piece),
                    ]
                    copies.append(pltpu.make_async_copy(ref.at[k - 1], dst, sems.at[len(copies)]))
        for k, ref in enumerate(wouts):
            dst = wout_ref.at[pl.ds(pl.multiple_of((z ^ k) * depth, depth), depth)]
            copies.append(pltpu.make_async_copy(ref, dst, sems.at[len(copies)]))
        return copies

    return [w_uvqk] + plane + across, wouts, place


def hidden_in_kernel(peers, mps, *refs):
    parts, (w_ref, gain_ref, local_ref, send_ref, x_ref) = refs[:peers], refs[peers:]
    me = lax.axis_index("section") * mps + lax.axis_index("mp")
    take = parts[0].shape[0]
    for k, ref in enumerate(parts):
        x_ref[pl.ds(pl.multiple_of((me ^ k) * take, take), take), :] = ref[...]
    local = jnp.dot(x_ref[...].astype(BF16), w_ref[...], preferred_element_type=F32)
    local_ref[...] = local
    cols = local.shape[1]
    send_ref[:, :cols] = (local * gain_ref[...].astype(F32)).astype(BF16)
    square = jnp.sum(local * local, axis=1, keepdims=True)
    hi = square.astype(BF16)
    lo = (square - hi.astype(F32)).astype(BF16)
    lane = lax.broadcasted_iota(jnp.int32, (local.shape[0], 128), 1)
    both = jnp.where(lane == 0, hi.astype(F32), jnp.where(lane == 1, lo.astype(F32), 0.0))
    send_ref[:, cols:] = both.astype(BF16)


def up_kernel(mps, chunks, *refs):
    parts, (w_any, half_ref, send_ref, x_ref, w_ref, sems) = refs[:mps], refs[mps:]
    wide = w_ref.shape[1]
    each = wide // chunks
    copies = [
        pltpu.make_async_copy(
            w_any.at[:, c * each : (c + 1) * each], w_ref.at[:, c * each : (c + 1) * each], sems.at[c]
        )
        for c in range(chunks)
    ]
    for c in copies:
        c.start()
    m = lax.axis_index("mp")
    cols = parts[0].shape[1] - 128
    square = None
    for k, ref in enumerate(parts):
        x_ref[:, pl.ds(pl.multiple_of((m ^ k) * cols, cols), cols)] = ref[:, :cols]
        tail = jnp.sum(ref[:, cols:].astype(F32), axis=1, keepdims=True)
        square = tail if square is None else square + tail
    x = x_ref[...]
    for c in range(chunks):
        copies[c].wait()
        at = slice(c * each, (c + 1) * each)
        half = jnp.dot(x, w_ref[:, at], preferred_element_type=F32)
        half_ref[:, at] = half
        send_ref[:, at] = half.astype(BF16)
    hi = square.astype(BF16)
    lo = (square - hi.astype(F32)).astype(BF16)
    lane = lax.broadcasted_iota(jnp.int32, (square.shape[0], 128), 1)
    half_ref[:, wide:] = jnp.broadcast_to(square, (square.shape[0], 128))
    both = jnp.where(lane == 0, hi.astype(F32), jnp.where(lane == 1, lo.astype(F32), 0.0))
    send_ref[:, wide:] = both.astype(BF16)


def down_kernel(chunks, half_ref, other_ref, local_ref, w_any, out_ref, part_ref, w_ref, sems):
    wide = w_ref.shape[1]
    each = wide // chunks
    copies = [
        pltpu.make_async_copy(
            w_any.at[:, c * each : (c + 1) * each], w_ref.at[:, c * each : (c + 1) * each], sems.at[c]
        )
        for c in range(chunks)
    ]
    for c in copies:
        c.start()
    units = w_ref.shape[0]
    square = half_ref[:, units : units + 1] + jnp.sum(other_ref[:, units:].astype(F32), axis=1, keepdims=True)
    inv = lax.rsqrt(square / DM + EPSILON)
    up = (half_ref[:, :units] + other_ref[:, :units].astype(F32)) * inv
    hidden = jax.nn.gelu(up, approximate=True).astype(BF16)
    for c in range(chunks):
        copies[c].wait()
        at = slice(c * each, (c + 1) * each)
        part_ref[:, at] = jnp.dot(hidden, w_ref[:, at], preferred_element_type=F32)
    m = lax.axis_index("mp")
    cols = local_ref.shape[1]
    own = pl.ds(pl.multiple_of(m * cols, cols), cols)
    part_ref[:, own] = part_ref[:, own] + local_ref[...]
    out_ref[...] = part_ref[...].astype(BF16)


def sum_kernel(sections, mps, got_ref, out_ref):
    got = got_ref[...].astype(F32)
    take, wide = out_ref.shape[0], got.shape[1]
    for s in range(sections):
        total = got[s * mps * take : (s * mps + 1) * take]
        for k in range(s * mps + 1, (s + 1) * mps):
            total = total + got[k * take : (k + 1) * take]
        out_ref[:, s * wide : (s + 1) * wide] = total.astype(BF16)


def cross_block(micro_rows, w_in, ffn_gain, w_up, w_down, sections, mps):
    peers = sections * mps
    take, width = micro_rows.shape
    rows = take * peers
    cols = w_in.shape[1]
    units = w_up.shape[1]
    half_width = w_down.shape[1]
    group = ("section", "mp")

    parts = [micro_rows] + [swap(micro_rows, group, peers, k) for k in range(1, peers)]
    local, send = pl.pallas_call(
        functools.partial(hidden_in_kernel, peers, mps),
        out_shape=[
            jax.ShapeDtypeStruct((rows, cols), F32),
            jax.ShapeDtypeStruct((rows, cols + 128), BF16),
        ],
        in_specs=[VMEM] * (peers + 2),
        out_specs=[VMEM] * 2,
        scratch_shapes=[pltpu.VMEM((rows, width), F32)],
        compiler_params=params(16),
        cost_estimate=pl.CostEstimate(
            flops=2 * rows * width * cols, bytes_accessed=2 * width * cols, transcendentals=0
        ),
        name="hidden_in",
    )(*parts, w_in, ffn_gain)

    got = [send] + [swap(send, "mp", mps, k) for k in range(1, mps)]
    chunks = 4
    half, half_send = pl.pallas_call(
        functools.partial(up_kernel, mps, chunks),
        out_shape=[
            jax.ShapeDtypeStruct((rows, units + 128), F32),
            jax.ShapeDtypeStruct((rows, units + 128), BF16),
        ],
        in_specs=[VMEM] * mps + [ANY],
        out_specs=[VMEM] * 2,
        scratch_shapes=[
            pltpu.VMEM((rows, cols * mps), BF16),
            pltpu.VMEM(w_up.shape, BF16),
            pltpu.SemaphoreType.DMA((chunks,)),
        ],
        compiler_params=params(32),
        cost_estimate=pl.CostEstimate(
            flops=2 * rows * w_up.size, bytes_accessed=2 * w_up.size, transcendentals=0
        ),
        name="up_half",
    )(*got, w_up)

    other = swap(half_send, "section", sections, 1)
    partial = pl.pallas_call(
        functools.partial(down_kernel, chunks),
        out_shape=jax.ShapeDtypeStruct((rows, half_width), BF16),
        in_specs=[VMEM] * 3 + [ANY],
        out_specs=VMEM,
        scratch_shapes=[
            pltpu.VMEM((rows, half_width), F32),
            pltpu.VMEM(w_down.shape, BF16),
            pltpu.SemaphoreType.DMA((chunks,)),
        ],
        compiler_params=params(32),
        cost_estimate=pl.CostEstimate(
            flops=2 * rows * w_down.size, bytes_accessed=2 * w_down.size, transcendentals=rows * units
        ),
        name="down_part",
    )(half, other, local, w_down)

    arrived = lax.all_to_all(partial.reshape(peers, take, half_width), group, split_axis=0, concat_axis=0, tiled=True)
    return pl.pallas_call(
        functools.partial(sum_kernel, sections, mps),
        out_shape=jax.ShapeDtypeStruct((take, half_width * sections), BF16),
        in_specs=[VMEM],
        out_specs=VMEM,
        compiler_params=params(16),
        name="sum_rows",
    )(arrived.reshape(rows, half_width))


def per_device(sections, dps, mps, events, hist_len, sess_len, w_uvqk, w_out, attn_gain, w_in, ffn_gain, w_up, w_down):
    events = events[0]
    length, width = events.shape
    sess = sess_len.shape[1]
    micro_count = sess // MICRO
    gain = attn_gain.reshape(1, width)
    weights, wouts, place = gather_weights(w_uvqk, w_out, sections, dps, mps)
    encode = functools.partial(encoder_call, events, hist_len, sess_len, gain, place, weights, wouts)

    first = min(length, micro_count * SESS_MAX)
    micro_rows, kv, sums = encode([], None, 0, first, micro_count, F32)
    cross_out = cross_block(micro_rows, w_in, ffn_gain, w_up, w_down, sections, mps)

    kvs, row0, step = [kv], first, 256
    pooled = None
    while row0 < length:
        pooled, kv, sums = encode(kvs, sums, row0, step, sess, BF16)
        kvs.append(kv)
        row0 += step
    return (pooled, cross_out)


def solution(mesh):
    sizes = [mesh.shape[name] for name in ("section", "dp", "mp")]
    return jax.shard_map(
        functools.partial(per_device, *sizes),
        mesh=mesh,
        in_specs=(
            P(("section", "dp", "mp"), None, None),
            P(("section", "dp", "mp")),
            P(("section", "dp", "mp"), None),
            P("dp", None),
            P("dp", None),
            P(),
            P(None, ("section", "mp")),
            P(None, ("section", "mp")),
            P("section", "mp"),
            P("mp", "section"),
        ),
        out_specs=(P(("section", "dp", "mp"), None), P(("section", "dp", "mp"), None)),
        check_vma=False,
    )
```

```python
import functools

import jax
import jax.numpy as jnp
from jax import lax
from jax.experimental import pallas as pl
from jax.experimental.pallas import tpu as pltpu
from jax.sharding import PartitionSpec as P

HEADS = 4
DM = 4096
MICRO = 4
SESS_MAX = 64
EPSILON = 1e-06
F32 = jnp.float32
BF16 = jnp.bfloat16

VMEM = pl.BlockSpec(memory_space=pltpu.VMEM)
SMEM = pl.BlockSpec(memory_space=pltpu.SMEM)
HBM = pl.BlockSpec(memory_space=pltpu.HBM)


def params(mib):
    return pltpu.CompilerParams(vmem_limit_bytes=mib * 1024 * 1024)


def swap(x, axis, size, flip):
    return lax.ppermute(x, axis, [(i, i ^ flip) for i in range(size)])


def silu_half(h):
    return h + h * jnp.tanh(h)


def encoder_rows(place, n_w, n_wout, row0, rows, copies_out, *refs):
    refs = list(refs)
    hist_ref, sess_ref, ev_ref, gain_ref = refs[:4]
    refs = refs[4:]
    copies = []
    if place is not None:
        w_parts, wout_parts, refs = refs[:n_w], refs[n_w : n_w + n_wout], refs[n_w + n_wout :]
        pooled_ref, w_ref, wout_ref, kv_out, sums_out = refs[:5]
        q_ref, gate_ref, att_ref, sems = refs[5:]
        prior = []
        copies = place(w_parts, wout_parts, w_ref, wout_ref, sems)
    else:
        w_ref, wout_ref, kv_ref, sums_ref, pooled_ref = refs[:5]
        q_ref, gate_ref, att_ref, kv_out = refs[5:]
        prior = [kv_ref]
    for c in copies:
        c.start()
    for c in copies:
        c.wait()
    width = ev_ref.shape[1]
    head = width // HEADS
    hist = hist_ref[0]

    sess = sess_ref.shape[1]
    lens = jnp.broadcast_to(sess_ref[...], (sess, sess))
    at_row = lax.broadcasted_iota(jnp.int32, (sess, sess), 0)
    at_col = lax.broadcasted_iota(jnp.int32, (sess, sess), 1)
    ends = jnp.sum(jnp.where(at_col <= at_row, lens, 0).astype(F32), axis=1, keepdims=True)
    starts = jnp.sum(jnp.where(at_col < at_row, lens, 0).astype(F32), axis=1, keepdims=True)
    ends = jnp.minimum(ends, hist.astype(F32))
    pos = (lax.broadcasted_iota(jnp.int32, (sess, rows), 1) + row0).astype(F32)
    member = jnp.where((pos >= starts) & (pos < ends), 1.0, 0.0).astype(BF16)
    n_valid = jnp.maximum(ends - starts, 0.0)

    step = min(rows, 256)
    for r in range(0, rows, step):
        x = ev_ref[row0 + r : row0 + r + step, :]
        at = slice(r, r + step)
        row_pos = lax.broadcasted_iota(jnp.int32, (step, 1), 0) + (row0 + r)

        def act(n):
            part = jnp.dot(x, w_ref[:, n * width : (n + 1) * width], preferred_element_type=F32)
            return silu_half(part * 0.5)

        gate_ref[at, :] = act(0)
        kv_out[at, :width] = jnp.where(row_pos < hist, act(1), 0.0).astype(BF16)
        q_ref[at, :] = act(2).astype(BF16)
        kv_out[at, width:] = act(3).astype(BF16)

    blocks = []
    for ref in prior + [kv_out]:
        for r in range(0, ref.shape[0], step):
            blocks.append((ref, r))
    tri = lax.broadcasted_iota(jnp.int32, (step, step), 1) <= lax.broadcasted_iota(
        jnp.int32, (step, step), 0
    )
    before = len(blocks) - rows // step
    for i in range(rows // step):
        at = slice(i * step, (i + 1) * step)
        for h in range(HEADS):
            q = q_ref[at, h * head : (h + 1) * head]
            total = None
            for j in range(before + i + 1):
                ref, r = blocks[j]
                k = ref[r : r + step, width + h * head : width + (h + 1) * head]
                v = ref[r : r + step, h * head : (h + 1) * head]
                s = lax.dot_general(q, k, (((1,), (1,)), ((), ())), preferred_element_type=F32)
                wts = silu_half(s * (0.5 * head**-0.5))
                if j == before + i:
                    wts = jnp.where(tri, wts, 0.0)
                mixed = jnp.dot(wts.astype(BF16), v, preferred_element_type=F32)
                total = mixed if total is None else total + mixed
            att_ref[at, h * head : (h + 1) * head] = total

    sums_ev = jnp.dot(member, ev_ref[row0 : row0 + rows, :], preferred_element_type=F32)
    att = att_ref[...]
    inv = lax.rsqrt(jnp.mean(att * att, axis=1, keepdims=True) + EPSILON)
    gated = (att * inv * gain_ref[...] * gate_ref[...]).astype(BF16)
    sums_g = jnp.dot(member, gated, preferred_element_type=F32)
    if place is not None:
        sums_out[:, :width] = sums_ev
        sums_out[:, width:] = sums_g
    else:
        sums_ev = sums_ev + sums_ref[:, :width]
        sums_g = sums_g + sums_ref[:, width:]

    hi = sums_g.astype(BF16)
    rest = sums_g - hi.astype(F32)
    mid = rest.astype(BF16)
    low = (rest - mid.astype(F32)).astype(BF16)
    terms = jnp.dot(jnp.concatenate([low, mid, hi], axis=0), wout_ref[...], preferred_element_type=F32)
    out = terms[:sess] + terms[sess : 2 * sess] + terms[2 * sess :] + sums_ev
    out = out / jnp.maximum(n_valid, 1.0)
    if copies_out:
        peers, take = copies_out
        out = jnp.concatenate([out[:take]] * peers, axis=0)
    pooled_ref[...] = out.astype(BF16)


def encoder_call(hist_len, sess_len, events, gain, row0, rows, weights, copies_out=None, carried=None):
    width = events.shape[1]
    sess = sess_len.shape[1]
    place, w_parts, wout_parts = weights if carried is None else (None, [], [])
    scratch = [
        pltpu.VMEM((rows, width), BF16),
        pltpu.VMEM((rows, width), F32),
        pltpu.VMEM((rows, width), F32),
    ]
    if carried is None:
        operands = [*w_parts, *wout_parts]
        peers, take = copies_out
        out_shape = [
            jax.ShapeDtypeStruct((peers * take, width), BF16),
            jax.ShapeDtypeStruct((width, 4 * width), BF16),
            jax.ShapeDtypeStruct((width, width), BF16),
            jax.ShapeDtypeStruct((rows, 2 * width), BF16),
            jax.ShapeDtypeStruct((sess, 2 * width), F32),
        ]
        scratch.append(pltpu.SemaphoreType.DMA((64,)))
    else:
        operands = carried
        out_shape = [jax.ShapeDtypeStruct((sess, width), BF16)]
        scratch.append(pltpu.VMEM((rows, 2 * width), BF16))
    return pl.pallas_call(
        functools.partial(encoder_rows, place, len(w_parts), len(wout_parts), row0, rows, copies_out),
        in_specs=[SMEM] + [VMEM] * (3 + len(operands)),
        out_specs=[VMEM] * len(out_shape),
        out_shape=out_shape,
        scratch_shapes=scratch,
        compiler_params=params(16),
        cost_estimate=pl.CostEstimate(
            flops=2 * rows * width * 4 * width + 4 * rows * (row0 + rows) * width,
            bytes_accessed=6 * 1024 * 1024,
            transcendentals=4 * rows * width + HEADS * rows * (row0 + rows),
        ),
        name=f"encode_rows_{row0}",
    )(hist_len, sess_len, events, gain, *operands)


def load_kernel(n_parts, n_load, *refs):
    parts, refs = refs[:n_parts], refs[n_parts:]
    from_refs, refs = refs[:n_load], refs[n_load:]
    to_refs, refs = refs[:n_load], refs[n_load:]
    sems = refs[-1]
    copies = [pltpu.make_async_copy(a, b, sems.at[i]) for i, (a, b) in enumerate(zip(from_refs, to_refs))]
    for c in copies:
        c.start()
    for k, part in enumerate(parts):
        refs[0][k] = part[...]
    for c in copies:
        c.wait()


def load_call(parts, loads):
    out_shape = [jax.ShapeDtypeStruct(x.shape, x.dtype) for x in loads]
    if parts:
        out_shape.append(jax.ShapeDtypeStruct((len(parts), *parts[0].shape), parts[0].dtype))
    out = pl.pallas_call(
        functools.partial(load_kernel, len(parts), len(loads)),
        in_specs=[VMEM] * len(parts) + [HBM] * len(loads),
        out_specs=[VMEM] * len(out_shape),
        out_shape=out_shape,
        scratch_shapes=[pltpu.SemaphoreType.DMA((len(loads),))],
        compiler_params=params(8),
        name="load",
    )(*parts, *loads)
    return (out[:-1], out[-1]) if parts else (out, None)


def gather_weights(w_uvqk, w_out, loads, sections, dps, mps):
    depth, wide = w_uvqk.shape
    peers = sections * mps
    piece = wide // peers
    part = depth // sections
    if wide % (128 * peers) or part % 16:
        full = lax.all_gather(w_uvqk, "dp", axis=0, tiled=True)
        full_out = lax.all_gather(w_out, "dp", axis=0, tiled=True)

        def place_whole(ws, wouts, w_ref, wout_ref, sems):
            return [
                pltpu.make_async_copy(ws[0], w_ref, sems.at[0]),
                pltpu.make_async_copy(wouts[0], wout_ref, sems.at[1]),
            ]

        return (place_whole, [full], [full_out]), load_call([], loads)[0]

    s, m = lax.axis_index("section"), lax.axis_index("mp")
    mine = lax.dynamic_slice_in_dim(w_uvqk, (s * mps + m) * piece, piece, 1)
    got = jnp.stack([swap(mine, "dp", dps, k) for k in range(1, dps)])
    plane = [got] + [swap(got, "mp", mps, k) for k in range(1, mps)]
    half = lax.dynamic_slice_in_dim(w_out, s * part, part, 0)
    parts = [swap(half, "dp", dps, k) for k in range(1, dps)]
    (w_uvqk, w_out, *loads), got_out = load_call(parts, [w_uvqk, w_out, *loads])
    ws, wouts = [w_uvqk] + plane, [w_out, got_out]
    if sections == 2:
        ws = ws + [swap(p, "section", sections, 1) for p in plane]
        wouts = wouts + [swap(got_out, "section", sections, 1)]

    def place(ws, wouts, w_ref, wout_ref, sems):
        z = lax.axis_index("dp")
        sec, col = lax.axis_index("section"), lax.axis_index("mp")
        copies = []

        def add(src, dst):
            copies.append(pltpu.make_async_copy(src, dst, sems.at[len(copies)]))

        own = pl.ds(pl.multiple_of(z * depth, depth), depth)
        add(ws[0], w_ref.at[own])
        add(wouts[0], wout_ref.at[own])
        for i, ref in enumerate(ws[1:]):
            spot = ((sec ^ (i // mps)) * mps + (col ^ (i % mps))) * piece
            for k in range(1, dps):
                at = pl.ds(pl.multiple_of((z ^ k) * depth, depth), depth)
                add(ref.at[k - 1], w_ref.at[at, pl.ds(pl.multiple_of(spot, piece), piece)])
        for i, ref in enumerate(wouts[1:]):
            for k in range(1, dps):
                at = pl.ds(pl.multiple_of((z ^ k) * depth + (sec ^ i) * part, part), part)
                add(ref.at[k - 1], wout_ref.at[at])
        return copies

    return (place, ws, wouts), loads


def hidden_in_kernel(copies_out, x_ref, w_ref, gain_ref, local_ref, send_ref):
    local = jnp.dot(x_ref[...], w_ref[...], preferred_element_type=F32)
    local_ref[...] = local
    rows, cols = local.shape
    scaled = (local * gain_ref[...].astype(F32)).astype(BF16)
    tail = two_terms(jnp.sum(local * local, axis=1, keepdims=True))
    for k in range(copies_out):
        send_ref[k, :, :cols] = scaled
        send_ref[k, :, cols:] = tail


def two_terms(square):
    hi = square.astype(BF16).astype(F32)
    lane = lax.broadcasted_iota(jnp.int32, (square.shape[0], 128), 1)
    return jnp.where(lane == 0, hi, jnp.where(lane == 1, square - hi, 0.0)).astype(BF16)


def up_kernel(chunks, got_ref, w_ref, half_ref, send_ref):
    mps, rows, cols = got_ref.shape
    cols = cols - 128
    wide = w_ref.shape[1]
    each = wide // chunks
    square = None
    for k in range(mps):
        tail = jnp.sum(got_ref[k, :, cols:].astype(F32), axis=1, keepdims=True)
        square = tail if square is None else square + tail
    x = jnp.concatenate([got_ref[k, :, :cols] for k in range(mps)], axis=1)
    for c in range(chunks):
        at = slice(c * each, (c + 1) * each)
        half = jnp.dot(x, w_ref[:, at], preferred_element_type=F32)
        half_ref[:, at] = half
        send_ref[:, at] = half.astype(BF16)
    half_ref[:, wide:] = jnp.broadcast_to(square, (rows, 128))
    send_ref[:, wide:] = two_terms(square)


def down_kernel(chunks, half_ref, other_ref, local_ref, w_ref, out_ref, part_ref):
    units, wide = w_ref.shape
    each = wide // chunks
    square = half_ref[:, units : units + 1] + jnp.sum(other_ref[:, units:].astype(F32), axis=1, keepdims=True)
    inv = lax.rsqrt(square / DM + EPSILON)
    up = (half_ref[:, :units] + other_ref[:, :units].astype(F32)) * inv
    hidden = jax.nn.gelu(up, approximate=True).astype(BF16)
    for c in range(chunks):
        at = slice(c * each, (c + 1) * each)
        part_ref[:, at] = jnp.dot(hidden, w_ref[:, at], preferred_element_type=F32)
    m = lax.axis_index("mp")
    cols = local_ref.shape[1]
    own = pl.ds(pl.multiple_of(m * cols, cols), cols)
    part_ref[:, own] = part_ref[:, own] + local_ref[...]
    out_ref[...] = part_ref[...].astype(BF16)


def sum_kernel(sections, mps, got_ref, out_ref):
    got = got_ref[...].astype(F32)
    take, wide = out_ref.shape[0], got.shape[1]
    for s in range(sections):
        total = got[s * mps * take : (s * mps + 1) * take]
        for k in range(s * mps + 1, (s + 1) * mps):
            total = total + got[k * take : (k + 1) * take]
        out_ref[:, s * wide : (s + 1) * wide] = total.astype(BF16)


def cross_block(micro_rows, take, w_in, ffn_gain, w_up, w_down, sections, mps):
    peers = sections * mps
    rows, width = micro_rows.shape
    cols = w_in.shape[1]
    units = w_up.shape[1]
    half_width = w_down.shape[1]
    group = ("section", "mp")
    chunks = 4

    arrived = lax.all_to_all(
        micro_rows.reshape(peers, take, width), group, split_axis=0, concat_axis=0, tiled=True
    ).reshape(rows, width)
    local, send = pl.pallas_call(
        functools.partial(hidden_in_kernel, mps),
        out_shape=[
            jax.ShapeDtypeStruct((rows, cols), F32),
            jax.ShapeDtypeStruct((mps, rows, cols + 128), BF16),
        ],
        in_specs=[VMEM] * 3,
        out_specs=[VMEM] * 2,
        compiler_params=params(8),
        cost_estimate=pl.CostEstimate(
            flops=2 * rows * width * cols, bytes_accessed=2 * width * cols, transcendentals=0
        ),
        name="hidden_in",
    )(arrived, w_in, ffn_gain)

    got = lax.all_to_all(send, "mp", split_axis=0, concat_axis=0, tiled=True)
    half, half_send = pl.pallas_call(
        functools.partial(up_kernel, chunks),
        out_shape=[
            jax.ShapeDtypeStruct((rows, units + 128), F32),
            jax.ShapeDtypeStruct((rows, units + 128), BF16),
        ],
        in_specs=[VMEM] * 2,
        out_specs=[VMEM] * 2,
        compiler_params=params(8),
        cost_estimate=pl.CostEstimate(
            flops=2 * rows * w_up.size, bytes_accessed=2 * w_up.size, transcendentals=0
        ),
        name="up_half",
    )(got, w_up)

    other = swap(half_send, "section", sections, 1)
    partial = pl.pallas_call(
        functools.partial(down_kernel, chunks),
        out_shape=jax.ShapeDtypeStruct((rows, half_width), BF16),
        in_specs=[VMEM] * 4,
        out_specs=VMEM,
        scratch_shapes=[pltpu.VMEM((rows, half_width), F32)],
        compiler_params=params(8),
        cost_estimate=pl.CostEstimate(
            flops=2 * rows * w_down.size, bytes_accessed=2 * w_down.size, transcendentals=rows * units
        ),
        name="down_part",
    )(half, other, local, w_down)

    arrived = lax.all_to_all(
        partial.reshape(peers, take, half_width), group, split_axis=0, concat_axis=0, tiled=True
    ).reshape(rows, half_width)
    return pl.pallas_call(
        functools.partial(sum_kernel, sections, mps),
        out_shape=jax.ShapeDtypeStruct((take, half_width * sections), BF16),
        in_specs=[VMEM],
        out_specs=VMEM,
        compiler_params=params(8),
        name="sum_rows",
    )(arrived)


def per_device(sections, dps, mps, events, hist_len, sess_len, w_uvqk, w_out, attn_gain, w_in, ffn_gain, w_up, w_down):
    events = events[0]
    length, width = events.shape
    sess = sess_len.shape[1]
    take = sess // MICRO
    loads = [sess_len, events, attn_gain.reshape(1, width), w_in, ffn_gain]
    weights, loads = gather_weights(w_uvqk, w_out, loads, sections, dps, mps)
    sess_len, events, gain, w_in, ffn_gain = loads
    encode = functools.partial(encoder_call, hist_len, sess_len, events, gain)

    first = take * SESS_MAX
    micro_rows, *carried = encode(0, first, weights, copies_out=(sections * mps, take))
    cross_out = cross_block(micro_rows, take, w_in, ffn_gain, w_up, w_down, sections, mps)
    (pooled,) = encode(first, length - first, weights, carried=carried)
    return (pooled, cross_out)


def solution(mesh):
    sizes = [mesh.shape[name] for name in ("section", "dp", "mp")]
    return jax.shard_map(
        functools.partial(per_device, *sizes),
        mesh=mesh,
        in_specs=(
            P(("section", "dp", "mp"), None, None),
            P(("section", "dp", "mp")),
            P(("section", "dp", "mp"), None),
            P("dp", None),
            P("dp", None),
            P(),
            P(None, ("section", "mp")),
            P(None, ("section", "mp")),
            P("section", "mp"),
            P("mp", "section"),
        ),
        out_specs=(P(("section", "dp", "mp"), None), P(("section", "dp", "mp"), None)),
        check_vma=False,
    )
```

```python
import functools

import jax
import jax.numpy as jnp
from jax import lax
from jax.experimental import pallas as pl
from jax.experimental.pallas import tpu as pltpu
from jax.sharding import PartitionSpec as P

HEADS = 4
DM = 4096
MICRO = 4
SESS_MAX = 64
EPSILON = 1e-06
F32 = jnp.float32
BF16 = jnp.bfloat16

VMEM = pl.BlockSpec(memory_space=pltpu.VMEM)
HBM = pl.BlockSpec(memory_space=pltpu.HBM)


def params(mib):
    return pltpu.CompilerParams(vmem_limit_bytes=mib * 1024 * 1024)


def swap(x, axis, size, flip):
    return lax.ppermute(x, axis, [(i, i ^ flip) for i in range(size)])


def silu_half(h):
    return h + h * jnp.tanh(h)


def encoder_rows(place, n_w, n_wout, row0, rows, copies_out, *refs):
    refs = list(refs)
    bounds_ref, ev_ref, gain_ref = refs[:3]
    refs = refs[3:]
    copies = []
    if place is not None:
        w_parts, wout_parts, refs = refs[:n_w], refs[n_w : n_w + n_wout], refs[n_w + n_wout :]
        pooled_ref, w_ref, wout_ref, kv_out, sums_out = refs[:5]
        q_ref, gate_ref, att_ref, sems = refs[5:]
        prior = []
        copies = place(w_parts, wout_parts, w_ref, wout_ref, sems)
    else:
        w_ref, wout_ref, kv_ref, sums_ref, pooled_ref = refs[:5]
        q_ref, gate_ref, att_ref, kv_out = refs[5:]
        prior = [kv_ref]
    for c in copies:
        c.start()
    for c in copies:
        c.wait()
    width = ev_ref.shape[1]
    head = width // HEADS
    starts, ends, hist = bounds_ref[0, :, :1], bounds_ref[1, :, :1], bounds_ref[2, :1, :1]
    sess = starts.shape[0]

    pos = (lax.broadcasted_iota(jnp.int32, (sess, rows), 1) + row0).astype(F32)
    member = jnp.where((pos >= starts) & (pos < ends), 1.0, 0.0).astype(BF16)
    n_valid = jnp.maximum(ends - starts, 0.0)

    step = min(rows, 256)
    for r in range(0, rows, step):
        x = ev_ref[r : r + step, :]
        at = slice(r, r + step)
        row_pos = lax.broadcasted_iota(jnp.int32, (step, 1), 0).astype(F32) + (row0 + r)

        def act(n):
            part = jnp.dot(x, w_ref[:, n * width : (n + 1) * width], preferred_element_type=F32)
            return silu_half(part * 0.5)

        gate_ref[at, :] = act(0)
        kv_out[at, :width] = jnp.where(row_pos < hist, act(1), 0.0).astype(BF16)
        q_ref[at, :] = act(2).astype(BF16)
        kv_out[at, width:] = act(3).astype(BF16)

    blocks = []
    for ref in prior + [kv_out]:
        for r in range(0, ref.shape[0], step):
            blocks.append((ref, r))
    tri = lax.broadcasted_iota(jnp.int32, (step, step), 1) <= lax.broadcasted_iota(
        jnp.int32, (step, step), 0
    )
    before = len(blocks) - rows // step
    for i in range(rows // step):
        at = slice(i * step, (i + 1) * step)
        for h in range(HEADS):
            q = q_ref[at, h * head : (h + 1) * head]
            total = None
            for j in range(before + i + 1):
                ref, r = blocks[j]
                k = ref[r : r + step, width + h * head : width + (h + 1) * head]
                v = ref[r : r + step, h * head : (h + 1) * head]
                s = lax.dot_general(q, k, (((1,), (1,)), ((), ())), preferred_element_type=F32)
                wts = silu_half(s * (0.5 * head**-0.5))
                if j == before + i:
                    wts = jnp.where(tri, wts, 0.0)
                mixed = jnp.dot(wts.astype(BF16), v, preferred_element_type=F32)
                total = mixed if total is None else total + mixed
            att_ref[at, h * head : (h + 1) * head] = total

    sums_ev = jnp.dot(member, ev_ref[...], preferred_element_type=F32)
    att = att_ref[...]
    inv = lax.rsqrt(jnp.mean(att * att, axis=1, keepdims=True) + EPSILON)
    gated = (att * inv * gain_ref[:1] * gate_ref[...]).astype(BF16)
    sums_g = jnp.dot(member, gated, preferred_element_type=F32)
    if place is not None:
        sums_out[:, :width] = sums_ev
        sums_out[:, width:] = sums_g
    else:
        sums_ev = sums_ev + sums_ref[:, :width]
        sums_g = sums_g + sums_ref[:, width:]

    hi = sums_g.astype(BF16)
    rest = sums_g - hi.astype(F32)
    mid = rest.astype(BF16)
    low = (rest - mid.astype(F32)).astype(BF16)
    terms = jnp.dot(jnp.concatenate([low, mid, hi], axis=0), wout_ref[...], preferred_element_type=F32)
    out = terms[:sess] + terms[sess : 2 * sess] + terms[2 * sess :] + sums_ev
    out = out / jnp.maximum(n_valid, 1.0)
    if copies_out:
        peers, take = copies_out
        out = jnp.concatenate([out[:take]] * peers, axis=0)
    pooled_ref[...] = out.astype(pooled_ref.dtype)


def encoder_call(bounds, gain, events, row0, weights, copies_out=None, carried=None):
    rows, width = events.shape
    sess = bounds.shape[1]
    place, w_parts, wout_parts = weights if carried is None else (None, [], [])
    scratch = [
        pltpu.VMEM((rows, width), BF16),
        pltpu.VMEM((rows, width), F32),
        pltpu.VMEM((rows, width), F32),
    ]
    if carried is None:
        operands = [*w_parts, *wout_parts]
        peers, take = copies_out
        out_shape = [
            jax.ShapeDtypeStruct((peers * take, width), BF16),
            jax.ShapeDtypeStruct((width, 4 * width), BF16),
            jax.ShapeDtypeStruct((width, width), BF16),
            jax.ShapeDtypeStruct((rows, 2 * width), BF16),
            jax.ShapeDtypeStruct((sess, 2 * width), F32),
        ]
        scratch.append(pltpu.SemaphoreType.DMA((64,)))
    else:
        operands = carried
        out_shape = [jax.ShapeDtypeStruct((sess, width), F32)]
        scratch.append(pltpu.VMEM((rows, 2 * width), BF16))
    return pl.pallas_call(
        functools.partial(encoder_rows, place, len(w_parts), len(wout_parts), row0, rows, copies_out),
        in_specs=[VMEM] * (3 + len(operands)),
        out_specs=[VMEM] * len(out_shape),
        out_shape=out_shape,
        scratch_shapes=scratch,
        compiler_params=params(16),
        cost_estimate=pl.CostEstimate(
            flops=2 * rows * width * 4 * width + 4 * rows * (row0 + rows) * width,
            bytes_accessed=6 * 1024 * 1024,
            transcendentals=4 * rows * width + HEADS * rows * (row0 + rows),
        ),
        name=f"encode_rows_{row0}",
    )(bounds, events, gain, *operands)


def parity(m):
    return (m & 1) ^ ((m >> 1) & 1)


def split_kernel(*refs):
    *parts, next_ref, left_ref, right_ref, next_out = refs
    next_out[...] = next_ref[...]
    half = left_ref.shape[2]
    for k, part in enumerate(parts):
        left_ref[k] = part[:, :half]
        right_ref[k] = part[:, half:]


def gather_weights(w_uvqk, w_out, w_in, ffn_gain, sections, dps, mps):
    depth, wide = w_uvqk.shape
    gains = [ffn_gain] + [swap(ffn_gain, "mp", mps, k) for k in range(1, mps)]
    if (sections, mps) != (2, 4) or wide % 1024 or depth % 32:
        full = lax.all_gather(w_uvqk, "dp", axis=0, tiled=True)
        full_out = lax.all_gather(w_out, "dp", axis=0, tiled=True)
        blocks = [[w_in]] + [[swap(w_in, "mp", mps, k)] for k in range(1, mps)]

        def place_whole(ws, wouts, w_ref, wout_ref, sems):
            return [
                pltpu.make_async_copy(ws[0], w_ref, sems.at[0]),
                pltpu.make_async_copy(wouts[0], wout_ref, sems.at[1]),
            ]

        return (place_whole, [full], [full_out]), blocks, gains

    quarter, part = wide // 4, depth // 2
    sec, m = lax.axis_index("section"), lax.axis_index("mp")
    mine = lax.dynamic_slice_in_dim(w_uvqk, (sec * 2 + parity(m)) * quarter, quarter, 1)
    half = lax.dynamic_slice_in_dim(w_out, sec * part, part, 0)
    got = [swap(mine, "dp", dps, k) for k in range(1, dps)]
    left, right, half = pl.pallas_call(
        split_kernel,
        in_specs=[VMEM] * (len(got) + 1),
        out_specs=[VMEM] * 3,
        out_shape=[
            *[jax.ShapeDtypeStruct((len(got), depth, quarter // 2), BF16)] * 2,
            jax.ShapeDtypeStruct(half.shape, BF16),
        ],
        compiler_params=params(8),
        cost_estimate=pl.CostEstimate(flops=0, bytes_accessed=16 * 1024 * 1024, transcendentals=0),
        name="split",
    )(*got, half)
    plane = [left, right, swap(left, "mp", mps, 1), swap(right, "mp", mps, 2)]
    ws = [w_uvqk[:, : wide // 2], w_uvqk[:, wide // 2 :]] + plane + [swap(p, "section", sections, 1) for p in plane]
    got_out = [swap(half, "dp", dps, k) for k in range(1, dps)]
    wouts = [w_out[:part], w_out[part:]] + got_out + [swap(p, "section", sections, 1) for p in got_out]

    from_x, from_y = swap(w_in, "mp", mps, 1), swap(w_in, "mp", mps, 2)
    cut = w_in.shape[0] // 32 * 16
    diagonal = [swap(from_x[:cut], "mp", mps, 2), swap(from_y[cut:], "mp", mps, 1)]

    def place(ws, wouts, w_ref, wout_ref, sems):
        z = lax.axis_index("dp")
        sec, m = lax.axis_index("section"), lax.axis_index("mp")
        copies = []

        def add(src, dst):
            copies.append(pltpu.make_async_copy(src, dst, sems.at[len(copies)]))

        def rows_of(k):
            return (z ^ k) * depth

        own = pl.ds(pl.multiple_of(rows_of(0), depth), depth)
        for i in range(2):
            add(ws[i], w_ref.at[own, pl.ds(i * (wide // 2), wide // 2)])
            add(wouts[i], wout_ref.at[pl.ds(pl.multiple_of(rows_of(0) + i * part, part), part)])
        for i, ref in enumerate(ws[2:]):
            spot = (sec ^ (i // 4)) * 2 * quarter + (parity(m) ^ (i // 2 % 2)) * quarter + (i % 2) * (quarter // 2)
            cols = pl.ds(pl.multiple_of(spot, quarter // 2), quarter // 2)
            for k in range(1, dps):
                add(ref.at[k - 1], w_ref.at[pl.ds(pl.multiple_of(rows_of(k), depth), depth), cols])
        for i, ref in enumerate(wouts[2:]):
            k = i % (dps - 1) + 1
            at = rows_of(k) + (sec ^ (i // (dps - 1))) * part
            add(ref, wout_ref.at[pl.ds(pl.multiple_of(at, part), part)])
        return copies

    return (place, ws, wouts), [[w_in], [from_x], [from_y], diagonal], gains


def two_terms(square):
    hi = square.astype(BF16).astype(F32)
    lane = lax.broadcasted_iota(jnp.int32, (square.shape[0], 128), 1)
    return jnp.where(lane == 0, hi, jnp.where(lane == 1, square - hi, 0.0)).astype(BF16)


def up_kernel(chunks, pieces, x_ref, *refs):
    w_in_refs, refs = refs[: sum(pieces)], refs[sum(pieces) :]
    gain_refs, refs = refs[: len(pieces)], refs[len(pieces) :]
    w_ref, local_ref, half_ref, send_ref, normed_ref = refs
    m = lax.axis_index("mp")
    x = x_ref[...]
    square = None
    at = 0
    for k, n in enumerate(pieces):
        block = jnp.concatenate([r[...] for r in w_in_refs[at : at + n]], axis=0)
        at += n
        hidden = jnp.dot(x, block, preferred_element_type=F32)
        part = jnp.sum(hidden * hidden, axis=1, keepdims=True)
        square = part if square is None else square + part
        gain = gain_refs[k][...].astype(F32)
        cols = hidden.shape[1]
        normed_ref[:, pl.ds(pl.multiple_of((m ^ k) * cols, cols), cols)] = (hidden * gain).astype(BF16)
        if k == 0:
            local_ref[...] = hidden
    normed = normed_ref[...]
    wide = w_ref.shape[1]
    each = wide // chunks
    for c in range(chunks):
        at = slice(c * each, (c + 1) * each)
        half = jnp.dot(normed, w_ref[:, at], preferred_element_type=F32)
        half_ref[:, at] = half
        send_ref[:, at] = half.astype(BF16)
    half_ref[:, wide:] = jnp.broadcast_to(square, (x.shape[0], 128))
    send_ref[:, wide:] = two_terms(square)


def down_kernel(chunks, half_ref, other_ref, local_ref, w_ref, _, out_ref, part_ref):
    units, wide = w_ref.shape
    each = wide // chunks
    square = half_ref[:, units : units + 1] + jnp.sum(other_ref[:, units:].astype(F32), axis=1, keepdims=True)
    inv = lax.rsqrt(square / DM + EPSILON)
    up = (half_ref[:, :units] + other_ref[:, :units].astype(F32)) * inv
    hidden = jax.nn.gelu(up, approximate=True).astype(BF16)
    for c in range(chunks):
        at = slice(c * each, (c + 1) * each)
        part_ref[:, at] = jnp.dot(hidden, w_ref[:, at], preferred_element_type=F32)
    m = lax.axis_index("mp")
    cols = local_ref.shape[1]
    own = pl.ds(pl.multiple_of(m * cols, cols), cols)
    part_ref[:, own] = part_ref[:, own] + local_ref[...]
    out_ref[...] = part_ref[...].astype(BF16)


def sum_kernel(sections, mps, got_ref, out_ref):
    got = got_ref[...].astype(F32)
    take, wide = out_ref.shape[0], got.shape[1]
    for s in range(sections):
        total = got[s * mps * take : (s * mps + 1) * take]
        for k in range(s * mps + 1, (s + 1) * mps):
            total = total + got[k * take : (k + 1) * take]
        out_ref[:, s * wide : (s + 1) * wide] = total.astype(BF16)


def cross_block(micro_rows, take, w_in_blocks, gains, w_up, w_down, encode_rest, sections, mps):
    peers = sections * mps
    rows, width = micro_rows.shape
    cols = w_up.shape[0] // mps
    units = w_up.shape[1]
    half_width = w_down.shape[1]
    group = ("section", "mp")
    chunks = 4

    arrived = lax.all_to_all(
        micro_rows.reshape(peers, take, width), group, split_axis=0, concat_axis=0, tiled=True
    ).reshape(rows, width)
    blocks = [piece for block in w_in_blocks for piece in block]
    local, half, half_send = pl.pallas_call(
        functools.partial(up_kernel, chunks, [len(block) for block in w_in_blocks]),
        out_shape=[
            jax.ShapeDtypeStruct((rows, cols), F32),
            jax.ShapeDtypeStruct((rows, units + 128), F32),
            jax.ShapeDtypeStruct((rows, units + 128), BF16),
        ],
        in_specs=[VMEM] * (len(blocks) + len(gains) + 2),
        out_specs=[VMEM] * 3,
        scratch_shapes=[pltpu.VMEM((rows, w_up.shape[0]), BF16)],
        compiler_params=params(10),
        cost_estimate=pl.CostEstimate(
            flops=2 * rows * w_up.size, bytes_accessed=2 * w_up.size, transcendentals=0
        ),
        name="up_half",
    )(arrived, *blocks, *gains, w_up)

    other = swap(half_send, "section", sections, 1)
    rest = encode_rest()
    partial = pl.pallas_call(
        functools.partial(down_kernel, chunks),
        out_shape=jax.ShapeDtypeStruct((rows, half_width), BF16),
        in_specs=[VMEM] * 4 + [HBM],
        out_specs=VMEM,
        scratch_shapes=[pltpu.VMEM((rows, half_width), F32)],
        compiler_params=params(8),
        cost_estimate=pl.CostEstimate(
            flops=2 * rows * w_down.size, bytes_accessed=2 * w_down.size, transcendentals=rows * units
        ),
        name="down_part",
    )(half, other, local, w_down, rest)

    arrived = lax.all_to_all(
        partial.reshape(peers, take, half_width), group, split_axis=0, concat_axis=0, tiled=True
    ).reshape(rows, half_width)
    cross_out = pl.pallas_call(
        functools.partial(sum_kernel, sections, mps),
        out_shape=jax.ShapeDtypeStruct((take, half_width * sections), BF16),
        in_specs=[VMEM],
        out_specs=VMEM,
        compiler_params=params(8),
        name="sum_rows",
    )(arrived)
    return rest, partial, cross_out


def round_kernel(x_ref, _, out_ref):
    out_ref[...] = x_ref[...].astype(BF16)


def per_device(sections, dps, mps, events, hist_len, sess_len, w_uvqk, w_out, attn_gain, w_in, ffn_gain, w_up, w_down):
    events = events[0]
    length, width = events.shape
    sess = sess_len.shape[1]
    take = sess // MICRO
    gain = jnp.broadcast_to(attn_gain, (8, width))
    weights, w_in_blocks, gains = gather_weights(w_uvqk, w_out, w_in, ffn_gain, sections, dps, mps)
    ends = jnp.sum(jnp.where(jnp.tri(sess, dtype=jnp.bool_), sess_len, 0), axis=1)
    bounds = jnp.stack([ends - sess_len[0], jnp.minimum(ends, hist_len), jnp.broadcast_to(hist_len, ends.shape)])
    bounds = jnp.broadcast_to(bounds.astype(F32)[:, :, None], (3, sess, 128))
    encode = functools.partial(encoder_call, bounds, gain)

    first = take * SESS_MAX
    micro_rows, *carried = encode(events[:first], 0, weights, copies_out=(sections * mps, take))

    def encode_rest():
        return encode(events[first:], first, weights, carried=carried)[0]

    pooled, after, cross_out = cross_block(micro_rows, take, w_in_blocks, gains, w_up, w_down, encode_rest, sections, mps)
    pooled = pl.pallas_call(
        round_kernel,
        out_shape=jax.ShapeDtypeStruct(pooled.shape, BF16),
        in_specs=[VMEM, HBM],
        out_specs=VMEM,
        compiler_params=params(8),
        name="round_pooled",
    )(pooled, after)
    return (pooled, cross_out)


def solution(mesh):
    sizes = [mesh.shape[name] for name in ("section", "dp", "mp")]
    return jax.shard_map(
        functools.partial(per_device, *sizes),
        mesh=mesh,
        in_specs=(
            P(("section", "dp", "mp"), None, None),
            P(("section", "dp", "mp")),
            P(("section", "dp", "mp"), None),
            P("dp", None),
            P("dp", None),
            P(),
            P(None, ("section", "mp")),
            P(None, ("section", "mp")),
            P("section", "mp"),
            P("mp", "section"),
        ),
        out_specs=(P(("section", "dp", "mp"), None), P(("section", "dp", "mp"), None)),
        check_vma=False,
    )
```

```python
import functools

import jax
import jax.numpy as jnp
from jax import lax
from jax.experimental import pallas as pl
from jax.experimental.pallas import tpu as pltpu
from jax.sharding import PartitionSpec as P

HEADS = 4
DM = 4096
MICRO = 4
SESS_MAX = 64
EPSILON = 1e-06
F32 = jnp.float32
BF16 = jnp.bfloat16

VMEM = pl.BlockSpec(memory_space=pltpu.VMEM)


def swap(x, axis, size, flip):
    return lax.ppermute(x, axis, [(i, i ^ flip) for i in range(size)])


def silu_half(h):
    return h + h * jnp.tanh(h)


def in_order(ref, at, dps):
    if dps == 1:
        return ref[at, :]
    z = lax.axis_index("dp")
    cols = ref.shape[1] // dps
    return jnp.concatenate([ref[at, pl.ds(pl.multiple_of((z ^ k) * cols, cols), cols)] for k in range(dps)], axis=1)


def project(dps, row0, hist, ev_ref, w_ref, gate_ref, q_ref, kv_ref):
    rows, width = ev_ref.shape
    step = min(rows, 256)
    for r in range(0, rows, step):
        at = slice(r, r + step)
        x = in_order(ev_ref, at, dps)
        row_pos = lax.broadcasted_iota(jnp.int32, (step, 1), 0).astype(F32) + (row0 + r)

        def act(n):
            part = jnp.dot(x, w_ref[:, n * width : (n + 1) * width], preferred_element_type=F32)
            return silu_half(part * 0.5)

        gate_ref[at, :] = act(0).astype(gate_ref.dtype)
        kv_ref[at, :width] = jnp.where(row_pos < hist, act(1), 0.0).astype(BF16)
        q_ref[at, :] = act(2).astype(BF16)
        kv_ref[at, width:] = act(3).astype(BF16)


def attend(q_ref, kv_refs, gate_ref, gain_ref, att_ref):
    rows, width = q_ref.shape
    head = width // HEADS
    step = min(rows, 256)
    blocks = [(ref, r) for ref in kv_refs for r in range(0, ref.shape[0], step)]
    tri = lax.broadcasted_iota(jnp.int32, (step, step), 1) <= lax.broadcasted_iota(
        jnp.int32, (step, step), 0
    )
    before = len(blocks) - rows // step
    for i in range(rows // step):
        at = slice(i * step, (i + 1) * step)
        for h in range(HEADS):
            q = q_ref[at, h * head : (h + 1) * head]
            total = None
            for j in range(before + i + 1):
                ref, r = blocks[j]
                k = ref[r : r + step, width + h * head : width + (h + 1) * head]
                v = ref[r : r + step, h * head : (h + 1) * head]
                s = lax.dot_general(q, k, (((1,), (1,)), ((), ())), preferred_element_type=F32)
                wts = silu_half(s * (0.5 * head**-0.5))
                if j == before + i:
                    wts = jnp.where(tri, wts, 0.0)
                mixed = jnp.dot(wts.astype(BF16), v, preferred_element_type=F32)
                total = mixed if total is None else total + mixed
            att_ref[at, h * head : (h + 1) * head] = total
    att = att_ref[...]
    inv = lax.rsqrt(jnp.mean(att * att, axis=1, keepdims=True) + EPSILON)
    return (att * inv * gain_ref[:1] * gate_ref[...].astype(F32)).astype(BF16)


def membership(bounds_ref, row0, rows):
    starts, ends = bounds_ref[0, :, :1], bounds_ref[1, :, :1]
    pos = (lax.broadcasted_iota(jnp.int32, (starts.shape[0], rows), 1) + row0).astype(F32)
    return jnp.where((pos >= starts) & (pos < ends), 1.0, 0.0).astype(BF16)


def pool(dps, bounds_ref, sums_ev, sums_ref, wout_ref):
    n_valid = jnp.maximum(bounds_ref[1, :, :1] - bounds_ref[0, :, :1], 1.0)
    sess = sums_ev.shape[0]
    sums_g = in_order(sums_ref, slice(None), dps)
    hi = sums_g.astype(BF16)
    rest = sums_g - hi.astype(F32)
    mid = rest.astype(BF16)
    low = (rest - mid.astype(F32)).astype(BF16)
    terms = jnp.dot(jnp.concatenate([low, mid, hi], axis=0), wout_ref[...], preferred_element_type=F32)
    return (terms[:sess] + terms[sess : 2 * sess] + terms[2 * sess :] + sums_ev) / n_valid


def first_kernel(place, dps, copies_out, n_parts, bounds_ref, ev_ref, gain_ref, *refs):
    parts, refs = refs[:n_parts], refs[n_parts:]
    pooled_ref, w_ref, wout_ref, kv_ref, sums_ev_ref, sums_g_ref, q_ref, gate_ref, att_ref, sems = refs
    copies = place(parts, w_ref, wout_ref, sems)
    for c in copies:
        c.start()
    member = membership(bounds_ref, 0, ev_ref.shape[0])
    sums_ev = jnp.dot(member, ev_ref[...], preferred_element_type=F32)
    sums_ev_ref[...] = sums_ev
    for c in copies:
        c.wait()
    project(dps, 0, bounds_ref[2, :1, :1], ev_ref, w_ref, gate_ref, q_ref, kv_ref)
    gated = attend(q_ref, [kv_ref], gate_ref, gain_ref, att_ref)
    sums_g_ref[...] = jnp.dot(member, gated, preferred_element_type=F32)
    out = pool(dps, bounds_ref, sums_ev, sums_g_ref, wout_ref)
    peers, take = copies_out
    pooled_ref[...] = jnp.concatenate([out[:take]] * peers, axis=0).astype(BF16)


def project_kernel(dps, row0, bounds_ref, ev_ref, w_ref, sums_ev_ref, _, gate_ref, q_ref, kv_ref, out_ref):
    project(dps, row0, bounds_ref[2, :1, :1], ev_ref, w_ref, gate_ref, q_ref, kv_ref)
    member = membership(bounds_ref, row0, ev_ref.shape[0])
    out_ref[...] = sums_ev_ref[...] + jnp.dot(member, ev_ref[...], preferred_element_type=F32)


def attend_kernel(row0, bounds_ref, gain_ref, gate_ref, q_ref, kv_first, kv_ref, sums_ref, _, out_ref, att_ref):
    member = membership(bounds_ref, row0, q_ref.shape[0])
    gated = attend(q_ref, [kv_first, kv_ref], gate_ref, gain_ref, att_ref)
    out_ref[...] = sums_ref[...] + jnp.dot(member, gated, preferred_element_type=F32)


def call(kernel, name, operands, out_shape, scratch, mib, flops, size, transcendentals=0):
    return pl.pallas_call(
        kernel,
        in_specs=[VMEM] * len(operands),
        out_specs=[VMEM] * len(out_shape),
        out_shape=[jax.ShapeDtypeStruct(shape, kind) for shape, kind in out_shape],
        scratch_shapes=scratch,
        compiler_params=pltpu.CompilerParams(vmem_limit_bytes=mib * 1024 * 1024),
        cost_estimate=pl.CostEstimate(flops=flops, bytes_accessed=size, transcendentals=transcendentals),
        name=name,
    )(*operands)


def parity(m):
    return (m & 1) ^ ((m >> 1) & 1)


def split_kernel(*refs):
    *parts, left_ref, right_ref = refs
    half = left_ref.shape[2]
    for k, part in enumerate(parts):
        left_ref[k] = part[:, :half]
        right_ref[k] = part[:, half:]


def gather_weights(w_uvqk, w_out, w_in, ffn_gain, sections, dps, mps):
    depth, wide = w_uvqk.shape
    width = w_out.shape[1]
    w_in = jnp.concatenate([w_in, jnp.broadcast_to(ffn_gain, (16, w_in.shape[1]))], axis=0)
    if (sections, mps) != (2, 4) or wide != 4 * width or depth % 128:
        ws = [lax.all_gather(x, "dp", axis=0, tiled=True) for x in (w_uvqk, w_out)]
        blocks = [[w_in]] + [[swap(w_in, "mp", mps, k)] for k in range(1, mps)]

        def place_whole(parts, w_ref, wout_ref, sems):
            return [
                pltpu.make_async_copy(parts[0], w_ref, sems.at[0]),
                pltpu.make_async_copy(parts[1], wout_ref, sems.at[1]),
            ]

        return place_whole, ws, blocks, 1

    part = depth // 4
    cut = width // 2
    sec, m = lax.axis_index("section"), lax.axis_index("mp")
    share = sec * 2 + parity(m)
    mine = jnp.concatenate(
        [
            lax.dynamic_slice_in_dim(w_uvqk, share * width, width, 1),
            lax.dynamic_slice_in_dim(w_out, share * part, part, 0),
        ],
        axis=0,
    )
    got = [swap(mine, "dp", dps, k) for k in range(1, dps)]
    left, right = call(
        split_kernel,
        "split",
        got,
        [((len(got), depth + part, cut), BF16)] * 2,
        [],
        8,
        0,
        16 * 1024 * 1024,
    )
    plane = [left, right, swap(left, "mp", mps, 1), swap(right, "mp", mps, 2)]
    parts = [w_uvqk[:, : wide // 2], w_uvqk[:, wide // 2 :], w_out[: depth // 2], w_out[depth // 2 :]]
    parts = parts + plane + [swap(p, "section", sections, 1) for p in plane]

    from_x, from_y = swap(w_in, "mp", mps, 1), swap(w_in, "mp", mps, 2)
    middle = w_in.shape[0] // 32 * 16
    diagonal = [swap(from_x[:middle], "mp", mps, 2), swap(from_y[middle:], "mp", mps, 1)]

    def place(parts, w_ref, wout_ref, sems):
        sec, m = lax.axis_index("section"), lax.axis_index("mp")
        w_ref, wout_ref = w_ref.reshape(dps, depth, wide), wout_ref.reshape(dps, depth, width)
        copies = []

        def add(src, dst):
            copies.append(pltpu.make_async_copy(src, dst, sems.at[len(copies)]))

        for i in range(2):
            add(parts[i], w_ref.at[0, :, i * (wide // 2) : (i + 1) * (wide // 2)])
            add(parts[2 + i], wout_ref.at[0, i * (depth // 2) : (i + 1) * (depth // 2)])
        for i, ref in enumerate(parts[4:]):
            owner = (sec ^ (i // 4)) * 2 + (parity(m) ^ (i // 2 % 2))
            at = (i % 2) * cut
            cols = pl.ds(pl.multiple_of(owner * width + at, cut), cut)
            add(ref.at[:, :depth], w_ref.at[1:, :, cols])
            rows = pl.ds(pl.multiple_of(owner * part, part), part)
            add(ref.at[:, depth:], wout_ref.at[1:, rows, at : at + cut])
        return copies

    return place, parts, [[w_in], [from_x], [from_y], diagonal], dps


def two_terms(square):
    hi = square.astype(BF16).astype(F32)
    lane = lax.broadcasted_iota(jnp.int32, (square.shape[0], 128), 1)
    return jnp.where(lane == 0, hi, jnp.where(lane == 1, square - hi, 0.0)).astype(BF16)


def up_kernel(chunks, pieces, x_ref, *refs):
    w_in_refs, refs = refs[: sum(pieces)], refs[sum(pieces) :]
    w_ref, local_ref, half_ref, send_ref, normed_ref = refs
    m = lax.axis_index("mp")
    depth = x_ref.shape[1]
    x = x_ref[...]
    square = None
    at = 0
    for k, n in enumerate(pieces):
        block = jnp.concatenate([r[...] for r in w_in_refs[at : at + n]], axis=0)
        at += n
        hidden = jnp.dot(x, block[:depth], preferred_element_type=F32)
        part = jnp.sum(hidden * hidden, axis=1, keepdims=True)
        square = part if square is None else square + part
        gain = block[depth:].astype(F32)[:1]
        cols = hidden.shape[1]
        normed_ref[:, pl.ds(pl.multiple_of((m ^ k) * cols, cols), cols)] = (hidden * gain).astype(BF16)
        if k == 0:
            local_ref[...] = hidden
    normed = normed_ref[...]
    wide = w_ref.shape[1]
    each = wide // chunks
    for c in range(chunks):
        at = slice(c * each, (c + 1) * each)
        half = jnp.dot(normed, w_ref[:, at], preferred_element_type=F32)
        half_ref[:, at] = half
        send_ref[:, at] = half.astype(BF16)
    half_ref[:, wide:] = jnp.broadcast_to(square, (x.shape[0], 128))
    send_ref[:, wide:] = two_terms(square)


def down_kernel(chunks, half_ref, other_ref, local_ref, w_ref, _, out_ref, part_ref):
    units, wide = w_ref.shape
    each = wide // chunks
    square = half_ref[:, units : units + 1] + jnp.sum(other_ref[:, units:].astype(F32), axis=1, keepdims=True)
    inv = lax.rsqrt(square / DM + EPSILON)
    up = (half_ref[:, :units] + other_ref[:, :units].astype(F32)) * inv
    hidden = jax.nn.gelu(up, approximate=True).astype(BF16)
    for c in range(chunks):
        at = slice(c * each, (c + 1) * each)
        part_ref[:, at] = jnp.dot(hidden, w_ref[:, at], preferred_element_type=F32)
    m = lax.axis_index("mp")
    cols = local_ref.shape[1]
    own = pl.ds(pl.multiple_of(m * cols, cols), cols)
    part_ref[:, own] = part_ref[:, own] + local_ref[...]
    out_ref[...] = part_ref[...].astype(BF16)


def finish_kernel(sections, mps, dps, got_ref, bounds_ref, sums_ev_ref, sums_g_ref, wout_ref, out_ref, pooled_ref):
    pooled_ref[...] = pool(dps, bounds_ref, sums_ev_ref[...], sums_g_ref, wout_ref).astype(BF16)
    got = got_ref[...].astype(F32)
    take, wide = out_ref.shape[0], got.shape[1]
    for s in range(sections):
        total = got[s * mps * take : (s * mps + 1) * take]
        for k in range(s * mps + 1, (s + 1) * mps):
            total = total + got[k * take : (k + 1) * take]
        out_ref[:, s * wide : (s + 1) * wide] = total.astype(BF16)


def per_device(sections, dps, mps, events, hist_len, sess_len, w_uvqk, w_out, attn_gain, w_in, ffn_gain, w_up, w_down):
    events = events[0]
    length, width = events.shape
    sess = sess_len.shape[1]
    take = sess // MICRO
    peers = sections * mps
    rows = take * peers
    cols = w_in.shape[1]
    units = w_up.shape[1]
    half_width = w_down.shape[1]
    group = ("section", "mp")
    first = take * SESS_MAX
    rest = length - first

    gain = jnp.broadcast_to(attn_gain, (8, width))
    ends = jnp.sum(jnp.where(jnp.tri(sess, dtype=jnp.bool_), sess_len, 0), axis=1)
    bounds = jnp.stack([ends - sess_len[0], jnp.minimum(ends, hist_len), jnp.broadcast_to(hist_len, ends.shape)])
    bounds = jnp.broadcast_to(bounds.astype(F32)[:, :, None], (3, sess, 128))
    place, parts, w_in_blocks, dps = gather_weights(w_uvqk, w_out, w_in, ffn_gain, sections, dps, mps)

    micro_rows, full_w, full_wout, kv_first, sums_ev, sums_g = call(
        functools.partial(first_kernel, place, dps, (peers, take), len(parts)),
        "encode_first",
        [bounds, events[:first], gain, *parts],
        [
            ((rows, width), BF16),
            ((width, 4 * width), BF16),
            ((width, width), BF16),
            ((first, 2 * width), BF16),
            ((sess, width), F32),
            ((sess, width), F32),
        ],
        [
            pltpu.VMEM((first, width), BF16),
            pltpu.VMEM((first, width), F32),
            pltpu.VMEM((first, width), F32),
            pltpu.SemaphoreType.DMA((32,)),
        ],
        16,
        8 * first * width * width + 2 * first * first * width,
        6 * 1024 * 1024,
        4 * first * width + HEADS * first * first,
    )
    arrived = lax.all_to_all(
        micro_rows.reshape(peers, take, width), group, split_axis=0, concat_axis=0, tiled=True
    ).reshape(rows, width)
    blocks = [piece for block in w_in_blocks for piece in block]
    local, half, half_send = call(
        functools.partial(up_kernel, 4, [len(block) for block in w_in_blocks]),
        "up_half",
        [arrived, *blocks, w_up],
        [((rows, cols), F32), ((rows, units + 128), F32), ((rows, units + 128), BF16)],
        [pltpu.VMEM((rows, w_up.shape[0]), BF16)],
        10,
        2 * rows * w_up.size,
        2 * w_up.size,
    )
    other = swap(half_send, "section", sections, 1)
    gate, queries, kv_rest, sums_ev = call(
        functools.partial(project_kernel, dps, first),
        "project_rest",
        [bounds, events[first:], full_w, sums_ev, local],
        [((rest, width), BF16), ((rest, width), BF16), ((rest, 2 * width), BF16), ((sess, width), F32)],
        [],
        10,
        8 * rest * width * width,
        6 * 1024 * 1024,
        4 * rest * width,
    )
    (partial,) = call(
        functools.partial(down_kernel, 4),
        "down_part",
        [half, other, local, w_down, sums_ev],
        [((rows, half_width), BF16)],
        [pltpu.VMEM((rows, half_width), F32)],
        8,
        2 * rows * w_down.size,
        2 * w_down.size,
        rows * units,
    )
    arrived = lax.all_to_all(
        partial.reshape(peers, take, half_width), group, split_axis=0, concat_axis=0, tiled=True
    ).reshape(rows, half_width)
    (sums_g,) = call(
        functools.partial(attend_kernel, first),
        "attend_rest",
        [bounds, gain, gate, queries, kv_first, kv_rest, sums_g, partial],
        [((sess, width), F32)],
        [pltpu.VMEM((rest, width), F32)],
        10,
        4 * rest * length * width,
        6 * 1024 * 1024,
        HEADS * rest * length,
    )
    cross_out, pooled = call(
        functools.partial(finish_kernel, sections, mps, dps),
        "finish",
        [arrived, bounds, sums_ev, sums_g, full_wout],
        [((take, half_width * sections), BF16), ((sess, width), BF16)],
        [],
        8,
        6 * sess * width * width,
        2 * 1024 * 1024,
    )
    return (pooled, cross_out)


def solution(mesh):
    sizes = [mesh.shape[name] for name in ("section", "dp", "mp")]
    return jax.shard_map(
        functools.partial(per_device, *sizes),
        mesh=mesh,
        in_specs=(
            P(("section", "dp", "mp"), None, None),
            P(("section", "dp", "mp")),
            P(("section", "dp", "mp"), None),
            P("dp", None),
            P("dp", None),
            P(),
            P(None, ("section", "mp")),
            P(None, ("section", "mp")),
            P("section", "mp"),
            P("mp", "section"),
        ),
        out_specs=(P(("section", "dp", "mp"), None), P(("section", "dp", "mp"), None)),
        check_vma=False,
    )
```

```python
import functools

import jax
import jax.numpy as jnp
from jax import lax
from jax.experimental import pallas as pl
from jax.experimental.pallas import tpu as pltpu
from jax.sharding import PartitionSpec as P

HEADS = 4
DM = 4096
MICRO = 4
SESS_MAX = 64
EPSILON = 1e-06
F32 = jnp.float32
BF16 = jnp.bfloat16

VMEM = pl.BlockSpec(memory_space=pltpu.VMEM)


def swap(x, axis, size, flip):
    return lax.ppermute(x, axis, [(i, i ^ flip) for i in range(size)])


def silu_half(h):
    return h + h * jnp.tanh(h)


def in_order(ref, at, dps):
    if dps == 1:
        return ref[at, :]
    z = lax.axis_index("dp")
    cols = ref.shape[1] // dps
    return jnp.concatenate([ref[at, pl.ds(pl.multiple_of((z ^ k) * cols, cols), cols)] for k in range(dps)], axis=1)


def project(dps, row0, hist, ev_ref, w_ref, gate_ref, q_ref, kv_ref):
    rows, width = ev_ref.shape
    step = min(rows, 256)
    for r in range(0, rows, step):
        at = slice(r, r + step)
        x = in_order(ev_ref, at, dps)
        row_pos = lax.broadcasted_iota(jnp.int32, (step, 1), 0).astype(F32) + (row0 + r)

        def act(n):
            part = jnp.dot(x, w_ref[:, n * width : (n + 1) * width], preferred_element_type=F32)
            return silu_half(part * 0.5)

        gate_ref[at, :] = act(0).astype(gate_ref.dtype)
        kv_ref[at, :width] = jnp.where(row_pos < hist, act(1), 0.0).astype(BF16)
        q_ref[at, :] = act(2).astype(BF16)
        kv_ref[at, width:] = act(3).astype(BF16)


def attend(q_ref, kv_refs, gate_ref, gain_ref, att_ref):
    rows, width = q_ref.shape
    head = width // HEADS
    step = min(rows, 256)
    blocks = [(ref, r) for ref in kv_refs for r in range(0, ref.shape[0], step)]
    tri = lax.broadcasted_iota(jnp.int32, (step, step), 1) <= lax.broadcasted_iota(
        jnp.int32, (step, step), 0
    )
    before = len(blocks) - rows // step
    for i in range(rows // step):
        at = slice(i * step, (i + 1) * step)
        for h in range(HEADS):
            q = q_ref[at, h * head : (h + 1) * head]
            total = None
            for j in range(before + i + 1):
                ref, r = blocks[j]
                k = ref[r : r + step, width + h * head : width + (h + 1) * head]
                v = ref[r : r + step, h * head : (h + 1) * head]
                s = lax.dot_general(q, k, (((1,), (1,)), ((), ())), preferred_element_type=F32)
                wts = silu_half(s * (0.5 * head**-0.5))
                if j == before + i:
                    wts = jnp.where(tri, wts, 0.0)
                mixed = jnp.dot(wts.astype(BF16), v, preferred_element_type=F32)
                total = mixed if total is None else total + mixed
            att_ref[at, h * head : (h + 1) * head] = total
    att = att_ref[...]
    inv = lax.rsqrt(jnp.mean(att * att, axis=1, keepdims=True) + EPSILON)
    return (att * inv * gain_ref[:1] * gate_ref[...].astype(F32)).astype(BF16)


def membership(bounds_ref, row0, rows):
    starts, ends = bounds_ref[0, :, :1], bounds_ref[1, :, :1]
    pos = (lax.broadcasted_iota(jnp.int32, (starts.shape[0], rows), 1) + row0).astype(F32)
    return jnp.where((pos >= starts) & (pos < ends), 1.0, 0.0).astype(BF16)


def pool(dps, bounds_ref, sums_ev, sums_ref, wout_ref):
    n_valid = jnp.maximum(bounds_ref[1, :, :1] - bounds_ref[0, :, :1], 1.0)
    sess = sums_ev.shape[0]
    sums_g = in_order(sums_ref, slice(None), dps)
    hi = sums_g.astype(BF16)
    rest = sums_g - hi.astype(F32)
    mid = rest.astype(BF16)
    low = (rest - mid.astype(F32)).astype(BF16)
    terms = jnp.dot(jnp.concatenate([low, mid, hi], axis=0), wout_ref[...], preferred_element_type=F32)
    return (terms[:sess] + terms[sess : 2 * sess] + terms[2 * sess :] + sums_ev) / n_valid


def first_kernel(place, dps, copies_out, n_parts, bounds_ref, ev_ref, gain_ref, *refs):
    parts, refs = refs[:n_parts], refs[n_parts:]
    pooled_ref, w_ref, wout_ref, kv_ref, sums_ev_ref, sums_g_ref, q_ref, gate_ref, att_ref = refs
    place(parts, w_ref, wout_ref)
    member = membership(bounds_ref, 0, ev_ref.shape[0])
    sums_ev = jnp.dot(member, ev_ref[...], preferred_element_type=F32)
    sums_ev_ref[...] = sums_ev
    project(dps, 0, bounds_ref[2, :1, :1], ev_ref, w_ref, gate_ref, q_ref, kv_ref)
    gated = attend(q_ref, [kv_ref], gate_ref, gain_ref, att_ref)
    sums_g_ref[...] = jnp.dot(member, gated, preferred_element_type=F32)
    out = pool(dps, bounds_ref, sums_ev, sums_g_ref, wout_ref)
    peers, take = copies_out
    pooled_ref[...] = jnp.concatenate([out[:take]] * peers, axis=0).astype(BF16)


def halves(ref):
    cols = ref.shape[1] // 2
    return ref.at[:, :cols], ref.at[:, cols:]


def project_kernel(dps, row0, bounds_ref, ev_ref, w_ref, sums_ev_ref, _, qg_ref, kv_ref, out_ref):
    q_ref, gate_ref = halves(qg_ref)
    project(dps, row0, bounds_ref[2, :1, :1], ev_ref, w_ref, gate_ref, q_ref, kv_ref)
    member = membership(bounds_ref, row0, ev_ref.shape[0])
    out_ref[...] = sums_ev_ref[...] + jnp.dot(member, ev_ref[...], preferred_element_type=F32)


def attend_kernel(row0, bounds_ref, gain_ref, qg_ref, kv_first, kv_ref, sums_ref, _, out_ref, att_ref):
    q_ref, gate_ref = halves(qg_ref)
    member = membership(bounds_ref, row0, q_ref.shape[0])
    gated = attend(q_ref, [kv_first, kv_ref], gate_ref, gain_ref, att_ref)
    out_ref[...] = sums_ref[...] + jnp.dot(member, gated, preferred_element_type=F32)


def call(kernel, name, operands, out_shape, scratch, mib, flops, size, transcendentals=0):
    return pl.pallas_call(
        kernel,
        in_specs=[VMEM] * len(operands),
        out_specs=[VMEM] * len(out_shape),
        out_shape=[jax.ShapeDtypeStruct(shape, kind) for shape, kind in out_shape],
        scratch_shapes=scratch,
        compiler_params=pltpu.CompilerParams(vmem_limit_bytes=mib * 1024 * 1024),
        cost_estimate=pl.CostEstimate(flops=flops, bytes_accessed=size, transcendentals=transcendentals),
        name=name,
    )(*operands)


def parity(m):
    return (m & 1) ^ ((m >> 1) & 1)


def split_kernel(*refs):
    *parts, left_ref, right_ref = refs
    half = left_ref.shape[2]
    for k, part in enumerate(parts):
        left_ref[k] = part[:, :half]
        right_ref[k] = part[:, half:]


def gather_weights(w_uvqk, w_out, w_in, ffn_gain, sections, dps, mps):
    depth, wide = w_uvqk.shape
    width = w_out.shape[1]
    w_in = jnp.concatenate([w_in, jnp.broadcast_to(ffn_gain, (16, w_in.shape[1]))], axis=0)
    if (sections, dps, mps) != (2, 4, 4) or wide != 4 * width or depth % 128:
        ws = [lax.all_gather(x, "dp", axis=0, tiled=True) for x in (w_uvqk, w_out)]
        blocks = [[w_in]] + [[swap(w_in, "mp", mps, k)] for k in range(1, mps)]

        def place_whole(parts, w_ref, wout_ref):
            w_ref[...] = parts[0][...]
            wout_ref[...] = parts[1][...]

        return place_whole, ws, blocks, 1

    part = depth // 4
    cut = width // 2
    sec, m = lax.axis_index("section"), lax.axis_index("mp")
    share = sec * 2 + parity(m)
    mine = jnp.concatenate(
        [
            lax.dynamic_slice_in_dim(w_uvqk, share * width, width, 1),
            lax.dynamic_slice_in_dim(w_out, share * part, part, 0),
        ],
        axis=0,
    )
    near, far = swap(mine, "dp", dps, 1), swap(mine, "dp", dps, 2)
    parts, owners = [w_uvqk[:, : wide // 2], w_uvqk[:, wide // 2 :], w_out[: depth // 2], w_out[depth // 2 :]], []
    for at, got in ((1, [near, far]), (3, [swap(far, "dp", dps, 1)])):
        left, right = call(
            split_kernel,
            f"split_{at}",
            got,
            [((len(got), depth + part, cut), BF16)] * 2,
            [],
            8,
            0,
            16 * 1024 * 1024,
        )
        plane = [left, right, swap(left, "mp", mps, 1), swap(right, "mp", mps, 2)]
        parts = parts + plane + [swap(p, "section", sections, 1) for p in plane]
        owners = owners + [(at, i // 4, i // 2 % 2, i % 2 * cut) for i in range(8)]

    from_x, from_y = swap(w_in, "mp", mps, 1), swap(w_in, "mp", mps, 2)
    middle = w_in.shape[0] // 32 * 16
    diagonal = [swap(from_x[:middle], "mp", mps, 2), swap(from_y[middle:], "mp", mps, 1)]

    def place(parts, w_ref, wout_ref):
        sec, m = lax.axis_index("section"), lax.axis_index("mp")
        for i in range(2):
            w_ref[:depth, i * (wide // 2) : (i + 1) * (wide // 2)] = parts[i][...]
            wout_ref[i * (depth // 2) : (i + 1) * (depth // 2)] = parts[2 + i][...]
        for ref, (first, other_sec, other_half, at) in zip(parts[4:], owners):
            owner = (sec ^ other_sec) * 2 + (parity(m) ^ other_half)
            cols = pl.ds(pl.multiple_of(owner * width + at, cut), cut)
            for k in range(ref.shape[0]):
                row = (first + k) * depth
                w_ref[row : row + depth, cols] = ref[k, :depth]
                rows = pl.ds(pl.multiple_of(row + owner * part, part), part)
                wout_ref[rows, at : at + cut] = ref[k, depth:]

    return place, parts, [[w_in], [from_x], [from_y], diagonal], dps


def two_terms(square):
    hi = square.astype(BF16).astype(F32)
    lane = lax.broadcasted_iota(jnp.int32, (square.shape[0], 128), 1)
    return jnp.where(lane == 0, hi, jnp.where(lane == 1, square - hi, 0.0)).astype(BF16)


def up_kernel(chunks, pieces, x_ref, *refs):
    w_in_refs, refs = refs[: sum(pieces)], refs[sum(pieces) :]
    w_ref, local_ref, half_ref, send_ref, normed_ref = refs
    m = lax.axis_index("mp")
    depth = x_ref.shape[1]
    x = x_ref[...]
    square = None
    at = 0
    for k, n in enumerate(pieces):
        block = jnp.concatenate([r[...] for r in w_in_refs[at : at + n]], axis=0)
        at += n
        hidden = jnp.dot(x, block[:depth], preferred_element_type=F32)
        part = jnp.sum(hidden * hidden, axis=1, keepdims=True)
        square = part if square is None else square + part
        gain = block[depth:].astype(F32)[:1]
        cols = hidden.shape[1]
        normed_ref[:, pl.ds(pl.multiple_of((m ^ k) * cols, cols), cols)] = (hidden * gain).astype(BF16)
        if k == 0:
            local_ref[...] = hidden
    normed = normed_ref[...]
    wide = w_ref.shape[1]
    each = wide // chunks
    for c in range(chunks):
        at = slice(c * each, (c + 1) * each)
        half = jnp.dot(normed, w_ref[:, at], preferred_element_type=F32)
        half_ref[:, at] = half
        send_ref[:, at] = half.astype(BF16)
    half_ref[:, wide:] = jnp.broadcast_to(square, (x.shape[0], 128))
    send_ref[:, wide:] = two_terms(square)


def down_kernel(chunks, half_ref, other_ref, local_ref, w_ref, _, out_ref, part_ref):
    units, wide = w_ref.shape
    each = wide // chunks
    square = half_ref[:, units : units + 1] + jnp.sum(other_ref[:, units:].astype(F32), axis=1, keepdims=True)
    inv = lax.rsqrt(square / DM + EPSILON)
    up = (half_ref[:, :units] + other_ref[:, :units].astype(F32)) * inv
    hidden = jax.nn.gelu(up, approximate=True).astype(BF16)
    for c in range(chunks):
        at = slice(c * each, (c + 1) * each)
        part_ref[:, at] = jnp.dot(hidden, w_ref[:, at], preferred_element_type=F32)
    m = lax.axis_index("mp")
    cols = local_ref.shape[1]
    own = pl.ds(pl.multiple_of(m * cols, cols), cols)
    part_ref[:, own] = part_ref[:, own] + local_ref[...]
    out_ref[...] = part_ref[...].astype(BF16)


def finish_kernel(sections, mps, dps, got_ref, bounds_ref, sums_ev_ref, sums_g_ref, wout_ref, out_ref, pooled_ref):
    pooled_ref[...] = pool(dps, bounds_ref, sums_ev_ref[...], sums_g_ref, wout_ref).astype(BF16)
    got = got_ref[...].astype(F32)
    take, wide = out_ref.shape[0], got.shape[1]
    for s in range(sections):
        total = got[s * mps * take : (s * mps + 1) * take]
        for k in range(s * mps + 1, (s + 1) * mps):
            total = total + got[k * take : (k + 1) * take]
        out_ref[:, s * wide : (s + 1) * wide] = total.astype(BF16)


def per_device(sections, dps, mps, events, hist_len, sess_len, w_uvqk, w_out, attn_gain, w_in, ffn_gain, w_up, w_down):
    events = events[0]
    length, width = events.shape
    sess = sess_len.shape[1]
    take = sess // MICRO
    peers = sections * mps
    rows = take * peers
    cols = w_in.shape[1]
    units = w_up.shape[1]
    half_width = w_down.shape[1]
    group = ("section", "mp")
    first = take * SESS_MAX
    rest = length - first

    gain = jnp.broadcast_to(attn_gain, (8, width))
    ends = jnp.sum(jnp.where(jnp.tri(sess, dtype=jnp.bool_), sess_len, 0), axis=1)
    bounds = jnp.stack([ends - sess_len[0], jnp.minimum(ends, hist_len), jnp.broadcast_to(hist_len, ends.shape)])
    bounds = jnp.broadcast_to(bounds.astype(F32)[:, :, None], (3, sess, 128))
    place, parts, w_in_blocks, dps = gather_weights(w_uvqk, w_out, w_in, ffn_gain, sections, dps, mps)

    micro_rows, full_w, full_wout, kv_first, sums_ev, sums_g = call(
        functools.partial(first_kernel, place, dps, (peers, take), len(parts)),
        "encode_first",
        [bounds, events[:first], gain, *parts],
        [
            ((rows, width), BF16),
            ((width, 4 * width), BF16),
            ((width, width), BF16),
            ((first, 2 * width), BF16),
            ((sess, width), F32),
            ((sess, width), F32),
        ],
        [
            pltpu.VMEM((first, width), BF16),
            pltpu.VMEM((first, width), F32),
            pltpu.VMEM((first, width), F32),
        ],
        16,
        8 * first * width * width + 2 * first * first * width,
        6 * 1024 * 1024,
        4 * first * width + HEADS * first * first,
    )
    arrived = lax.all_to_all(
        micro_rows.reshape(peers, take, width), group, split_axis=0, concat_axis=0, tiled=True
    ).reshape(rows, width)
    blocks = [piece for block in w_in_blocks for piece in block]
    local, half, half_send = call(
        functools.partial(up_kernel, 4, [len(block) for block in w_in_blocks]),
        "up_half",
        [arrived, *blocks, w_up],
        [((rows, cols), F32), ((rows, units + 128), F32), ((rows, units + 128), BF16)],
        [pltpu.VMEM((rows, w_up.shape[0]), BF16)],
        10,
        2 * rows * w_up.size,
        2 * w_up.size,
    )
    other = swap(half_send, "section", sections, 1)
    queries_gate, kv_rest, sums_ev = call(
        functools.partial(project_kernel, dps, first),
        "project_rest",
        [bounds, events[first:], full_w, sums_ev, local],
        [((rest, 2 * width), BF16), ((rest, 2 * width), BF16), ((sess, width), F32)],
        [],
        10,
        8 * rest * width * width,
        6 * 1024 * 1024,
        4 * rest * width,
    )
    (partial,) = call(
        functools.partial(down_kernel, 4),
        "down_part",
        [half, other, local, w_down, sums_ev],
        [((rows, half_width), BF16)],
        [pltpu.VMEM((rows, half_width), F32)],
        8,
        2 * rows * w_down.size,
        2 * w_down.size,
        rows * units,
    )
    arrived = lax.all_to_all(
        partial.reshape(peers, take, half_width), group, split_axis=0, concat_axis=0, tiled=True
    ).reshape(rows, half_width)
    (sums_g,) = call(
        functools.partial(attend_kernel, first),
        "attend_rest",
        [bounds, gain, queries_gate, kv_first, kv_rest, sums_g, partial],
        [((sess, width), F32)],
        [pltpu.VMEM((rest, width), F32)],
        10,
        4 * rest * length * width,
        6 * 1024 * 1024,
        HEADS * rest * length,
    )
    cross_out, pooled = call(
        functools.partial(finish_kernel, sections, mps, dps),
        "finish",
        [arrived, bounds, sums_ev, sums_g, full_wout],
        [((take, half_width * sections), BF16), ((sess, width), BF16)],
        [],
        8,
        6 * sess * width * width,
        2 * 1024 * 1024,
    )
    return (pooled, cross_out)


def solution(mesh):
    sizes = [mesh.shape[name] for name in ("section", "dp", "mp")]
    return jax.shard_map(
        functools.partial(per_device, *sizes),
        mesh=mesh,
        in_specs=(
            P(("section", "dp", "mp"), None, None),
            P(("section", "dp", "mp")),
            P(("section", "dp", "mp"), None),
            P("dp", None),
            P("dp", None),
            P(),
            P(None, ("section", "mp")),
            P(None, ("section", "mp")),
            P("section", "mp"),
            P("mp", "section"),
        ),
        out_specs=(P(("section", "dp", "mp"), None), P(("section", "dp", "mp"), None)),
        check_vma=False,
    )
```

```python
import functools

import jax
import jax.numpy as jnp
from jax import lax
from jax.experimental import pallas as pl
from jax.experimental.pallas import tpu as pltpu
from jax.sharding import PartitionSpec as P

HEADS = 4
DM = 4096
MICRO = 4
SESS_MAX = 64
EPSILON = 1e-06
F32 = jnp.float32
BF16 = jnp.bfloat16

VMEM = pl.BlockSpec(memory_space=pltpu.VMEM)


def swap(x, axis, size, flip):
    return lax.ppermute(x, axis, [(i, i ^ flip) for i in range(size)])


def silu_half(h):
    return h + h * jnp.tanh(h)


def order_of(dps):
    return [0, *range(2, dps), 1]


def in_order(ref, at, dps):
    if dps == 1:
        return ref[at, :]
    z = lax.axis_index("dp")
    cols = ref.shape[1] // dps
    return jnp.concatenate([ref[at, pl.ds(pl.multiple_of((z ^ k) * cols, cols), cols)] for k in order_of(dps)], axis=1)


def project(dps, row0, hist, ev_ref, w_ref, gate_ref, q_ref, kv_ref):
    rows, width = ev_ref.shape
    step = min(rows, 256)
    for r in range(0, rows, step):
        at = slice(r, r + step)
        x = in_order(ev_ref, at, dps)
        row_pos = lax.broadcasted_iota(jnp.int32, (step, 1), 0).astype(F32) + (row0 + r)

        def act(n):
            part = jnp.dot(x, w_ref[:, n * width : (n + 1) * width], preferred_element_type=F32)
            return silu_half(part * 0.5)

        gate_ref[at, :] = act(0).astype(gate_ref.dtype)
        kv_ref[at, :width] = jnp.where(row_pos < hist, act(1), 0.0).astype(BF16)
        q_ref[at, :] = act(2).astype(BF16)
        kv_ref[at, width:] = act(3).astype(BF16)


def attend(q_ref, kv_refs, gate_ref, gain_ref, att_ref):
    rows, width = q_ref.shape
    head = width // HEADS
    step = min(rows, 256)
    blocks = [(ref, r) for ref in kv_refs for r in range(0, ref.shape[0], step)]
    tri = lax.broadcasted_iota(jnp.int32, (step, step), 1) <= lax.broadcasted_iota(
        jnp.int32, (step, step), 0
    )
    before = len(blocks) - rows // step
    for i in range(rows // step):
        at = slice(i * step, (i + 1) * step)
        for h in range(HEADS):
            q = q_ref[at, h * head : (h + 1) * head]
            total = None
            for j in range(before + i + 1):
                ref, r = blocks[j]
                k = ref[r : r + step, width + h * head : width + (h + 1) * head]
                v = ref[r : r + step, h * head : (h + 1) * head]
                s = lax.dot_general(q, k, (((1,), (1,)), ((), ())), preferred_element_type=F32)
                wts = silu_half(s * (0.5 * head**-0.5))
                if j == before + i:
                    wts = jnp.where(tri, wts, 0.0)
                mixed = jnp.dot(wts.astype(BF16), v, preferred_element_type=F32)
                total = mixed if total is None else total + mixed
            att_ref[at, h * head : (h + 1) * head] = total
    att = att_ref[...]
    inv = lax.rsqrt(jnp.mean(att * att, axis=1, keepdims=True) + EPSILON)
    return (att * inv * gain_ref[:1] * gate_ref[...].astype(F32)).astype(BF16)


def membership(bounds_ref, row0, rows):
    starts, ends = bounds_ref[0, :, :1], bounds_ref[1, :, :1]
    pos = (lax.broadcasted_iota(jnp.int32, (starts.shape[0], rows), 1) + row0).astype(F32)
    return jnp.where((pos >= starts) & (pos < ends), 1.0, 0.0).astype(BF16)


def pool(dps, bounds_ref, sums_ev, sums_ref, wout_ref):
    n_valid = jnp.maximum(bounds_ref[1, :, :1] - bounds_ref[0, :, :1], 1.0)
    sess = sums_ev.shape[0]
    sums_g = in_order(sums_ref, slice(None), dps)
    hi = sums_g.astype(BF16)
    rest = sums_g - hi.astype(F32)
    mid = rest.astype(BF16)
    low = (rest - mid.astype(F32)).astype(BF16)
    terms = jnp.dot(jnp.concatenate([low, mid, hi], axis=0), wout_ref[...], preferred_element_type=F32)
    return (terms[:sess] + terms[sess : 2 * sess] + terms[2 * sess :] + sums_ev) / n_valid


def first_kernel(place, dps, copies_out, n_parts, bounds_ref, ev_ref, gain_ref, *refs):
    parts, refs = refs[:n_parts], refs[n_parts:]
    pooled_ref, w_ref, wout_ref, kv_ref, sums_ev_ref, sums_g_ref, q_ref, gate_ref, att_ref = refs
    place(parts, w_ref, wout_ref)
    member = membership(bounds_ref, 0, ev_ref.shape[0])
    sums_ev = jnp.dot(member, ev_ref[...], preferred_element_type=F32)
    sums_ev_ref[...] = sums_ev
    project(dps, 0, bounds_ref[2, :1, :1], ev_ref, w_ref, gate_ref, q_ref, kv_ref)
    gated = attend(q_ref, [kv_ref], gate_ref, gain_ref, att_ref)
    sums_g_ref[...] = jnp.dot(member, gated, preferred_element_type=F32)
    out = pool(dps, bounds_ref, sums_ev, sums_g_ref, wout_ref)
    peers, take = copies_out
    pooled_ref[...] = jnp.concatenate([out[:take]] * peers, axis=0).astype(BF16)


def halves(ref):
    cols = ref.shape[1] // 2
    return ref.at[:, :cols], ref.at[:, cols:]


def project_kernel(dps, row0, bounds_ref, ev_ref, w_ref, sums_ev_ref, _, qg_ref, kv_ref, out_ref):
    q_ref, gate_ref = halves(qg_ref)
    project(dps, row0, bounds_ref[2, :1, :1], ev_ref, w_ref, gate_ref, q_ref, kv_ref)
    member = membership(bounds_ref, row0, ev_ref.shape[0])
    out_ref[...] = sums_ev_ref[...] + jnp.dot(member, ev_ref[...], preferred_element_type=F32)


def attend_kernel(row0, bounds_ref, gain_ref, qg_ref, kv_first, kv_ref, sums_ref, _, out_ref, att_ref):
    q_ref, gate_ref = halves(qg_ref)
    member = membership(bounds_ref, row0, q_ref.shape[0])
    gated = attend(q_ref, [kv_first, kv_ref], gate_ref, gain_ref, att_ref)
    out_ref[...] = sums_ref[...] + jnp.dot(member, gated, preferred_element_type=F32)


def call(kernel, name, operands, out_shape, scratch, mib, flops, size, transcendentals=0):
    return pl.pallas_call(
        kernel,
        in_specs=[VMEM] * len(operands),
        out_specs=[VMEM] * len(out_shape),
        out_shape=[jax.ShapeDtypeStruct(shape, kind) for shape, kind in out_shape],
        scratch_shapes=scratch,
        compiler_params=pltpu.CompilerParams(vmem_limit_bytes=mib * 1024 * 1024),
        cost_estimate=pl.CostEstimate(flops=flops, bytes_accessed=size, transcendentals=transcendentals),
        name=name,
    )(*operands)


def parity(m):
    return (m & 1) ^ ((m >> 1) & 1)


def split_kernel(*refs):
    *parts, left_ref, right_ref, both_ref = refs
    half = left_ref.shape[2]
    for k, part in enumerate(parts):
        for i, ref in enumerate((left_ref, right_ref)):
            piece = part[:, i * half : (i + 1) * half]
            ref[k] = piece
            both_ref[i, k] = piece


def merge_kernel(left_ref, right_ref, next_ref, both_ref, next_out):
    both_ref[0] = left_ref[...]
    both_ref[1] = right_ref[...]
    next_out[...] = next_ref[...]


def gather_weights(w_uvqk, w_out, w_in, ffn_gain, sections, dps, mps):
    depth, wide = w_uvqk.shape
    width = w_out.shape[1]
    w_in = jnp.concatenate([w_in, jnp.broadcast_to(ffn_gain, (16, w_in.shape[1]))], axis=0)
    if (sections, mps) != (2, 4) or wide != 4 * width or depth % 128:
        ws = [lax.all_gather(x, "dp", axis=0, tiled=True) for x in (w_uvqk, w_out)]
        blocks = [[w_in]] + [[swap(w_in, "mp", mps, k)] for k in range(1, mps)]

        def place_whole(parts, w_ref, wout_ref):
            w_ref[...] = parts[0][...]
            wout_ref[...] = parts[1][...]

        return place_whole, ws, blocks, 1

    part = depth // 4
    cut = width // 2
    sec, m = lax.axis_index("section"), lax.axis_index("mp")
    share = sec * 2 + parity(m)
    mine = jnp.concatenate(
        [
            lax.dynamic_slice_in_dim(w_uvqk, share * width, width, 1),
            lax.dynamic_slice_in_dim(w_out, share * part, part, 0),
        ],
        axis=0,
    )
    got = [swap(mine, "dp", dps, k) for k in order_of(dps)[1:]]
    size = (len(got), depth + part, cut)
    left, right, both = call(
        split_kernel, "split", got, [(size, BF16), (size, BF16), ((2, *size), BF16)], [], 8, 0, 16 * 1024 * 1024
    )
    from_x, from_y = swap(w_in, "mp", mps, 1), swap(w_in, "mp", mps, 2)
    others, w_in_later = call(
        merge_kernel,
        "merge",
        [swap(left, "mp", mps, 1), swap(right, "mp", mps, 2), w_in],
        [((2, *size), BF16), (w_in.shape, BF16)],
        [],
        8,
        0,
        1024 * 1024,
    )
    plane = [both, others]
    parts = [w_uvqk[:, : wide // 2], w_uvqk[:, wide // 2 :], w_out[: depth // 2], w_out[depth // 2 :]]
    parts = parts + plane + [swap(p, "section", sections, 1) for p in plane]
    blocks = [[w_in], [from_x], [from_y], [swap(w_in_later, "mp", mps, 3)]]

    def place(parts, w_ref, wout_ref):
        sec, m = lax.axis_index("section"), lax.axis_index("mp")
        for i in range(2):
            w_ref[:depth, i * (wide // 2) : (i + 1) * (wide // 2)] = parts[i][...]
            wout_ref[i * (depth // 2) : (i + 1) * (depth // 2)] = parts[2 + i][...]
        for i, ref in enumerate(parts[4:]):
            owner = (sec ^ (i // 2)) * 2 + (parity(m) ^ (i % 2))
            for side in range(2):
                at = side * cut
                cols = pl.ds(pl.multiple_of(owner * width + at, cut), cut)
                for k in range(dps - 1):
                    row = (k + 1) * depth
                    w_ref[row : row + depth, cols] = ref[side, k, :depth]
                    rows = pl.ds(pl.multiple_of(row + owner * part, part), part)
                    wout_ref[rows, at : at + cut] = ref[side, k, depth:]

    return place, parts, blocks, dps


def two_terms(square):
    hi = square.astype(BF16).astype(F32)
    lane = lax.broadcasted_iota(jnp.int32, (square.shape[0], 128), 1)
    return jnp.where(lane == 0, hi, jnp.where(lane == 1, square - hi, 0.0)).astype(BF16)


def up_kernel(chunks, pieces, x_ref, *refs):
    w_in_refs, refs = refs[: sum(pieces)], refs[sum(pieces) :]
    w_ref, local_ref, half_ref, send_ref, normed_ref = refs
    m = lax.axis_index("mp")
    depth = x_ref.shape[1]
    x = x_ref[...]
    square = None
    at = 0
    for k, n in enumerate(pieces):
        block = jnp.concatenate([r[...] for r in w_in_refs[at : at + n]], axis=0)
        at += n
        hidden = jnp.dot(x, block[:depth], preferred_element_type=F32)
        part = jnp.sum(hidden * hidden, axis=1, keepdims=True)
        square = part if square is None else square + part
        gain = block[depth:].astype(F32)[:1]
        cols = hidden.shape[1]
        normed_ref[:, pl.ds(pl.multiple_of((m ^ k) * cols, cols), cols)] = (hidden * gain).astype(BF16)
        if k == 0:
            local_ref[...] = hidden
    normed = normed_ref[...]
    wide = w_ref.shape[1]
    each = wide // chunks
    for c in range(chunks):
        at = slice(c * each, (c + 1) * each)
        half = jnp.dot(normed, w_ref[:, at], preferred_element_type=F32)
        half_ref[:, at] = half
        send_ref[:, at] = half.astype(BF16)
    half_ref[:, wide:] = jnp.broadcast_to(square, (x.shape[0], 128))
    send_ref[:, wide:] = two_terms(square)


def down_kernel(chunks, half_ref, other_ref, local_ref, w_ref, _, out_ref, part_ref):
    units, wide = w_ref.shape
    each = wide // chunks
    square = half_ref[:, units : units + 1] + jnp.sum(other_ref[:, units:].astype(F32), axis=1, keepdims=True)
    inv = lax.rsqrt(square / DM + EPSILON)
    up = (half_ref[:, :units] + other_ref[:, :units].astype(F32)) * inv
    hidden = jax.nn.gelu(up, approximate=True).astype(BF16)
    for c in range(chunks):
        at = slice(c * each, (c + 1) * each)
        part_ref[:, at] = jnp.dot(hidden, w_ref[:, at], preferred_element_type=F32)
    m = lax.axis_index("mp")
    cols = local_ref.shape[1]
    own = pl.ds(pl.multiple_of(m * cols, cols), cols)
    part_ref[:, own] = part_ref[:, own] + local_ref[...]
    out_ref[...] = part_ref[...].astype(BF16)


def finish_kernel(sections, mps, dps, got_ref, bounds_ref, sums_ev_ref, sums_g_ref, wout_ref, out_ref, pooled_ref):
    pooled_ref[...] = pool(dps, bounds_ref, sums_ev_ref[...], sums_g_ref, wout_ref).astype(BF16)
    got = got_ref[...].astype(F32)
    take, wide = out_ref.shape[0], got.shape[1]
    for s in range(sections):
        total = got[s * mps * take : (s * mps + 1) * take]
        for k in range(s * mps + 1, (s + 1) * mps):
            total = total + got[k * take : (k + 1) * take]
        out_ref[:, s * wide : (s + 1) * wide] = total.astype(BF16)


def per_device(sections, dps, mps, events, hist_len, sess_len, w_uvqk, w_out, attn_gain, w_in, ffn_gain, w_up, w_down):
    events = events[0]
    length, width = events.shape
    sess = sess_len.shape[1]
    take = sess // MICRO
    peers = sections * mps
    rows = take * peers
    cols = w_in.shape[1]
    units = w_up.shape[1]
    half_width = w_down.shape[1]
    group = ("section", "mp")
    first = take * SESS_MAX
    rest = length - first

    gain = jnp.broadcast_to(attn_gain, (8, width))
    ends = jnp.sum(jnp.where(jnp.tri(sess, dtype=jnp.bool_), sess_len, 0), axis=1)
    bounds = jnp.stack([ends - sess_len[0], jnp.minimum(ends, hist_len), jnp.broadcast_to(hist_len, ends.shape)])
    bounds = jnp.broadcast_to(bounds.astype(F32)[:, :, None], (3, sess, 128))
    place, parts, w_in_blocks, dps = gather_weights(w_uvqk, w_out, w_in, ffn_gain, sections, dps, mps)

    micro_rows, full_w, full_wout, kv_first, sums_ev, sums_g = call(
        functools.partial(first_kernel, place, dps, (peers, take), len(parts)),
        "encode_first",
        [bounds, events[:first], gain, *parts],
        [
            ((rows, width), BF16),
            ((width, 4 * width), BF16),
            ((width, width), BF16),
            ((first, 2 * width), BF16),
            ((sess, width), F32),
            ((sess, width), F32),
        ],
        [
            pltpu.VMEM((first, width), BF16),
            pltpu.VMEM((first, width), F32),
            pltpu.VMEM((first, width), F32),
        ],
        16,
        8 * first * width * width + 2 * first * first * width,
        6 * 1024 * 1024,
        4 * first * width + HEADS * first * first,
    )
    arrived = lax.all_to_all(
        micro_rows.reshape(peers, take, width), group, split_axis=0, concat_axis=0, tiled=True
    ).reshape(rows, width)
    blocks = [piece for block in w_in_blocks for piece in block]
    local, half, half_send = call(
        functools.partial(up_kernel, 4, [len(block) for block in w_in_blocks]),
        "up_half",
        [arrived, *blocks, w_up],
        [((rows, cols), F32), ((rows, units + 128), F32), ((rows, units + 128), BF16)],
        [pltpu.VMEM((rows, w_up.shape[0]), BF16)],
        10,
        2 * rows * w_up.size,
        2 * w_up.size,
    )
    other = swap(half_send, "section", sections, 1)
    queries_gate, kv_rest, sums_ev = call(
        functools.partial(project_kernel, dps, first),
        "project_rest",
        [bounds, events[first:], full_w, sums_ev, local],
        [((rest, 2 * width), BF16), ((rest, 2 * width), BF16), ((sess, width), F32)],
        [],
        10,
        8 * rest * width * width,
        6 * 1024 * 1024,
        4 * rest * width,
    )
    (partial,) = call(
        functools.partial(down_kernel, 4),
        "down_part",
        [half, other, local, w_down, sums_ev],
        [((rows, half_width), BF16)],
        [pltpu.VMEM((rows, half_width), F32)],
        8,
        2 * rows * w_down.size,
        2 * w_down.size,
        rows * units,
    )
    arrived = lax.all_to_all(
        partial.reshape(peers, take, half_width), group, split_axis=0, concat_axis=0, tiled=True
    ).reshape(rows, half_width)
    (sums_g,) = call(
        functools.partial(attend_kernel, first),
        "attend_rest",
        [bounds, gain, queries_gate, kv_first, kv_rest, sums_g, partial],
        [((sess, width), F32)],
        [pltpu.VMEM((rest, width), F32)],
        10,
        4 * rest * length * width,
        6 * 1024 * 1024,
        HEADS * rest * length,
    )
    cross_out, pooled = call(
        functools.partial(finish_kernel, sections, mps, dps),
        "finish",
        [arrived, bounds, sums_ev, sums_g, full_wout],
        [((take, half_width * sections), BF16), ((sess, width), BF16)],
        [],
        8,
        6 * sess * width * width,
        2 * 1024 * 1024,
    )
    return (pooled, cross_out)


def solution(mesh):
    sizes = [mesh.shape[name] for name in ("section", "dp", "mp")]
    return jax.shard_map(
        functools.partial(per_device, *sizes),
        mesh=mesh,
        in_specs=(
            P(("section", "dp", "mp"), None, None),
            P(("section", "dp", "mp")),
            P(("section", "dp", "mp"), None),
            P("dp", None),
            P("dp", None),
            P(),
            P(None, ("section", "mp")),
            P(None, ("section", "mp")),
            P("section", "mp"),
            P("mp", "section"),
        ),
        out_specs=(P(("section", "dp", "mp"), None), P(("section", "dp", "mp"), None)),
        check_vma=False,
    )
```

```python
import functools

import jax
import jax.numpy as jnp
from jax import lax
from jax.experimental import pallas as pl
from jax.experimental.pallas import tpu as pltpu
from jax.sharding import PartitionSpec as P

HEADS = 4
DM = 4096
MICRO = 4
SESS_MAX = 64
EPSILON = 1e-06
F32 = jnp.float32
BF16 = jnp.bfloat16

VMEM = pl.BlockSpec(memory_space=pltpu.VMEM)


def swap(x, axis, size, flip):
    return lax.ppermute(x, axis, [(i, i ^ flip) for i in range(size)])


def silu_half(h):
    return h + h * jnp.tanh(h)


def order_of(dps):
    return [0, *range(2, dps), 1]


def in_order(ref, at, dps):
    if dps == 1:
        return ref[at, :]
    z = lax.axis_index("dp")
    cols = ref.shape[1] // dps
    return jnp.concatenate([ref[at, pl.ds(pl.multiple_of((z ^ k) * cols, cols), cols)] for k in order_of(dps)], axis=1)


def project(dps, row0, hist, ev_ref, w_ref, gate_ref, q_ref, kv_ref):
    rows, width = ev_ref.shape
    step = min(rows, 256)
    for r in range(0, rows, step):
        at = slice(r, r + step)
        x = in_order(ev_ref, at, dps)
        row_pos = lax.broadcasted_iota(jnp.int32, (step, 1), 0).astype(F32) + (row0 + r)

        def act(n):
            part = jnp.dot(x, w_ref[:, n * width : (n + 1) * width], preferred_element_type=F32)
            return silu_half(part * 0.5)

        gate_ref[at, :] = act(0).astype(gate_ref.dtype)
        kv_ref[at, :width] = jnp.where(row_pos < hist, act(1), 0.0).astype(BF16)
        q_ref[at, :] = act(2).astype(BF16)
        kv_ref[at, width:] = act(3).astype(BF16)


def attend(q_ref, kv_refs, gate_ref, gain_ref, att_ref):
    rows, width = q_ref.shape
    head = width // HEADS
    step = min(rows, 256)
    blocks = [(ref, r) for ref in kv_refs for r in range(0, ref.shape[0], step)]
    tri = lax.broadcasted_iota(jnp.int32, (step, step), 1) <= lax.broadcasted_iota(
        jnp.int32, (step, step), 0
    )
    before = len(blocks) - rows // step
    for i in range(rows // step):
        at = slice(i * step, (i + 1) * step)
        for h in range(HEADS):
            q = q_ref[at, h * head : (h + 1) * head]
            total = None
            for j in range(before + i + 1):
                ref, r = blocks[j]
                k = ref[r : r + step, width + h * head : width + (h + 1) * head]
                v = ref[r : r + step, h * head : (h + 1) * head]
                s = lax.dot_general(q, k, (((1,), (1,)), ((), ())), preferred_element_type=F32)
                wts = silu_half(s * (0.5 * head**-0.5))
                if j == before + i:
                    wts = jnp.where(tri, wts, 0.0)
                mixed = jnp.dot(wts.astype(BF16), v, preferred_element_type=F32)
                total = mixed if total is None else total + mixed
            att_ref[at, h * head : (h + 1) * head] = total
    att = att_ref[...]
    inv = lax.rsqrt(jnp.mean(att * att, axis=1, keepdims=True) + EPSILON)
    return (att * inv * gain_ref[:1] * gate_ref[...].astype(F32)).astype(BF16)


def membership(bounds_ref, row0, rows):
    starts, ends = bounds_ref[0, :, :1], bounds_ref[1, :, :1]
    pos = (lax.broadcasted_iota(jnp.int32, (starts.shape[0], rows), 1) + row0).astype(F32)
    return jnp.where((pos >= starts) & (pos < ends), 1.0, 0.0).astype(BF16)


def pool(dps, bounds_ref, sums_ev, sums_ref, wout_ref):
    n_valid = jnp.maximum(bounds_ref[1, :, :1] - bounds_ref[0, :, :1], 1.0)
    sess = sums_ev.shape[0]
    sums_g = in_order(sums_ref, slice(None), dps)
    hi = sums_g.astype(BF16)
    rest = sums_g - hi.astype(F32)
    mid = rest.astype(BF16)
    low = (rest - mid.astype(F32)).astype(BF16)
    terms = jnp.dot(jnp.concatenate([low, mid, hi], axis=0), wout_ref[...], preferred_element_type=F32)
    return (terms[:sess] + terms[sess : 2 * sess] + terms[2 * sess :] + sums_ev) / n_valid


def first_kernel(place, dps, copies_out, n_parts, bounds_ref, ev_ref, gain_ref, *refs):
    parts, refs = refs[:n_parts], refs[n_parts:]
    pooled_ref, w_ref, wout_ref, kv_ref, sums_ev_ref, sums_g_ref, q_ref, gate_ref, att_ref = refs
    place(parts, w_ref, wout_ref)
    member = membership(bounds_ref, 0, ev_ref.shape[0])
    sums_ev = jnp.dot(member, ev_ref[...], preferred_element_type=F32)
    sums_ev_ref[...] = sums_ev
    project(dps, 0, bounds_ref[2, :1, :1], ev_ref, w_ref, gate_ref, q_ref, kv_ref)
    gated = attend(q_ref, [kv_ref], gate_ref, gain_ref, att_ref)
    sums_g_ref[...] = jnp.dot(member, gated, preferred_element_type=F32)
    out = pool(dps, bounds_ref, sums_ev, sums_g_ref, wout_ref)
    peers, take = copies_out
    pooled_ref[...] = jnp.concatenate([out[:take]] * peers, axis=0).astype(BF16)


def halves(ref):
    cols = ref.shape[1] // 2
    return ref.at[:, :cols], ref.at[:, cols:]


def project_kernel(dps, row0, bounds_ref, ev_ref, w_ref, sums_ev_ref, _, qg_ref, kv_ref, out_ref):
    q_ref, gate_ref = halves(qg_ref)
    project(dps, row0, bounds_ref[2, :1, :1], ev_ref, w_ref, gate_ref, q_ref, kv_ref)
    member = membership(bounds_ref, row0, ev_ref.shape[0])
    out_ref[...] = sums_ev_ref[...] + jnp.dot(member, ev_ref[...], preferred_element_type=F32)


def attend_kernel(row0, at, rows, bounds_ref, gain_ref, qg_ref, kv_first, kv_ref, sums_ref, _, out_ref, att_ref):
    here = pl.ds(at, rows)
    q_ref, gate_ref = halves(qg_ref)
    member = membership(bounds_ref, row0 + at, rows)
    kv_refs = [kv_first, kv_ref.at[: at + rows]]
    gated = attend(q_ref.at[here], kv_refs, gate_ref.at[here], gain_ref, att_ref)
    out_ref[...] = sums_ref[...] + jnp.dot(member, gated, preferred_element_type=F32)


def call(kernel, name, operands, out_shape, scratch, mib, flops, size, transcendentals=0):
    return pl.pallas_call(
        kernel,
        in_specs=[VMEM] * len(operands),
        out_specs=[VMEM] * len(out_shape),
        out_shape=[jax.ShapeDtypeStruct(shape, kind) for shape, kind in out_shape],
        scratch_shapes=scratch,
        compiler_params=pltpu.CompilerParams(vmem_limit_bytes=mib * 1024 * 1024),
        cost_estimate=pl.CostEstimate(flops=flops, bytes_accessed=size, transcendentals=transcendentals),
        name=name,
    )(*operands)


def parity(m):
    return (m & 1) ^ ((m >> 1) & 1)


def split_kernel(*refs):
    *parts, left_ref, right_ref = refs
    half = left_ref.shape[2]
    for k, part in enumerate(parts):
        left_ref[k] = part[:, :half]
        right_ref[k] = part[:, half:]


def gather_weights(w_uvqk, w_out, w_in, ffn_gain, sections, dps, mps):
    depth, wide = w_uvqk.shape
    width = w_out.shape[1]
    w_in = jnp.concatenate([w_in, jnp.broadcast_to(ffn_gain, (16, w_in.shape[1]))], axis=0)
    if (sections, mps) != (2, 4) or wide != 4 * width or depth % 128:
        ws = [lax.all_gather(x, "dp", axis=0, tiled=True) for x in (w_uvqk, w_out)]
        blocks = [[w_in]] + [[swap(w_in, "mp", mps, k)] for k in range(1, mps)]

        def place_whole(parts, w_ref, wout_ref):
            w_ref[...] = parts[0][...]
            wout_ref[...] = parts[1][...]

        return place_whole, ws, blocks, 1

    part = depth // 4
    cut = width // 2
    sec, m = lax.axis_index("section"), lax.axis_index("mp")
    share = sec * 2 + parity(m)
    mine = jnp.concatenate(
        [
            lax.dynamic_slice_in_dim(w_uvqk, share * width, width, 1),
            lax.dynamic_slice_in_dim(w_out, share * part, part, 0),
        ],
        axis=0,
    )
    got = [swap(mine, "dp", dps, k) for k in order_of(dps)[1:]]
    left, right = call(
        split_kernel,
        "split",
        got,
        [((len(got), depth + part, cut), BF16)] * 2,
        [],
        8,
        0,
        16 * 1024 * 1024,
    )
    plane = [left, right, swap(left, "mp", mps, 1), swap(right, "mp", mps, 2)]
    parts = [w_uvqk[:, : wide // 2], w_uvqk[:, wide // 2 :], w_out[: depth // 2], w_out[depth // 2 :]]
    parts = parts + plane + [swap(p, "section", sections, 1) for p in plane]

    from_x, from_y = swap(w_in, "mp", mps, 1), swap(w_in, "mp", mps, 2)
    middle = w_in.shape[0] // 32 * 16
    diagonal = [swap(from_x[:middle], "mp", mps, 2), swap(from_y[middle:], "mp", mps, 1)]

    def place(parts, w_ref, wout_ref):
        sec, m = lax.axis_index("section"), lax.axis_index("mp")
        for i in range(2):
            w_ref[:depth, i * (wide // 2) : (i + 1) * (wide // 2)] = parts[i][...]
            wout_ref[i * (depth // 2) : (i + 1) * (depth // 2)] = parts[2 + i][...]
        for i, ref in enumerate(parts[4:]):
            owner = (sec ^ (i // 4)) * 2 + (parity(m) ^ (i // 2 % 2))
            at = i % 2 * cut
            cols = pl.ds(pl.multiple_of(owner * width + at, cut), cut)
            for k in range(dps - 1):
                row = (k + 1) * depth
                w_ref[row : row + depth, cols] = ref[k, :depth]
                rows = pl.ds(pl.multiple_of(row + owner * part, part), part)
                wout_ref[rows, at : at + cut] = ref[k, depth:]

    return place, parts, [[w_in], [from_x], [from_y], diagonal], dps


def two_terms(square):
    hi = square.astype(BF16).astype(F32)
    lane = lax.broadcasted_iota(jnp.int32, (square.shape[0], 128), 1)
    return jnp.where(lane == 0, hi, jnp.where(lane == 1, square - hi, 0.0)).astype(BF16)


def up_kernel(chunks, pieces, x_ref, *refs):
    w_in_refs, refs = refs[: sum(pieces)], refs[sum(pieces) :]
    w_ref, local_ref, half_ref, send_ref, normed_ref = refs
    m = lax.axis_index("mp")
    depth = x_ref.shape[1]
    x = x_ref[...]
    square = None
    at = 0
    for k, n in enumerate(pieces):
        block = jnp.concatenate([r[...] for r in w_in_refs[at : at + n]], axis=0)
        at += n
        hidden = jnp.dot(x, block[:depth], preferred_element_type=F32)
        part = jnp.sum(hidden * hidden, axis=1, keepdims=True)
        square = part if square is None else square + part
        gain = block[depth:].astype(F32)[:1]
        cols = hidden.shape[1]
        normed_ref[:, pl.ds(pl.multiple_of((m ^ k) * cols, cols), cols)] = (hidden * gain).astype(BF16)
        if k == 0:
            local_ref[...] = hidden
    normed = normed_ref[...]
    wide = w_ref.shape[1]
    each = wide // chunks
    for c in range(chunks):
        at = slice(c * each, (c + 1) * each)
        half = jnp.dot(normed, w_ref[:, at], preferred_element_type=F32)
        half_ref[:, at] = half
        send_ref[:, at] = half.astype(BF16)
    half_ref[:, wide:] = jnp.broadcast_to(square, (x.shape[0], 128))
    send_ref[:, wide:] = two_terms(square)


def down_kernel(chunks, sections, mps, take, half_ref, other_ref, local_ref, w_ref, _, own_ref, *refs):
    *send_refs, part_ref = refs
    units, wide = w_ref.shape
    each = wide // chunks
    square = half_ref[:, units : units + 1] + jnp.sum(other_ref[:, units:].astype(F32), axis=1, keepdims=True)
    inv = lax.rsqrt(square / DM + EPSILON)
    up = (half_ref[:, :units] + other_ref[:, :units].astype(F32)) * inv
    hidden = jax.nn.gelu(up, approximate=True).astype(BF16)
    for c in range(chunks):
        at = slice(c * each, (c + 1) * each)
        part_ref[:, at] = jnp.dot(hidden, w_ref[:, at], preferred_element_type=F32)
    m = lax.axis_index("mp")
    cols = local_ref.shape[1]
    own = pl.ds(pl.multiple_of(m * cols, cols), cols)
    part_ref[:, own] = part_ref[:, own] + local_ref[...]
    for k, ref in enumerate([own_ref, *send_refs]):
        starts = [pl.multiple_of((s * mps + (m ^ k)) * take, take) for s in range(sections)]
        mine = [part_ref[pl.ds(start, take), :] for start in starts]
        ref[...] = jnp.concatenate(mine, axis=0).astype(ref.dtype)


def add_kernel(own_ref, *refs):
    *got_refs, _, keep_ref, send_ref, total_ref = refs
    total = own_ref[...]
    for ref in got_refs:
        total = total + ref[...].astype(F32)
    total_ref[...] = total
    sec = lax.axis_index("section")
    take = keep_ref.shape[0]
    keep_ref[...] = total_ref[pl.ds(pl.multiple_of(sec * take, take), take), :]
    send_ref[...] = total_ref[pl.ds(pl.multiple_of((1 - sec) * take, take), take), :]


def finish_kernel(dps, keep_ref, got_ref, bounds_ref, sums_ev_ref, sums_g_ref, wout_ref, out_ref, pooled_ref):
    pooled_ref[...] = pool(dps, bounds_ref, sums_ev_ref[...], sums_g_ref, wout_ref).astype(BF16)
    sec = lax.axis_index("section")
    wide = keep_ref.shape[1]
    out_ref[:, pl.ds(pl.multiple_of(sec * wide, wide), wide)] = keep_ref[...].astype(BF16)
    out_ref[:, pl.ds(pl.multiple_of((1 - sec) * wide, wide), wide)] = got_ref[...].astype(BF16)


def per_device(sections, dps, mps, events, hist_len, sess_len, w_uvqk, w_out, attn_gain, w_in, ffn_gain, w_up, w_down):
    events = events[0]
    length, width = events.shape
    sess = sess_len.shape[1]
    take = sess // MICRO
    peers = sections * mps
    rows = take * peers
    cols = w_in.shape[1]
    units = w_up.shape[1]
    half_width = w_down.shape[1]
    group = ("section", "mp")
    first = take * SESS_MAX
    rest = length - first

    gain = jnp.broadcast_to(attn_gain, (8, width))
    ends = jnp.sum(jnp.where(jnp.tri(sess, dtype=jnp.bool_), sess_len, 0), axis=1)
    bounds = jnp.stack([ends - sess_len[0], jnp.minimum(ends, hist_len), jnp.broadcast_to(hist_len, ends.shape)])
    bounds = jnp.broadcast_to(bounds.astype(F32)[:, :, None], (3, sess, 128))
    place, parts, w_in_blocks, dps = gather_weights(w_uvqk, w_out, w_in, ffn_gain, sections, dps, mps)

    micro_rows, full_w, full_wout, kv_first, sums_ev, sums_g = call(
        functools.partial(first_kernel, place, dps, (peers, take), len(parts)),
        "encode_first",
        [bounds, events[:first], gain, *parts],
        [
            ((rows, width), BF16),
            ((width, 4 * width), BF16),
            ((width, width), BF16),
            ((first, 2 * width), BF16),
            ((sess, width), F32),
            ((sess, width), F32),
        ],
        [
            pltpu.VMEM((first, width), BF16),
            pltpu.VMEM((first, width), F32),
            pltpu.VMEM((first, width), F32),
        ],
        16,
        8 * first * width * width + 2 * first * first * width,
        6 * 1024 * 1024,
        4 * first * width + HEADS * first * first,
    )
    arrived = lax.all_to_all(
        micro_rows.reshape(peers, take, width), group, split_axis=0, concat_axis=0, tiled=True
    ).reshape(rows, width)
    blocks = [piece for block in w_in_blocks for piece in block]
    local, half, half_send = call(
        functools.partial(up_kernel, 4, [len(block) for block in w_in_blocks]),
        "up_half",
        [arrived, *blocks, w_up],
        [((rows, cols), F32), ((rows, units + 128), F32), ((rows, units + 128), BF16)],
        [pltpu.VMEM((rows, w_up.shape[0]), BF16)],
        10,
        2 * rows * w_up.size,
        2 * w_up.size,
    )
    other = swap(half_send, "section", sections, 1)
    queries_gate, kv_rest, sums_ev = call(
        functools.partial(project_kernel, dps, first),
        "project_rest",
        [bounds, events[first:], full_w, sums_ev, local],
        [((rest, 2 * width), BF16), ((rest, 2 * width), BF16), ((sess, width), F32)],
        [],
        10,
        8 * rest * width * width,
        6 * 1024 * 1024,
        4 * rest * width,
    )
    pair = sections * take
    own, *sends = call(
        functools.partial(down_kernel, 4, sections, mps, take),
        "down_part",
        [half, other, local, w_down, sums_ev],
        [((pair, half_width), F32)] + [((pair, half_width), BF16)] * (mps - 1),
        [pltpu.VMEM((rows, half_width), F32)],
        8,
        2 * rows * w_down.size,
        2 * w_down.size,
        rows * units,
    )

    def attend_part(at, count, sums, after):
        return call(
            functools.partial(attend_kernel, first, at, count),
            f"attend_{at}",
            [bounds, gain, queries_gate, kv_first, kv_rest, sums, after],
            [((sess, width), F32)],
            [pltpu.VMEM((count, width), F32)],
            10,
            4 * count * (first + at + count) * width,
            4 * 1024 * 1024,
            HEADS * count * (first + at + count),
        )[0]

    got = [swap(x, "mp", mps, k + 1) for k, x in enumerate(sends)]
    sums_g = attend_part(0, rest // 2, sums_g, own)
    keep, send = call(
        add_kernel,
        "add_parts",
        [own, *got, sums_g],
        [((take, half_width), F32)] * 2,
        [pltpu.VMEM((pair, half_width), F32)],
        8,
        mps * pair * half_width,
        2 * mps * pair * half_width,
    )
    got = swap(send, "section", sections, 1)
    sums_g = attend_part(rest // 2, rest - rest // 2, sums_g, keep)
    cross_out, pooled = call(
        functools.partial(finish_kernel, dps),
        "finish",
        [keep, got, bounds, sums_ev, sums_g, full_wout],
        [((take, half_width * sections), BF16), ((sess, width), BF16)],
        [],
        8,
        6 * sess * width * width,
        2 * 1024 * 1024,
    )
    return (pooled, cross_out)


def solution(mesh):
    sizes = [mesh.shape[name] for name in ("section", "dp", "mp")]
    return jax.shard_map(
        functools.partial(per_device, *sizes),
        mesh=mesh,
        in_specs=(
            P(("section", "dp", "mp"), None, None),
            P(("section", "dp", "mp")),
            P(("section", "dp", "mp"), None),
            P("dp", None),
            P("dp", None),
            P(),
            P(None, ("section", "mp")),
            P(None, ("section", "mp")),
            P("section", "mp"),
            P("mp", "section"),
        ),
        out_specs=(P(("section", "dp", "mp"), None), P(("section", "dp", "mp"), None)),
        check_vma=False,
    )
```

```python
import functools

import jax
import jax.numpy as jnp
from jax import lax
from jax.experimental import pallas as pl
from jax.experimental.pallas import tpu as pltpu
from jax.sharding import PartitionSpec as P

HEADS = 4
DM = 4096
MICRO = 4
SESS_MAX = 64
EPSILON = 1e-06
F32 = jnp.float32
BF16 = jnp.bfloat16

VMEM = pl.BlockSpec(memory_space=pltpu.VMEM)


def swap(x, axis, size, flip):
    return lax.ppermute(x, axis, [(i, i ^ flip) for i in range(size)])


def silu_half(h):
    return h + h * jnp.tanh(h)


def order_of(dps):
    return [0, *range(2, dps), 1]


def in_order(ref, at, dps):
    if dps == 1:
        return ref[at, :]
    z = lax.axis_index("dp")
    cols = ref.shape[1] // dps
    return jnp.concatenate([ref[at, pl.ds(pl.multiple_of((z ^ k) * cols, cols), cols)] for k in order_of(dps)], axis=1)


def project(dps, row0, hist, ev_ref, w_ref, gate_ref, q_ref, kv_ref):
    rows, width = ev_ref.shape
    step = min(rows, 256)
    for r in range(0, rows, step):
        at = slice(r, r + step)
        x = in_order(ev_ref, at, dps)
        row_pos = lax.broadcasted_iota(jnp.int32, (step, 1), 0).astype(F32) + (row0 + r)

        def act(n):
            part = jnp.dot(x, w_ref[:, n * width : (n + 1) * width], preferred_element_type=F32)
            return silu_half(part * 0.5)

        gate_ref[at, :] = act(0).astype(gate_ref.dtype)
        kv_ref[at, :width] = jnp.where(row_pos < hist, act(1), 0.0).astype(BF16)
        q_ref[at, :] = act(2).astype(BF16)
        kv_ref[at, width:] = act(3).astype(BF16)


def attend(q_ref, kv_refs, gate_ref, gain_ref, att_ref):
    rows, width = q_ref.shape
    head = width // HEADS
    step = min(rows, 256)
    blocks = [(ref, r) for ref in kv_refs for r in range(0, ref.shape[0], step)]
    tri = lax.broadcasted_iota(jnp.int32, (step, step), 1) <= lax.broadcasted_iota(
        jnp.int32, (step, step), 0
    )
    before = len(blocks) - rows // step
    for i in range(rows // step):
        at = slice(i * step, (i + 1) * step)
        for h in range(HEADS):
            q = q_ref[at, h * head : (h + 1) * head]
            total = None
            for j in range(before + i + 1):
                ref, r = blocks[j]
                k = ref[r : r + step, width + h * head : width + (h + 1) * head]
                v = ref[r : r + step, h * head : (h + 1) * head]
                s = lax.dot_general(q, k, (((1,), (1,)), ((), ())), preferred_element_type=F32)
                wts = silu_half(s * (0.5 * head**-0.5))
                if j == before + i:
                    wts = jnp.where(tri, wts, 0.0)
                mixed = jnp.dot(wts.astype(BF16), v, preferred_element_type=F32)
                total = mixed if total is None else total + mixed
            att_ref[at, h * head : (h + 1) * head] = total
    att = att_ref[...]
    inv = lax.rsqrt(jnp.mean(att * att, axis=1, keepdims=True) + EPSILON)
    return (att * inv * gain_ref[:1] * gate_ref[...].astype(F32)).astype(BF16)


def membership(bounds_ref, row0, rows):
    starts, ends = bounds_ref[0, :, :1], bounds_ref[1, :, :1]
    pos = (lax.broadcasted_iota(jnp.int32, (starts.shape[0], rows), 1) + row0).astype(F32)
    return jnp.where((pos >= starts) & (pos < ends), 1.0, 0.0).astype(BF16)


def pool(dps, bounds_ref, sums_ev, sums_ref, wout_ref):
    n_valid = jnp.maximum(bounds_ref[1, :, :1] - bounds_ref[0, :, :1], 1.0)
    sess = sums_ev.shape[0]
    sums_g = in_order(sums_ref, slice(None), dps)
    hi = sums_g.astype(BF16)
    rest = sums_g - hi.astype(F32)
    mid = rest.astype(BF16)
    low = (rest - mid.astype(F32)).astype(BF16)
    terms = jnp.dot(jnp.concatenate([low, mid, hi], axis=0), wout_ref[...], preferred_element_type=F32)
    return (terms[:sess] + terms[sess : 2 * sess] + terms[2 * sess :] + sums_ev) / n_valid


def first_kernel(place, dps, copies_out, n_parts, bounds_ref, ev_ref, gain_ref, *refs):
    parts, refs = refs[:n_parts], refs[n_parts:]
    pooled_ref, w_ref, wout_ref, kv_ref, sums_ev_ref, sums_g_ref, q_ref, gate_ref, att_ref = refs
    place(parts, w_ref, wout_ref)
    member = membership(bounds_ref, 0, ev_ref.shape[0])
    sums_ev = jnp.dot(member, ev_ref[...], preferred_element_type=F32)
    sums_ev_ref[...] = sums_ev
    project(dps, 0, bounds_ref[2, :1, :1], ev_ref, w_ref, gate_ref, q_ref, kv_ref)
    gated = attend(q_ref, [kv_ref], gate_ref, gain_ref, att_ref)
    sums_g_ref[...] = jnp.dot(member, gated, preferred_element_type=F32)
    out = pool(dps, bounds_ref, sums_ev, sums_g_ref, wout_ref)
    peers, take = copies_out
    pooled_ref[...] = jnp.concatenate([out[:take]] * peers, axis=0).astype(BF16)


def halves(ref):
    cols = ref.shape[1] // 2
    return ref.at[:, :cols], ref.at[:, cols:]


def project_kernel(dps, row0, bounds_ref, ev_ref, w_ref, sums_ev_ref, _, qg_ref, kv_ref, out_ref):
    q_ref, gate_ref = halves(qg_ref)
    project(dps, row0, bounds_ref[2, :1, :1], ev_ref, w_ref, gate_ref, q_ref, kv_ref)
    member = membership(bounds_ref, row0, ev_ref.shape[0])
    out_ref[...] = sums_ev_ref[...] + jnp.dot(member, ev_ref[...], preferred_element_type=F32)


def attend_kernel(row0, at, rows, bounds_ref, gain_ref, qg_ref, kv_first, kv_ref, sums_ref, _, out_ref, att_ref):
    here = pl.ds(at, rows)
    q_ref, gate_ref = halves(qg_ref)
    member = membership(bounds_ref, row0 + at, rows)
    kv_refs = [kv_first, kv_ref.at[: at + rows]]
    gated = attend(q_ref.at[here], kv_refs, gate_ref.at[here], gain_ref, att_ref)
    out_ref[...] = sums_ref[...] + jnp.dot(member, gated, preferred_element_type=F32)


def call(kernel, name, operands, out_shape, scratch, mib, flops, size, transcendentals=0):
    return pl.pallas_call(
        kernel,
        in_specs=[VMEM] * len(operands),
        out_specs=[VMEM] * len(out_shape),
        out_shape=[jax.ShapeDtypeStruct(shape, kind) for shape, kind in out_shape],
        scratch_shapes=scratch,
        compiler_params=pltpu.CompilerParams(vmem_limit_bytes=mib * 1024 * 1024),
        cost_estimate=pl.CostEstimate(flops=flops, bytes_accessed=size, transcendentals=transcendentals),
        name=name,
    )(*operands)


def stack_kernel(*refs):
    *parts, out_ref = refs
    for k, part in enumerate(parts):
        out_ref[k] = part[...]


def gather_weights(w_uvqk, w_out, w_in, ffn_gain, sections, dps, mps):
    depth, wide = w_uvqk.shape
    width = w_out.shape[1]
    w_in = jnp.concatenate([w_in, jnp.broadcast_to(ffn_gain, (16, w_in.shape[1]))], axis=0)
    peers = sections * mps
    cut, part = wide // peers, depth // peers
    if (sections, mps) != (2, 4) or width != 2 * cut or depth % 128:
        ws = [lax.all_gather(x, "dp", axis=0, tiled=True) for x in (w_uvqk, w_out)]
        blocks = [[w_in]] + [[swap(w_in, "mp", mps, k)] for k in range(1, mps)]

        def place_whole(parts, w_ref, wout_ref):
            w_ref[...] = parts[0][...]
            wout_ref[...] = parts[1][...]

        return place_whole, ws, blocks, 1

    sec, m = lax.axis_index("section"), lax.axis_index("mp")
    share = sec * mps + m
    rows = lax.dynamic_slice_in_dim(w_out, share * part, part, 0)
    mine = jnp.concatenate(
        [lax.dynamic_slice_in_dim(w_uvqk, share * cut, cut, 1), rows[:, :cut], rows[:, cut:]], axis=0
    )
    got = [swap(mine, "dp", dps, k) for k in order_of(dps)[1:]]
    (stacked,) = call(
        stack_kernel, "stack", got, [((len(got), *mine.shape), BF16)], [], 8, 0, 16 * 1024 * 1024
    )
    plane = [stacked] + [swap(stacked, "mp", mps, k) for k in range(1, mps)]
    parts = [w_uvqk[:, : wide // 2], w_uvqk[:, wide // 2 :], w_out[: depth // 2], w_out[depth // 2 :]]
    parts = parts + plane + [swap(p, "section", sections, 1) for p in plane]

    from_x, from_y = swap(w_in, "mp", mps, 1), swap(w_in, "mp", mps, 2)
    middle = w_in.shape[0] // 32 * 16
    diagonal = [swap(from_x[:middle], "mp", mps, 2), swap(from_y[middle:], "mp", mps, 1)]

    def place(parts, w_ref, wout_ref):
        sec, m = lax.axis_index("section"), lax.axis_index("mp")
        for i in range(2):
            w_ref[:depth, i * (wide // 2) : (i + 1) * (wide // 2)] = parts[i][...]
            wout_ref[i * (depth // 2) : (i + 1) * (depth // 2)] = parts[2 + i][...]
        for i, ref in enumerate(parts[4:]):
            owner = (sec ^ (i // mps)) * mps + (m ^ (i % mps))
            cols = pl.ds(pl.multiple_of(owner * cut, cut), cut)
            for k in range(dps - 1):
                row = (k + 1) * depth
                w_ref[row : row + depth, cols] = ref[k, :depth]
                rows = pl.ds(pl.multiple_of(row + owner * part, part), part)
                wout_ref[rows, :cut] = ref[k, depth : depth + part]
                wout_ref[rows, cut:] = ref[k, depth + part :]

    return place, parts, [[w_in], [from_x], [from_y], diagonal], dps


def two_terms(square):
    hi = square.astype(BF16).astype(F32)
    lane = lax.broadcasted_iota(jnp.int32, (square.shape[0], 128), 1)
    return jnp.where(lane == 0, hi, jnp.where(lane == 1, square - hi, 0.0)).astype(BF16)


def up_kernel(chunks, pieces, x_ref, *refs):
    w_in_refs, refs = refs[: sum(pieces)], refs[sum(pieces) :]
    w_ref, local_ref, half_ref, send_ref, normed_ref = refs
    m = lax.axis_index("mp")
    depth = x_ref.shape[1]
    x = x_ref[...]
    square = None
    at = 0
    for k, n in enumerate(pieces):
        block = jnp.concatenate([r[...] for r in w_in_refs[at : at + n]], axis=0)
        at += n
        hidden = jnp.dot(x, block[:depth], preferred_element_type=F32)
        part = jnp.sum(hidden * hidden, axis=1, keepdims=True)
        square = part if square is None else square + part
        gain = block[depth:].astype(F32)[:1]
        cols = hidden.shape[1]
        normed_ref[:, pl.ds(pl.multiple_of((m ^ k) * cols, cols), cols)] = (hidden * gain).astype(BF16)
        if k == 0:
            local_ref[...] = hidden
    normed = normed_ref[...]
    wide = w_ref.shape[1]
    each = wide // chunks
    for c in range(chunks):
        at = slice(c * each, (c + 1) * each)
        half = jnp.dot(normed, w_ref[:, at], preferred_element_type=F32)
        half_ref[:, at] = half
        send_ref[:, at] = half.astype(BF16)
    half_ref[:, wide:] = jnp.broadcast_to(square, (x.shape[0], 128))
    send_ref[:, wide:] = two_terms(square)


def down_kernel(chunks, sections, mps, take, half_ref, other_ref, local_ref, w_ref, _, own_ref, *refs):
    *send_refs, part_ref = refs
    units, wide = w_ref.shape
    each = wide // chunks
    square = half_ref[:, units : units + 1] + jnp.sum(other_ref[:, units:].astype(F32), axis=1, keepdims=True)
    inv = lax.rsqrt(square / DM + EPSILON)
    up = (half_ref[:, :units] + other_ref[:, :units].astype(F32)) * inv
    hidden = jax.nn.gelu(up, approximate=True).astype(BF16)
    for c in range(chunks):
        at = slice(c * each, (c + 1) * each)
        part_ref[:, at] = jnp.dot(hidden, w_ref[:, at], preferred_element_type=F32)
    m = lax.axis_index("mp")
    cols = local_ref.shape[1]
    own = pl.ds(pl.multiple_of(m * cols, cols), cols)
    part_ref[:, own] = part_ref[:, own] + local_ref[...]
    for k, ref in enumerate([own_ref, *send_refs]):
        starts = [pl.multiple_of((s * mps + (m ^ k)) * take, take) for s in range(sections)]
        mine = [part_ref[pl.ds(start, take), :] for start in starts]
        ref[...] = jnp.concatenate(mine, axis=0).astype(ref.dtype)


def add_kernel(own_ref, *refs):
    *got_refs, _, keep_ref, send_ref, total_ref = refs
    total = own_ref[...]
    for ref in got_refs:
        total = total + ref[...].astype(F32)
    total_ref[...] = total
    sec = lax.axis_index("section")
    take = keep_ref.shape[0]
    keep_ref[...] = total_ref[pl.ds(pl.multiple_of(sec * take, take), take), :]
    send_ref[...] = total_ref[pl.ds(pl.multiple_of((1 - sec) * take, take), take), :]


def finish_kernel(dps, keep_ref, got_ref, bounds_ref, sums_ev_ref, sums_g_ref, wout_ref, out_ref, pooled_ref):
    pooled_ref[...] = pool(dps, bounds_ref, sums_ev_ref[...], sums_g_ref, wout_ref).astype(BF16)
    sec = lax.axis_index("section")
    wide = keep_ref.shape[1]
    out_ref[:, pl.ds(pl.multiple_of(sec * wide, wide), wide)] = keep_ref[...].astype(BF16)
    out_ref[:, pl.ds(pl.multiple_of((1 - sec) * wide, wide), wide)] = got_ref[...].astype(BF16)


def per_device(sections, dps, mps, events, hist_len, sess_len, w_uvqk, w_out, attn_gain, w_in, ffn_gain, w_up, w_down):
    events = events[0]
    length, width = events.shape
    sess = sess_len.shape[1]
    take = sess // MICRO
    peers = sections * mps
    rows = take * peers
    cols = w_in.shape[1]
    units = w_up.shape[1]
    half_width = w_down.shape[1]
    group = ("section", "mp")
    first = take * SESS_MAX
    rest = length - first

    gain = jnp.broadcast_to(attn_gain, (8, width))
    ends = jnp.sum(jnp.where(jnp.tri(sess, dtype=jnp.bool_), sess_len, 0), axis=1)
    bounds = jnp.stack([ends - sess_len[0], jnp.minimum(ends, hist_len), jnp.broadcast_to(hist_len, ends.shape)])
    bounds = jnp.broadcast_to(bounds.astype(F32)[:, :, None], (3, sess, 128))
    place, parts, w_in_blocks, dps = gather_weights(w_uvqk, w_out, w_in, ffn_gain, sections, dps, mps)

    micro_rows, full_w, full_wout, kv_first, sums_ev, sums_g = call(
        functools.partial(first_kernel, place, dps, (peers, take), len(parts)),
        "encode_first",
        [bounds, events[:first], gain, *parts],
        [
            ((rows, width), BF16),
            ((width, 4 * width), BF16),
            ((width, width), BF16),
            ((first, 2 * width), BF16),
            ((sess, width), F32),
            ((sess, width), F32),
        ],
        [
            pltpu.VMEM((first, width), BF16),
            pltpu.VMEM((first, width), F32),
            pltpu.VMEM((first, width), F32),
        ],
        16,
        8 * first * width * width + 2 * first * first * width,
        6 * 1024 * 1024,
        4 * first * width + HEADS * first * first,
    )
    arrived = lax.all_to_all(
        micro_rows.reshape(peers, take, width), group, split_axis=0, concat_axis=0, tiled=True
    ).reshape(rows, width)
    blocks = [piece for block in w_in_blocks for piece in block]
    local, half, half_send = call(
        functools.partial(up_kernel, 4, [len(block) for block in w_in_blocks]),
        "up_half",
        [arrived, *blocks, w_up],
        [((rows, cols), F32), ((rows, units + 128), F32), ((rows, units + 128), BF16)],
        [pltpu.VMEM((rows, w_up.shape[0]), BF16)],
        10,
        2 * rows * w_up.size,
        2 * w_up.size,
    )
    other = swap(half_send, "section", sections, 1)
    queries_gate, kv_rest, sums_ev = call(
        functools.partial(project_kernel, dps, first),
        "project_rest",
        [bounds, events[first:], full_w, sums_ev, local],
        [((rest, 2 * width), BF16), ((rest, 2 * width), BF16), ((sess, width), F32)],
        [],
        10,
        8 * rest * width * width,
        6 * 1024 * 1024,
        4 * rest * width,
    )
    pair = sections * take
    own, *sends = call(
        functools.partial(down_kernel, 4, sections, mps, take),
        "down_part",
        [half, other, local, w_down, sums_ev],
        [((pair, half_width), F32)] + [((pair, half_width), BF16)] * (mps - 1),
        [pltpu.VMEM((rows, half_width), F32)],
        8,
        2 * rows * w_down.size,
        2 * w_down.size,
        rows * units,
    )

    def attend_part(at, count, sums, after):
        return call(
            functools.partial(attend_kernel, first, at, count),
            f"attend_{at}",
            [bounds, gain, queries_gate, kv_first, kv_rest, sums, after],
            [((sess, width), F32)],
            [pltpu.VMEM((count, width), F32)],
            10,
            4 * count * (first + at + count) * width,
            4 * 1024 * 1024,
            HEADS * count * (first + at + count),
        )[0]

    got = [swap(x, "mp", mps, k + 1) for k, x in enumerate(sends)]
    sums_g = attend_part(0, rest // 2, sums_g, own)
    keep, send = call(
        add_kernel,
        "add_parts",
        [own, *got, sums_g],
        [((take, half_width), F32)] * 2,
        [pltpu.VMEM((pair, half_width), F32)],
        8,
        mps * pair * half_width,
        2 * mps * pair * half_width,
    )
    got = swap(send, "section", sections, 1)
    sums_g = attend_part(rest // 2, rest - rest // 2, sums_g, keep)
    cross_out, pooled = call(
        functools.partial(finish_kernel, dps),
        "finish",
        [keep, got, bounds, sums_ev, sums_g, full_wout],
        [((take, half_width * sections), BF16), ((sess, width), BF16)],
        [],
        8,
        6 * sess * width * width,
        2 * 1024 * 1024,
    )
    return (pooled, cross_out)


def solution(mesh):
    sizes = [mesh.shape[name] for name in ("section", "dp", "mp")]
    return jax.shard_map(
        functools.partial(per_device, *sizes),
        mesh=mesh,
        in_specs=(
            P(("section", "dp", "mp"), None, None),
            P(("section", "dp", "mp")),
            P(("section", "dp", "mp"), None),
            P("dp", None),
            P("dp", None),
            P(),
            P(None, ("section", "mp")),
            P(None, ("section", "mp")),
            P("section", "mp"),
            P("mp", "section"),
        ),
        out_specs=(P(("section", "dp", "mp"), None), P(("section", "dp", "mp"), None)),
        check_vma=False,
    )
```

```python
import functools

import jax
import jax.numpy as jnp
from jax import lax
from jax.experimental import pallas as pl
from jax.experimental.pallas import tpu as pltpu
from jax.sharding import PartitionSpec as P

HEADS = 4
DM = 4096
MICRO = 4
SESS_MAX = 64
EPSILON = 1e-06
F32 = jnp.float32
BF16 = jnp.bfloat16

VMEM = pl.BlockSpec(memory_space=pltpu.VMEM)


def swap(x, axis, size, flip):
    return lax.ppermute(x, axis, [(i, i ^ flip) for i in range(size)])


def silu_half(h):
    return h + h * jnp.tanh(h)


def order_of(dps):
    return [0, *range(2, dps), 1]


def in_order(ref, at, dps):
    if dps == 1:
        return ref[at, :]
    z = lax.axis_index("dp")
    cols = ref.shape[1] // dps
    return jnp.concatenate([ref[at, pl.ds(pl.multiple_of((z ^ k) * cols, cols), cols)] for k in order_of(dps)], axis=1)


def project(dps, row0, hist, ev_ref, w_ref, gate_ref, q_ref, kv_ref):
    rows, width = ev_ref.shape
    step = min(rows, 256)
    for r in range(0, rows, step):
        at = slice(r, r + step)
        x = in_order(ev_ref, at, dps)
        row_pos = lax.broadcasted_iota(jnp.int32, (step, 1), 0).astype(F32) + (row0 + r)

        def act(n):
            part = jnp.dot(x, w_ref[:, n * width : (n + 1) * width], preferred_element_type=F32)
            return silu_half(part * 0.5)

        gate_ref[at, :] = act(0).astype(gate_ref.dtype)
        kv_ref[at, :width] = jnp.where(row_pos < hist, act(1), 0.0).astype(BF16)
        q_ref[at, :] = act(2).astype(BF16)
        kv_ref[at, width:] = act(3).astype(BF16)


STEP = 256


def attend(q_ref, kv_refs, att_ref, pairs):
    rows, width = q_ref.shape
    head = width // HEADS
    step = min(rows, STEP)
    blocks = [(ref, r) for ref in kv_refs for r in range(0, ref.shape[0], step)]
    tri = lax.broadcasted_iota(jnp.int32, (step, step), 1) <= lax.broadcasted_iota(
        jnp.int32, (step, step), 0
    )
    before = len(blocks) - rows // step
    for i, h in pairs:
        at = slice(i * step, (i + 1) * step)
        q = q_ref[at, h * head : (h + 1) * head]
        total = None
        for j in range(before + i + 1):
            ref, r = blocks[j]
            k = ref[r : r + step, width + h * head : width + (h + 1) * head]
            v = ref[r : r + step, h * head : (h + 1) * head]
            s = lax.dot_general(q, k, (((1,), (1,)), ((), ())), preferred_element_type=F32)
            wts = silu_half(s * (0.5 * head**-0.5))
            if j == before + i:
                wts = jnp.where(tri, wts, 0.0)
            mixed = jnp.dot(wts.astype(BF16), v, preferred_element_type=F32)
            total = mixed if total is None else total + mixed
        att_ref[at, h * head : (h + 1) * head] = total


def all_pairs(rows):
    return [(i, h) for i in range(max(rows // STEP, 1)) for h in range(HEADS)]


def gated_rows(att, gain_ref, gate):
    inv = lax.rsqrt(jnp.mean(att * att, axis=1, keepdims=True) + EPSILON)
    return (att * inv * gain_ref[:1] * gate.astype(F32)).astype(BF16)


def membership(bounds_ref, row0, rows):
    starts, ends = bounds_ref[0, :, :1], bounds_ref[1, :, :1]
    pos = (lax.broadcasted_iota(jnp.int32, (starts.shape[0], rows), 1) + row0).astype(F32)
    return jnp.where((pos >= starts) & (pos < ends), 1.0, 0.0).astype(BF16)


def pool(dps, bounds_ref, sums_ev, sums_ref, wout_ref):
    n_valid = jnp.maximum(bounds_ref[1, :, :1] - bounds_ref[0, :, :1], 1.0)
    sess = sums_ev.shape[0]
    sums_g = in_order(sums_ref, slice(None), dps)
    hi = sums_g.astype(BF16)
    rest = sums_g - hi.astype(F32)
    mid = rest.astype(BF16)
    low = (rest - mid.astype(F32)).astype(BF16)
    terms = jnp.dot(jnp.concatenate([low, mid, hi], axis=0), wout_ref[...], preferred_element_type=F32)
    return (terms[:sess] + terms[sess : 2 * sess] + terms[2 * sess :] + sums_ev) / n_valid


def first_kernel(place, dps, n_parts, bounds_ref, ev_ref, gain_ref, *refs):
    parts, refs = refs[:n_parts], refs[n_parts:]
    pooled_ref, w_ref, wout_ref, kv_ref, sums_ev_ref, sums_g_ref, q_ref, gate_ref, att_ref = refs
    place(parts, w_ref, wout_ref)
    member = membership(bounds_ref, 0, ev_ref.shape[0])
    sums_ev = jnp.dot(member, ev_ref[...], preferred_element_type=F32)
    sums_ev_ref[...] = sums_ev
    project(dps, 0, bounds_ref[2, :1, :1], ev_ref, w_ref, gate_ref, q_ref, kv_ref)
    attend(q_ref, [kv_ref], att_ref, all_pairs(q_ref.shape[0]))
    gated = gated_rows(att_ref[...], gain_ref, gate_ref[...])
    sums_g_ref[...] = jnp.dot(member, gated, preferred_element_type=F32)
    out = pool(dps, bounds_ref, sums_ev, sums_g_ref, wout_ref)
    pooled_ref[...] = out[: pooled_ref.shape[0]]


def halves(ref):
    cols = ref.shape[1] // 2
    return ref.at[:, :cols], ref.at[:, cols:]


def project_kernel(dps, row0, bounds_ref, ev_ref, w_ref, sums_ev_ref, _, qg_ref, kv_ref, out_ref):
    q_ref, gate_ref = halves(qg_ref)
    project(dps, row0, bounds_ref[2, :1, :1], ev_ref, w_ref, gate_ref, q_ref, kv_ref)
    member = membership(bounds_ref, row0, ev_ref.shape[0])
    out_ref[...] = sums_ev_ref[...] + jnp.dot(member, ev_ref[...], preferred_element_type=F32)


def attend_kernel(pairs, qg_ref, kv_first, kv_ref, _, att_ref):
    attend(halves(qg_ref)[0], [kv_first, kv_ref], att_ref, pairs)


def attend_rest_kernel(row0, done, bounds_ref, gain_ref, qg_ref, kv_first, kv_ref, sums_ref, *refs):
    *before_refs, _, out_ref, att_ref = refs
    q_ref, gate_ref = halves(qg_ref)
    rows, width = q_ref.shape
    here = [pair for pair in all_pairs(rows) if not any(pair in pairs for pairs in done)]
    attend(q_ref, [kv_first, kv_ref], att_ref, here)
    head = width // HEADS
    step = min(rows, STEP)
    total = sums_ref[...]
    for i in range(rows // step):
        at = slice(i * step, (i + 1) * step)
        att = []
        for h in range(HEADS):
            ref = next((ref for ref, pairs in zip(before_refs, done) if (i, h) in pairs), att_ref)
            att.append(ref[at, h * head : (h + 1) * head])
        gated = gated_rows(jnp.concatenate(att, axis=1), gain_ref, gate_ref[at])
        member = membership(bounds_ref, row0 + i * step, step)
        total = total + jnp.dot(member, gated, preferred_element_type=F32)
    out_ref[...] = total


def call(kernel, name, operands, out_shape, scratch, mib, flops, size, transcendentals=0):
    return pl.pallas_call(
        kernel,
        in_specs=[VMEM] * len(operands),
        out_specs=[VMEM] * len(out_shape),
        out_shape=[jax.ShapeDtypeStruct(shape, kind) for shape, kind in out_shape],
        scratch_shapes=scratch,
        compiler_params=pltpu.CompilerParams(vmem_limit_bytes=mib * 1024 * 1024),
        cost_estimate=pl.CostEstimate(flops=flops, bytes_accessed=size, transcendentals=transcendentals),
        name=name,
    )(*operands)


def parity(m):
    return (m & 1) ^ ((m >> 1) & 1)


def split_kernel(*refs):
    *parts, left_ref, right_ref = refs
    half = left_ref.shape[2]
    for k, part in enumerate(parts):
        left_ref[k] = part[:, :half]
        right_ref[k] = part[:, half:]


def gather_weights(w_uvqk, w_out, w_in, ffn_gain, sections, dps, mps):
    depth, wide = w_uvqk.shape
    width = w_out.shape[1]
    w_in = jnp.concatenate([w_in, jnp.broadcast_to(ffn_gain, (16, w_in.shape[1]))], axis=0)
    if (sections, mps) != (2, 4) or wide != 4 * width or depth % 128:
        ws = [lax.all_gather(x, "dp", axis=0, tiled=True) for x in (w_uvqk, w_out)]
        blocks = [[w_in]] + [[swap(w_in, "mp", mps, k)] for k in range(1, mps)]

        def place_whole(parts, w_ref, wout_ref):
            w_ref[...] = parts[0][...]
            wout_ref[...] = parts[1][...]

        return place_whole, ws, blocks, 1

    part = depth // 4
    cut = width // 2
    sec, m = lax.axis_index("section"), lax.axis_index("mp")
    share = sec * 2 + parity(m)
    mine = jnp.concatenate(
        [
            lax.dynamic_slice_in_dim(w_uvqk, share * width, width, 1),
            lax.dynamic_slice_in_dim(w_out, share * part, part, 0),
        ],
        axis=0,
    )
    got = [swap(mine, "dp", dps, k) for k in order_of(dps)[1:]]
    left, right = call(
        split_kernel,
        "split",
        got,
        [((len(got), depth + part, cut), BF16)] * 2,
        [],
        8,
        0,
        16 * 1024 * 1024,
    )
    plane = [left, right, swap(left, "mp", mps, 1), swap(right, "mp", mps, 2)]
    parts = [w_uvqk[:, : wide // 2], w_uvqk[:, wide // 2 :], w_out[: depth // 2], w_out[depth // 2 :]]
    parts = parts + plane + [swap(p, "section", sections, 1) for p in plane]

    from_x, from_y = swap(w_in, "mp", mps, 1), swap(w_in, "mp", mps, 2)
    middle = w_in.shape[0] // 32 * 16
    diagonal = [swap(from_x[:middle], "mp", mps, 2), swap(from_y[middle:], "mp", mps, 1)]
    blocks = [[w_in], [from_x], [from_y], diagonal]

    def place(parts, w_ref, wout_ref):
        sec, m = lax.axis_index("section"), lax.axis_index("mp")
        for i in range(2):
            w_ref[:depth, i * (wide // 2) : (i + 1) * (wide // 2)] = parts[i][...]
            wout_ref[i * (depth // 2) : (i + 1) * (depth // 2)] = parts[2 + i][...]
        for i, ref in enumerate(parts[4:]):
            owner = (sec ^ (i // 4)) * 2 + (parity(m) ^ (i // 2 % 2))
            at = i % 2 * cut
            cols = pl.ds(pl.multiple_of(owner * width + at, cut), cut)
            for k in range(dps - 1):
                row = (k + 1) * depth
                w_ref[row : row + depth, cols] = ref[k, :depth]
                rows = pl.ds(pl.multiple_of(row + owner * part, part), part)
                wout_ref[rows, at : at + cut] = ref[k, depth:]

    return place, parts, blocks, dps


def two_terms(square):
    hi = square.astype(BF16).astype(F32)
    lane = lax.broadcasted_iota(jnp.int32, (square.shape[0], 128), 1)
    return jnp.where(lane == 0, hi, jnp.where(lane == 1, square - hi, 0.0)).astype(BF16)


def up_kernel(chunks, pieces, *refs):
    x_refs, refs = refs[: len(pieces)], refs[len(pieces) :]
    w_in_refs, refs = refs[: sum(pieces)], refs[sum(pieces) :]
    w_ref, local_ref, half_ref, send_ref, normed_ref = refs
    m = lax.axis_index("mp")
    x = jnp.concatenate([ref[...] for ref in x_refs], axis=0)
    depth = x.shape[1]
    square = None
    at = 0
    for k, n in enumerate(pieces):
        block = jnp.concatenate([r[...] for r in w_in_refs[at : at + n]], axis=0)
        at += n
        hidden = jnp.dot(x, block[:depth], preferred_element_type=F32)
        part = jnp.sum(hidden * hidden, axis=1, keepdims=True)
        square = part if square is None else square + part
        gain = block[depth:].astype(F32)[:1]
        cols = hidden.shape[1]
        normed_ref[:, pl.ds(pl.multiple_of((m ^ k) * cols, cols), cols)] = (hidden * gain).astype(BF16)
        if k == 0:
            local_ref[...] = hidden
    normed = normed_ref[...]
    wide = w_ref.shape[1]
    each = wide // chunks
    for c in range(chunks):
        at = slice(c * each, (c + 1) * each)
        half = jnp.dot(normed, w_ref[:, at], preferred_element_type=F32)
        half_ref[:, at] = half
        send_ref[:, at] = half.astype(BF16)
    half_ref[:, wide:] = jnp.broadcast_to(square, (x.shape[0], 128))
    send_ref[:, wide:] = two_terms(square)


def down_kernel(chunks, half_ref, other_ref, local_ref, w_ref, _, own_ref, *refs):
    *send_refs, part_ref = refs
    units, wide = w_ref.shape
    each = wide // chunks
    square = half_ref[:, units : units + 1] + jnp.sum(other_ref[:, units:].astype(F32), axis=1, keepdims=True)
    inv = lax.rsqrt(square / DM + EPSILON)
    up = (half_ref[:, :units] + other_ref[:, :units].astype(F32)) * inv
    hidden = jax.nn.gelu(up, approximate=True).astype(BF16)
    for c in range(chunks):
        at = slice(c * each, (c + 1) * each)
        part_ref[:, at] = jnp.dot(hidden, w_ref[:, at], preferred_element_type=F32)
    m = lax.axis_index("mp")
    cols = local_ref.shape[1]
    own = pl.ds(pl.multiple_of(m * cols, cols), cols)
    part_ref[:, own] = part_ref[:, own] + local_ref[...]
    for k, ref in enumerate([own_ref, *send_refs]):
        count = ref.shape[0]
        ref[...] = part_ref[k * count : (k + 1) * count, :].astype(ref.dtype)


def pair_kernel(own_ref, got_ref, _, out_ref, pair_ref):
    sec = lax.axis_index("section")
    take = own_ref.shape[0]
    pair_ref[pl.ds(pl.multiple_of(sec * take, take), take), :] = own_ref[...]
    pair_ref[pl.ds(pl.multiple_of((1 - sec) * take, take), take), :] = got_ref[...]
    out_ref[...] = pair_ref[...].astype(BF16)


def add_kernel(own_ref, *refs):
    *got_refs, _, keep_ref, send_ref, total_ref = refs
    total = own_ref[...]
    for ref in got_refs:
        total = total + ref[...].astype(F32)
    total_ref[...] = total
    sec = lax.axis_index("section")
    take = keep_ref.shape[0]
    keep_ref[...] = total_ref[pl.ds(pl.multiple_of(sec * take, take), take), :]
    send_ref[...] = total_ref[pl.ds(pl.multiple_of((1 - sec) * take, take), take), :]


def finish_kernel(dps, keep_ref, got_ref, bounds_ref, sums_ev_ref, sums_g_ref, wout_ref, out_ref, pooled_ref):
    pooled_ref[...] = pool(dps, bounds_ref, sums_ev_ref[...], sums_g_ref, wout_ref).astype(BF16)
    sec = lax.axis_index("section")
    wide = keep_ref.shape[1]
    out_ref[:, pl.ds(pl.multiple_of(sec * wide, wide), wide)] = keep_ref[...].astype(BF16)
    out_ref[:, pl.ds(pl.multiple_of((1 - sec) * wide, wide), wide)] = got_ref[...].astype(BF16)


def per_device(sections, dps, mps, events, hist_len, sess_len, w_uvqk, w_out, attn_gain, w_in, ffn_gain, w_up, w_down):
    events = events[0]
    length, width = events.shape
    sess = sess_len.shape[1]
    take = sess // MICRO
    peers = sections * mps
    rows = take * peers
    cols = w_in.shape[1]
    units = w_up.shape[1]
    half_width = w_down.shape[1]
    first = take * SESS_MAX
    rest = length - first

    gain = jnp.broadcast_to(attn_gain, (8, width))
    ends = jnp.sum(jnp.where(jnp.tri(sess, dtype=jnp.bool_), sess_len, 0), axis=1)
    bounds = jnp.stack([ends - sess_len[0], jnp.minimum(ends, hist_len), jnp.broadcast_to(hist_len, ends.shape)])
    bounds = jnp.broadcast_to(bounds.astype(F32)[:, :, None], (3, sess, 128))
    place, parts, w_in_blocks, dps = gather_weights(w_uvqk, w_out, w_in, ffn_gain, sections, dps, mps)

    micro_rows, full_w, full_wout, kv_first, sums_ev, sums_g = call(
        functools.partial(first_kernel, place, dps, len(parts)),
        "encode_first",
        [bounds, events[:first], gain, *parts],
        [
            ((take, width), F32),
            ((width, 4 * width), BF16),
            ((width, width), BF16),
            ((first, 2 * width), BF16),
            ((sess, width), F32),
            ((sess, width), F32),
        ],
        [
            pltpu.VMEM((first, width), BF16),
            pltpu.VMEM((first, width), F32),
            pltpu.VMEM((first, width), F32),
        ],
        16,
        8 * first * width * width + 2 * first * first * width,
        6 * 1024 * 1024,
        4 * first * width + HEADS * first * first,
    )
    got = swap(micro_rows, "section", sections, 1)
    queries_gate, kv_rest, sums_ev = call(
        functools.partial(project_kernel, dps, first),
        "project_rest",
        [bounds, events[first:], full_w, sums_ev, micro_rows],
        [((rest, 2 * width), BF16), ((rest, 2 * width), BF16), ((sess, width), F32)],
        [],
        10,
        8 * rest * width * width,
        6 * 1024 * 1024,
        4 * rest * width,
    )
    pair = sections * take
    (pair_rows,) = call(
        pair_kernel,
        "pair_rows",
        [micro_rows, got, sums_ev],
        [((pair, width), BF16)],
        [pltpu.VMEM((pair, width), F32)],
        8,
        0,
        4 * pair * width,
    )
    x = [pair_rows] + [swap(pair_rows, "mp", mps, k) for k in range(1, mps)]
    blocks = [piece for block in w_in_blocks for piece in block]
    local, half, half_send = call(
        functools.partial(up_kernel, 4, [len(block) for block in w_in_blocks]),
        "up_half",
        [*x, *blocks, w_up],
        [((rows, cols), F32), ((rows, units + 128), F32), ((rows, units + 128), BF16)],
        [pltpu.VMEM((rows, w_up.shape[0]), BF16)],
        10,
        2 * rows * w_up.size,
        2 * w_up.size,
    )

    pairs = all_pairs(rest)
    done = [pairs[: HEADS // 2], pairs[HEADS // 2 : -1]]

    def attend_part(which, after):
        share = len(done[which])
        return call(
            functools.partial(attend_kernel, done[which]),
            f"attend_{which}",
            [queries_gate, kv_first, kv_rest, after],
            [((rest, width), F32)],
            [],
            10,
            4 * rest * length * width * share // len(pairs),
            4 * 1024 * 1024,
            HEADS * rest * length * share // len(pairs),
        )[0]

    other = swap(half_send, "section", sections, 1)
    att = [attend_part(0, local)]
    own, *sends = call(
        functools.partial(down_kernel, 4),
        "down_part",
        [half, other, local, w_down, att[0]],
        [((pair, half_width), F32)] + [((pair, half_width), BF16)] * (mps - 1),
        [pltpu.VMEM((rows, half_width), F32)],
        8,
        2 * rows * w_down.size,
        2 * w_down.size,
        rows * units,
    )
    got = [swap(x, "mp", mps, k + 1) for k, x in enumerate(sends)]
    att.append(attend_part(1, own))
    keep, send = call(
        add_kernel,
        "add_parts",
        [own, *got, att[1]],
        [((take, half_width), F32)] * 2,
        [pltpu.VMEM((pair, half_width), F32)],
        8,
        mps * pair * half_width,
        2 * mps * pair * half_width,
    )
    got = swap(send, "section", sections, 1)
    (sums_g,) = call(
        functools.partial(attend_rest_kernel, first, done),
        "attend_last",
        [bounds, gain, queries_gate, kv_first, kv_rest, sums_g, *att, keep],
        [((sess, width), F32)],
        [pltpu.VMEM((rest, width), F32)],
        10,
        rest * length * width // 2,
        4 * 1024 * 1024,
        HEADS * rest * length // len(pairs),
    )
    cross_out, pooled = call(
        functools.partial(finish_kernel, dps),
        "finish",
        [keep, got, bounds, sums_ev, sums_g, full_wout],
        [((take, half_width * sections), BF16), ((sess, width), BF16)],
        [],
        8,
        6 * sess * width * width,
        2 * 1024 * 1024,
    )
    return (pooled, cross_out)


def solution(mesh):
    sizes = [mesh.shape[name] for name in ("section", "dp", "mp")]
    return jax.shard_map(
        functools.partial(per_device, *sizes),
        mesh=mesh,
        in_specs=(
            P(("section", "dp", "mp"), None, None),
            P(("section", "dp", "mp")),
            P(("section", "dp", "mp"), None),
            P("dp", None),
            P("dp", None),
            P(),
            P(None, ("section", "mp")),
            P(None, ("section", "mp")),
            P("section", "mp"),
            P("mp", "section"),
        ),
        out_specs=(P(("section", "dp", "mp"), None), P(("section", "dp", "mp"), None)),
        check_vma=False,
    )
```

```python
import functools

import jax
import jax.numpy as jnp
from jax import lax
from jax.experimental import pallas as pl
from jax.experimental.pallas import tpu as pltpu
from jax.sharding import PartitionSpec as P

HEADS = 4
DM = 4096
MICRO = 4
SESS_MAX = 64
EPSILON = 1e-06
F32 = jnp.float32
BF16 = jnp.bfloat16

VMEM = pl.BlockSpec(memory_space=pltpu.VMEM)


def swap(x, axis, size, flip):
    return lax.ppermute(x, axis, [(i, i ^ flip) for i in range(size)])


def silu_half(h):
    return h + h * jnp.tanh(h)


def order_of(dps):
    return [0, *range(2, dps), 1]


def in_order(ref, at, dps):
    if dps == 1:
        return ref[at, :]
    z = lax.axis_index("dp")
    cols = ref.shape[1] // dps
    return jnp.concatenate([ref[at, pl.ds(pl.multiple_of((z ^ k) * cols, cols), cols)] for k in order_of(dps)], axis=1)


def project(dps, row0, hist, ev_ref, w_ref, gate_ref, q_ref, kv_ref):
    rows, width = ev_ref.shape
    step = min(rows, 256)
    for r in range(0, rows, step):
        at = slice(r, r + step)
        x = in_order(ev_ref, at, dps)
        row_pos = lax.broadcasted_iota(jnp.int32, (step, 1), 0).astype(F32) + (row0 + r)

        def act(n):
            part = jnp.dot(x, w_ref[:, n * width : (n + 1) * width], preferred_element_type=F32)
            return silu_half(part * 0.5)

        gate_ref[at, :] = act(0).astype(gate_ref.dtype)
        kv_ref[at, :width] = jnp.where(row_pos < hist, act(1), 0.0).astype(BF16)
        q_ref[at, :] = act(2).astype(BF16)
        kv_ref[at, width:] = act(3).astype(BF16)


STEP = 256


def attend(q_ref, kv_refs, att_ref, pairs):
    rows, width = q_ref.shape
    head = width // HEADS
    step = min(rows, STEP)
    blocks = [(ref, r) for ref in kv_refs for r in range(0, ref.shape[0], step)]
    tri = lax.broadcasted_iota(jnp.int32, (step, step), 1) <= lax.broadcasted_iota(
        jnp.int32, (step, step), 0
    )
    before = len(blocks) - rows // step
    for i, h in pairs:
        at = slice(i * step, (i + 1) * step)
        q = q_ref[at, h * head : (h + 1) * head]
        total = None
        for j in range(before + i + 1):
            ref, r = blocks[j]
            k = ref[r : r + step, width + h * head : width + (h + 1) * head]
            v = ref[r : r + step, h * head : (h + 1) * head]
            s = lax.dot_general(q, k, (((1,), (1,)), ((), ())), preferred_element_type=F32)
            wts = silu_half(s * (0.5 * head**-0.5))
            if j == before + i:
                wts = jnp.where(tri, wts, 0.0)
            mixed = jnp.dot(wts.astype(BF16), v, preferred_element_type=F32)
            total = mixed if total is None else total + mixed
        att_ref[at, h * head : (h + 1) * head] = total


def all_pairs(rows):
    return [(i, h) for i in range(max(rows // STEP, 1)) for h in range(HEADS)]


def gated_rows(att, gain_ref, gate):
    inv = lax.rsqrt(jnp.mean(att * att, axis=1, keepdims=True) + EPSILON)
    return (att * inv * gain_ref[:1] * gate.astype(F32)).astype(BF16)


def membership(bounds_ref, row0, rows):
    starts, ends = bounds_ref[0, :, :1], bounds_ref[1, :, :1]
    pos = (lax.broadcasted_iota(jnp.int32, (starts.shape[0], rows), 1) + row0).astype(F32)
    return jnp.where((pos >= starts) & (pos < ends), 1.0, 0.0).astype(BF16)


def pool(dps, bounds_ref, sums_ev, sums_ref, wout_ref):
    n_valid = jnp.maximum(bounds_ref[1, :, :1] - bounds_ref[0, :, :1], 1.0)
    sess = sums_ev.shape[0]
    sums_g = in_order(sums_ref, slice(None), dps)
    hi = sums_g.astype(BF16)
    rest = sums_g - hi.astype(F32)
    mid = rest.astype(BF16)
    low = (rest - mid.astype(F32)).astype(BF16)
    terms = jnp.dot(jnp.concatenate([low, mid, hi], axis=0), wout_ref[...], preferred_element_type=F32)
    return (terms[:sess] + terms[sess : 2 * sess] + terms[2 * sess :] + sums_ev) / n_valid


def first_kernel(place, dps, copies_out, n_parts, bounds_ref, ev_ref, gain_ref, *refs):
    parts, refs = refs[:n_parts], refs[n_parts:]
    pooled_ref, w_ref, wout_ref, kv_ref, sums_ev_ref, sums_g_ref, q_ref, gate_ref, att_ref = refs
    place(parts, w_ref, wout_ref)
    member = membership(bounds_ref, 0, ev_ref.shape[0])
    sums_ev = jnp.dot(member, ev_ref[...], preferred_element_type=F32)
    sums_ev_ref[...] = sums_ev
    project(dps, 0, bounds_ref[2, :1, :1], ev_ref, w_ref, gate_ref, q_ref, kv_ref)
    attend(q_ref, [kv_ref], att_ref, all_pairs(q_ref.shape[0]))
    gated = gated_rows(att_ref[...], gain_ref, gate_ref[...])
    sums_g_ref[...] = jnp.dot(member, gated, preferred_element_type=F32)
    out = pool(dps, bounds_ref, sums_ev, sums_g_ref, wout_ref)
    peers, take = copies_out
    pooled_ref[...] = jnp.concatenate([out[:take]] * peers, axis=0).astype(BF16)


def halves(ref):
    cols = ref.shape[1] // 2
    return ref.at[:, :cols], ref.at[:, cols:]


def project_kernel(dps, row0, bounds_ref, ev_ref, w_ref, sums_ev_ref, _, qg_ref, kv_ref, out_ref):
    q_ref, gate_ref = halves(qg_ref)
    project(dps, row0, bounds_ref[2, :1, :1], ev_ref, w_ref, gate_ref, q_ref, kv_ref)
    member = membership(bounds_ref, row0, ev_ref.shape[0])
    out_ref[...] = sums_ev_ref[...] + jnp.dot(member, ev_ref[...], preferred_element_type=F32)


def attend_kernel(pairs, qg_ref, kv_first, kv_ref, _, att_ref):
    attend(halves(qg_ref)[0], [kv_first, kv_ref], att_ref, pairs)


def attend_rest_kernel(
    row0, pairs, dps, bounds_ref, gain_ref, qg_ref, kv_first, kv_ref, sums_ref, sums_ev_ref, wout_ref, before_ref, _, out_ref,
    att_ref, total_ref,
):
    q_ref, gate_ref = halves(qg_ref)
    rows, width = q_ref.shape
    attend(q_ref, [kv_first, kv_ref], att_ref, pairs)
    head = width // HEADS
    step = min(rows, STEP)
    total = sums_ref[...]
    for i in range(rows // step):
        at = slice(i * step, (i + 1) * step)
        att = [
            (att_ref if (i, h) in pairs else before_ref)[at, h * head : (h + 1) * head] for h in range(HEADS)
        ]
        gated = gated_rows(jnp.concatenate(att, axis=1), gain_ref, gate_ref[at])
        member = membership(bounds_ref, row0 + i * step, step)
        total = total + jnp.dot(member, gated, preferred_element_type=F32)
    total_ref[...] = total
    out_ref[...] = pool(dps, bounds_ref, sums_ev_ref[...], total_ref, wout_ref).astype(BF16)


def call(kernel, name, operands, out_shape, scratch, mib, flops, size, transcendentals=0):
    return pl.pallas_call(
        kernel,
        in_specs=[VMEM] * len(operands),
        out_specs=[VMEM] * len(out_shape),
        out_shape=[jax.ShapeDtypeStruct(shape, kind) for shape, kind in out_shape],
        scratch_shapes=scratch,
        compiler_params=pltpu.CompilerParams(vmem_limit_bytes=mib * 1024 * 1024),
        cost_estimate=pl.CostEstimate(flops=flops, bytes_accessed=size, transcendentals=transcendentals),
        name=name,
    )(*operands)


def parity(m):
    return (m & 1) ^ ((m >> 1) & 1)


def split_kernel(*refs):
    *parts, left_ref, right_ref = refs
    half = left_ref.shape[2]
    for k, part in enumerate(parts):
        left_ref[k] = part[:, :half]
        right_ref[k] = part[:, half:]


def gather_weights(w_uvqk, w_out, w_in, ffn_gain, sections, dps, mps):
    depth, wide = w_uvqk.shape
    width = w_out.shape[1]
    w_in = jnp.concatenate([w_in, ffn_gain, jnp.zeros((15, w_in.shape[1]), BF16)], axis=0)
    if (sections, mps) != (2, 4) or wide != 4 * width or depth % 128:
        ws = [lax.all_gather(x, "dp", axis=0, tiled=True) for x in (w_uvqk, w_out)]
        blocks = [[w_in]] + [[swap(w_in, "mp", mps, k)] for k in range(1, mps)]

        def place_whole(parts, w_ref, wout_ref):
            w_ref[...] = parts[0][...]
            wout_ref[...] = parts[1][...]

        return place_whole, ws, blocks, 1

    part = depth // 4
    cut = width // 2
    sec, m = lax.axis_index("section"), lax.axis_index("mp")
    share = sec * 2 + parity(m)
    mine = jnp.concatenate(
        [
            lax.dynamic_slice_in_dim(w_uvqk, share * width, width, 1),
            lax.dynamic_slice_in_dim(w_out, share * part, part, 0),
        ],
        axis=0,
    )
    got = [swap(mine, "dp", dps, k) for k in order_of(dps)[1:]]
    left, right = call(
        split_kernel,
        "split",
        got,
        [((len(got), depth + part, cut), BF16)] * 2,
        [],
        8,
        0,
        16 * 1024 * 1024,
    )
    plane = [left, right, swap(left, "mp", mps, 1), swap(right, "mp", mps, 2)]
    parts = [w_uvqk[:, : wide // 2], w_uvqk[:, wide // 2 :], w_out[: depth // 2], w_out[depth // 2 :]]
    parts = parts + plane + [swap(p, "section", sections, 1) for p in plane]

    from_x, from_y = swap(w_in, "mp", mps, 1), swap(w_in, "mp", mps, 2)
    middle = w_in.shape[0] // 32 * 16
    diagonal = [swap(from_x[:middle], "mp", mps, 2), swap(from_y[middle:], "mp", mps, 1)]
    blocks = [[w_in], [from_x], [from_y], diagonal]

    def place(parts, w_ref, wout_ref):
        sec, m = lax.axis_index("section"), lax.axis_index("mp")
        for i in range(2):
            w_ref[:depth, i * (wide // 2) : (i + 1) * (wide // 2)] = parts[i][...]
            wout_ref[i * (depth // 2) : (i + 1) * (depth // 2)] = parts[2 + i][...]
        for i, ref in enumerate(parts[4:]):
            owner = (sec ^ (i // 4)) * 2 + (parity(m) ^ (i // 2 % 2))
            at = i % 2 * cut
            cols = pl.ds(pl.multiple_of(owner * width + at, cut), cut)
            for k in range(dps - 1):
                row = (k + 1) * depth
                w_ref[row : row + depth, cols] = ref[k, :depth]
                rows = pl.ds(pl.multiple_of(row + owner * part, part), part)
                wout_ref[rows, at : at + cut] = ref[k, depth:]

    return place, parts, blocks, dps


def two_terms(square):
    hi = square.astype(BF16).astype(F32)
    lane = lax.broadcasted_iota(jnp.int32, (square.shape[0], 128), 1)
    return jnp.where(lane == 0, hi, jnp.where(lane == 1, square - hi, 0.0)).astype(BF16)


def up_kernel(chunks, pieces, x_ref, *refs):
    w_in_refs, refs = refs[: sum(pieces)], refs[sum(pieces) :]
    w_ref, local_ref, half_ref, send_ref, normed_ref = refs
    m = lax.axis_index("mp")
    depth = x_ref.shape[1]
    x = x_ref[...]
    square = None
    at = 0
    for k, n in enumerate(pieces):
        block = jnp.concatenate([r[...] for r in w_in_refs[at : at + n]], axis=0)
        at += n
        hidden = jnp.dot(x, block[:depth], preferred_element_type=F32)
        part = jnp.sum(hidden * hidden, axis=1, keepdims=True)
        square = part if square is None else square + part
        gain = block[depth:].astype(F32)[:1]
        cols = hidden.shape[1]
        normed_ref[:, pl.ds(pl.multiple_of((m ^ k) * cols, cols), cols)] = (hidden * gain).astype(BF16)
        if k == 0:
            local_ref[...] = hidden
    normed = normed_ref[...]
    wide = w_ref.shape[1]
    each = wide // chunks
    for c in range(chunks):
        at = slice(c * each, (c + 1) * each)
        half = jnp.dot(normed, w_ref[:, at], preferred_element_type=F32)
        half_ref[:, at] = half
        send_ref[:, at] = half.astype(BF16)
    half_ref[:, wide:] = jnp.broadcast_to(square, (x.shape[0], 128))
    send_ref[:, wide:] = two_terms(square)


def down_kernel(chunks, sections, mps, take, half_ref, other_ref, local_ref, w_ref, _, own_ref, *refs):
    *send_refs, part_ref = refs
    units, wide = w_ref.shape
    each = wide // chunks
    square = half_ref[:, units : units + 1] + jnp.sum(other_ref[:, units:].astype(F32), axis=1, keepdims=True)
    inv = lax.rsqrt(square / DM + EPSILON)
    up = (half_ref[:, :units] + other_ref[:, :units].astype(F32)) * inv
    hidden = jax.nn.gelu(up, approximate=True).astype(BF16)
    for c in range(chunks):
        at = slice(c * each, (c + 1) * each)
        part_ref[:, at] = jnp.dot(hidden, w_ref[:, at], preferred_element_type=F32)
    m = lax.axis_index("mp")
    cols = local_ref.shape[1]
    own = pl.ds(pl.multiple_of(m * cols, cols), cols)
    part_ref[:, own] = part_ref[:, own] + local_ref[...]
    for k, ref in enumerate([own_ref, *send_refs]):
        starts = [pl.multiple_of((s * mps + (m ^ k)) * take, take) for s in range(sections)]
        mine = [part_ref[pl.ds(start, take), :] for start in starts]
        ref[...] = jnp.concatenate(mine, axis=0).astype(ref.dtype)


def add_kernel(own_ref, *refs):
    *got_refs, _, keep_ref, send_ref, total_ref = refs
    total = own_ref[...]
    for ref in got_refs:
        total = total + ref[...].astype(F32)
    total_ref[...] = total
    sec = lax.axis_index("section")
    take = keep_ref.shape[0]
    keep_ref[...] = total_ref[pl.ds(pl.multiple_of(sec * take, take), take), :]
    send_ref[...] = total_ref[pl.ds(pl.multiple_of((1 - sec) * take, take), take), :]


def finish_kernel(keep_ref, got_ref, out_ref):
    sec = lax.axis_index("section")
    wide = keep_ref.shape[1]
    out_ref[:, pl.ds(pl.multiple_of(sec * wide, wide), wide)] = keep_ref[...].astype(BF16)
    out_ref[:, pl.ds(pl.multiple_of((1 - sec) * wide, wide), wide)] = got_ref[...].astype(BF16)


def per_device(sections, dps, mps, events, hist_len, sess_len, w_uvqk, w_out, attn_gain, w_in, ffn_gain, w_up, w_down):
    events = events[0]
    length, width = events.shape
    sess = sess_len.shape[1]
    take = sess // MICRO
    peers = sections * mps
    rows = take * peers
    cols = w_in.shape[1]
    units = w_up.shape[1]
    half_width = w_down.shape[1]
    group = ("section", "mp")
    first = take * SESS_MAX
    rest = length - first

    gain = jnp.broadcast_to(attn_gain, (8, width))
    ends = jnp.sum(jnp.where(jnp.tri(sess, dtype=jnp.bool_), sess_len, 0), axis=1)
    bounds = jnp.stack([ends - sess_len[0], jnp.minimum(ends, hist_len), jnp.broadcast_to(hist_len, ends.shape)])
    bounds = jnp.broadcast_to(bounds.astype(F32)[:, :, None], (3, sess, 128))
    place, parts, w_in_blocks, dps = gather_weights(w_uvqk, w_out, w_in, ffn_gain, sections, dps, mps)

    micro_rows, full_w, full_wout, kv_first, sums_ev, sums_g = call(
        functools.partial(first_kernel, place, dps, (peers, take), len(parts)),
        "encode_first",
        [bounds, events[:first], gain, *parts],
        [
            ((rows, width), BF16),
            ((width, 4 * width), BF16),
            ((width, width), BF16),
            ((first, 2 * width), BF16),
            ((sess, width), F32),
            ((sess, width), F32),
        ],
        [
            pltpu.VMEM((first, width), BF16),
            pltpu.VMEM((first, width), F32),
            pltpu.VMEM((first, width), F32),
        ],
        16,
        8 * first * width * width + 2 * first * first * width,
        6 * 1024 * 1024,
        4 * first * width + HEADS * first * first,
    )
    arrived = lax.all_to_all(
        micro_rows.reshape(peers, take, width), group, split_axis=0, concat_axis=0, tiled=True
    ).reshape(rows, width)
    blocks = [piece for block in w_in_blocks for piece in block]
    local, half, half_send = call(
        functools.partial(up_kernel, 4, [len(block) for block in w_in_blocks]),
        "up_half",
        [arrived, *blocks, w_up],
        [((rows, cols), F32), ((rows, units + 128), F32), ((rows, units + 128), BF16)],
        [pltpu.VMEM((rows, w_up.shape[0]), BF16)],
        10,
        2 * rows * w_up.size,
        2 * w_up.size,
    )
    other = swap(half_send, "section", sections, 1)
    queries_gate, kv_rest, sums_ev = call(
        functools.partial(project_kernel, dps, first),
        "project_rest",
        [bounds, events[first:], full_w, sums_ev, local],
        [((rest, 2 * width), BF16), ((rest, 2 * width), BF16), ((sess, width), F32)],
        [],
        10,
        8 * rest * width * width,
        6 * 1024 * 1024,
        4 * rest * width,
    )
    pair = sections * take
    own, *sends = call(
        functools.partial(down_kernel, 4, sections, mps, take),
        "down_part",
        [half, other, local, w_down, sums_ev],
        [((pair, half_width), F32)] + [((pair, half_width), BF16)] * (mps - 1),
        [pltpu.VMEM((rows, half_width), F32)],
        8,
        2 * rows * w_down.size,
        2 * w_down.size,
        rows * units,
    )

    got = [swap(x, "mp", mps, k + 1) for k, x in enumerate(sends)]
    pairs = all_pairs(rest)
    late = pairs[-1:]
    pairs = pairs[: -len(late)]
    (att,) = call(
        functools.partial(attend_kernel, pairs),
        "attend_most",
        [queries_gate, kv_first, kv_rest, own],
        [((rest, width), F32)],
        [],
        10,
        3 * rest * length * width,
        4 * 1024 * 1024,
        HEADS * rest * length,
    )
    keep, send = call(
        add_kernel,
        "add_parts",
        [own, *got, att],
        [((take, half_width), F32)] * 2,
        [pltpu.VMEM((pair, half_width), F32)],
        8,
        mps * pair * half_width,
        2 * mps * pair * half_width,
    )
    got = swap(send, "section", sections, 1)
    (pooled,) = call(
        functools.partial(attend_rest_kernel, first, late, dps),
        "attend_last",
        [bounds, gain, queries_gate, kv_first, kv_rest, sums_g, sums_ev, full_wout, att, keep],
        [((sess, width), BF16)],
        [pltpu.VMEM((rest, width), F32), pltpu.VMEM((sess, width), F32)],
        10,
        rest * length * width // 2,
        4 * 1024 * 1024,
        HEADS * rest * length // 8,
    )
    (cross_out,) = call(
        finish_kernel,
        "finish",
        [keep, got],
        [((take, half_width * sections), BF16)],
        [],
        8,
        0,
        16 * take * half_width,
    )
    return (pooled, cross_out)


def solution(mesh):
    sizes = [mesh.shape[name] for name in ("section", "dp", "mp")]
    return jax.shard_map(
        functools.partial(per_device, *sizes),
        mesh=mesh,
        in_specs=(
            P(("section", "dp", "mp"), None, None),
            P(("section", "dp", "mp")),
            P(("section", "dp", "mp"), None),
            P("dp", None),
            P("dp", None),
            P(),
            P(None, ("section", "mp")),
            P(None, ("section", "mp")),
            P("section", "mp"),
            P("mp", "section"),
        ),
        out_specs=(P(("section", "dp", "mp"), None), P(("section", "dp", "mp"), None)),
        check_vma=False,
    )
```

```python
import functools

import jax
import jax.numpy as jnp
from jax import lax
from jax.experimental import pallas as pl
from jax.experimental.pallas import tpu as pltpu
from jax.sharding import PartitionSpec as P

HEADS = 4
DM = 4096
MICRO = 4
SESS_MAX = 64
EPSILON = 1e-06
F32 = jnp.float32
BF16 = jnp.bfloat16

VMEM = pl.BlockSpec(memory_space=pltpu.VMEM)


def swap(x, axis, size, flip):
    return lax.ppermute(x, axis, [(i, i ^ flip) for i in range(size)])


def silu_half(h):
    return h + h * jnp.tanh(h)


def order_of(dps):
    return [0, *range(2, dps), 1]


def in_order(ref, at, dps):
    if dps == 1:
        return ref[at, :]
    z = lax.axis_index("dp")
    cols = ref.shape[1] // dps
    return jnp.concatenate([ref[at, pl.ds(pl.multiple_of((z ^ k) * cols, cols), cols)] for k in order_of(dps)], axis=1)


def project(dps, row0, hist, ev_ref, w_ref, gate_ref, q_ref, kv_ref):
    rows, width = ev_ref.shape
    step = min(rows, 512)
    for r in range(0, rows, step):
        at = slice(r, r + step)
        x = in_order(ev_ref, at, dps)
        row_pos = lax.broadcasted_iota(jnp.int32, (step, 1), 0).astype(F32) + (row0 + r)

        def act(n):
            part = jnp.dot(x, w_ref[:, n * width : (n + 1) * width], preferred_element_type=F32)
            return silu_half(part * 0.5)

        gate_ref[at, :] = act(0).astype(gate_ref.dtype)
        kv_ref[at, :width] = jnp.where(row_pos < hist, act(1), 0.0).astype(BF16)
        q_ref[at, :] = act(2).astype(BF16)
        kv_ref[at, width:] = act(3).astype(BF16)


STEP = 256


def attend(q_ref, kv_refs, att_ref, pairs):
    rows, width = q_ref.shape
    head = width // HEADS
    step = min(rows, STEP)
    tri = lax.broadcasted_iota(jnp.int32, (step, step), 1) <= lax.broadcasted_iota(
        jnp.int32, (step, step), 0
    )
    *earlier, own = kv_refs
    for i, h in pairs:
        at = slice(i * step, (i + 1) * step)
        q = q_ref[at, h * head : (h + 1) * head]
        runs = [(ref, slice(0, ref.shape[0])) for ref in earlier]
        if i:
            runs.append((own, slice(0, i * step)))
        total = None
        for ref, keys in [*runs, (own, at)]:
            k = ref[keys, width + h * head : width + (h + 1) * head]
            v = ref[keys, h * head : (h + 1) * head]
            s = lax.dot_general(q, k, (((1,), (1,)), ((), ())), preferred_element_type=F32)
            wts = silu_half(s * (0.5 * head**-0.5))
            if keys is at:
                wts = jnp.where(tri, wts, 0.0)
            mixed = jnp.dot(wts.astype(BF16), v, preferred_element_type=F32)
            total = mixed if total is None else total + mixed
        att_ref[at, h * head : (h + 1) * head] = total


def all_pairs(rows):
    return [(i, h) for i in range(max(rows // STEP, 1)) for h in range(HEADS)]


def gated_rows(att, gain_ref, gate):
    inv = lax.rsqrt(jnp.mean(att * att, axis=1, keepdims=True) + EPSILON)
    return (att * inv * gain_ref[:1] * gate.astype(F32)).astype(BF16)


def membership(bounds_ref, row0, rows):
    starts, ends = bounds_ref[0, :, :1], bounds_ref[1, :, :1]
    pos = (lax.broadcasted_iota(jnp.int32, (starts.shape[0], rows), 1) + row0).astype(F32)
    return jnp.where((pos >= starts) & (pos < ends), 1.0, 0.0).astype(BF16)


def pool(dps, bounds_ref, sums_ev, sums_ref, wout_ref):
    n_valid = jnp.maximum(bounds_ref[1, :, :1] - bounds_ref[0, :, :1], 1.0)
    sess = sums_ev.shape[0]
    sums_g = in_order(sums_ref, slice(None), dps)
    hi = sums_g.astype(BF16)
    rest = sums_g - hi.astype(F32)
    mid = rest.astype(BF16)
    low = (rest - mid.astype(F32)).astype(BF16)
    terms = jnp.dot(jnp.concatenate([low, mid, hi], axis=0), wout_ref[...], preferred_element_type=F32)
    return (terms[:sess] + terms[sess : 2 * sess] + terms[2 * sess :] + sums_ev) / n_valid


def first_kernel(place, dps, copies_out, n_parts, bounds_ref, ev_ref, gain_ref, *refs):
    parts, refs = refs[:n_parts], refs[n_parts:]
    pooled_ref, w_ref, wout_ref, kv_ref, sums_ev_ref, sums_g_ref, q_ref, gate_ref, att_ref = refs
    place(parts, w_ref, wout_ref)
    member = membership(bounds_ref, 0, ev_ref.shape[0])
    sums_ev = jnp.dot(member, ev_ref[...], preferred_element_type=F32)
    sums_ev_ref[...] = sums_ev
    project(dps, 0, bounds_ref[2, :1, :1], ev_ref, w_ref, gate_ref, q_ref, kv_ref)
    attend(q_ref, [kv_ref], att_ref, all_pairs(q_ref.shape[0]))
    gated = gated_rows(att_ref[...], gain_ref, gate_ref[...])
    sums_g_ref[...] = jnp.dot(member, gated, preferred_element_type=F32)
    out = pool(dps, bounds_ref, sums_ev, sums_g_ref, wout_ref)
    peers, take = copies_out
    pooled_ref[...] = jnp.concatenate([out[:take]] * peers, axis=0).astype(BF16)


def halves(ref):
    cols = ref.shape[1] // 2
    return ref.at[:, :cols], ref.at[:, cols:]


def project_kernel(dps, row0, bounds_ref, ev_ref, w_ref, sums_ev_ref, _, qg_ref, kv_ref, out_ref):
    q_ref, gate_ref = halves(qg_ref)
    project(dps, row0, bounds_ref[2, :1, :1], ev_ref, w_ref, gate_ref, q_ref, kv_ref)
    member = membership(bounds_ref, row0, ev_ref.shape[0])
    out_ref[...] = sums_ev_ref[...] + jnp.dot(member, ev_ref[...], preferred_element_type=F32)


def attend_kernel(pairs, qg_ref, kv_first, kv_ref, _, att_ref):
    attend(halves(qg_ref)[0], [kv_first, kv_ref], att_ref, pairs)


def attend_rest_kernel(
    row0, pairs, dps, bounds_ref, gain_ref, qg_ref, kv_first, kv_ref, sums_ref, sums_ev_ref, wout_ref, before_ref, _, out_ref,
    att_ref, total_ref,
):
    q_ref, gate_ref = halves(qg_ref)
    rows, width = q_ref.shape
    attend(q_ref, [kv_first, kv_ref], att_ref, pairs)
    head = width // HEADS
    step = min(rows, STEP)
    total = sums_ref[...]
    for i in range(rows // step):
        at = slice(i * step, (i + 1) * step)
        att = [
            (att_ref if (i, h) in pairs else before_ref)[at, h * head : (h + 1) * head] for h in range(HEADS)
        ]
        gated = gated_rows(jnp.concatenate(att, axis=1), gain_ref, gate_ref[at])
        member = membership(bounds_ref, row0 + i * step, step)
        total = total + jnp.dot(member, gated, preferred_element_type=F32)
    total_ref[...] = total
    out_ref[...] = pool(dps, bounds_ref, sums_ev_ref[...], total_ref, wout_ref).astype(BF16)


def call(kernel, name, operands, out_shape, scratch, mib, flops, size, transcendentals=0):
    return pl.pallas_call(
        kernel,
        in_specs=[VMEM] * len(operands),
        out_specs=[VMEM] * len(out_shape),
        out_shape=[jax.ShapeDtypeStruct(shape, kind) for shape, kind in out_shape],
        scratch_shapes=scratch,
        compiler_params=pltpu.CompilerParams(vmem_limit_bytes=mib * 1024 * 1024),
        cost_estimate=pl.CostEstimate(flops=flops, bytes_accessed=size, transcendentals=transcendentals),
        name=name,
    )(*operands)


def parity(m):
    return (m & 1) ^ ((m >> 1) & 1)


def split_kernel(*refs):
    *parts, left_ref, right_ref, both_ref = refs
    half = left_ref.shape[2]
    for k, part in enumerate(parts):
        for i, ref in enumerate((left_ref, right_ref)):
            piece = part[:, i * half : (i + 1) * half]
            ref[k] = piece
            both_ref[i, k] = piece


def gather_weights(w_uvqk, w_out, w_in, ffn_gain, sections, dps, mps):
    depth, wide = w_uvqk.shape
    width = w_out.shape[1]
    w_in = jnp.concatenate([w_in, ffn_gain, jnp.zeros((15, w_in.shape[1]), BF16)], axis=0)
    if (sections, mps) != (2, 4) or wide != 4 * width or depth % 128:
        ws = [lax.all_gather(x, "dp", axis=0, tiled=True) for x in (w_uvqk, w_out)]
        blocks = [[w_in]] + [[swap(w_in, "mp", mps, k)] for k in range(1, mps)]

        def place_whole(parts, w_ref, wout_ref):
            w_ref[...] = parts[0][...]
            wout_ref[...] = parts[1][...]

        return place_whole, ws, blocks, 1

    part = depth // 4
    cut = width // 2
    sec, m = lax.axis_index("section"), lax.axis_index("mp")
    share = sec * 2 + parity(m)
    mine = jnp.concatenate(
        [
            lax.dynamic_slice_in_dim(w_uvqk, share * width, width, 1),
            lax.dynamic_slice_in_dim(w_out, share * part, part, 0),
        ],
        axis=0,
    )
    got = [swap(mine, "dp", dps, k) for k in order_of(dps)[1:]]
    size = (len(got), depth + part, cut)
    left, right, both = call(
        split_kernel, "split", got, [(size, BF16), (size, BF16), ((2, *size), BF16)], [], 8, 0, 16 * 1024 * 1024
    )
    others = [swap(left, "mp", mps, 1), swap(right, "mp", mps, 2)]
    parts = [w_uvqk[:, : wide // 2], w_uvqk[:, wide // 2 :], w_out[: depth // 2], w_out[depth // 2 :]]
    parts = parts + [both, *others] + [swap(p, "section", sections, 1) for p in (both, *others)]

    from_x, from_y = swap(w_in, "mp", mps, 1), swap(w_in, "mp", mps, 2)
    middle = w_in.shape[0] // 32 * 16
    diagonal = [swap(from_x[:middle], "mp", mps, 2), swap(from_y[middle:], "mp", mps, 1)]
    blocks = [[w_in], [from_x], [from_y], diagonal]

    def place(parts, w_ref, wout_ref):
        sec, m = lax.axis_index("section"), lax.axis_index("mp")
        for i in range(2):
            w_ref[:depth, i * (wide // 2) : (i + 1) * (wide // 2)] = parts[i][...]
            wout_ref[i * (depth // 2) : (i + 1) * (depth // 2)] = parts[2 + i][...]
        for i, ref in enumerate(parts[4:]):
            other_sec, what = i // 3, i % 3
            owner = (sec ^ other_sec) * 2 + (parity(m) ^ (what > 0))
            for side in (0, 1) if what == 0 else (what - 1,):
                at = side * cut
                cols = pl.ds(pl.multiple_of(owner * width + at, cut), cut)
                for k in range(dps - 1):
                    piece = ref[side, k] if what == 0 else ref[k]
                    row = (k + 1) * depth
                    w_ref[row : row + depth, cols] = piece[:depth]
                    rows = pl.ds(pl.multiple_of(row + owner * part, part), part)
                    wout_ref[rows, at : at + cut] = piece[depth:]

    return place, parts, blocks, dps


def two_terms(square):
    hi = square.astype(BF16).astype(F32)
    lane = lax.broadcasted_iota(jnp.int32, (square.shape[0], 128), 1)
    return jnp.where(lane == 0, hi, jnp.where(lane == 1, square - hi, 0.0)).astype(BF16)


def up_kernel(chunks, pieces, x_ref, *refs):
    w_in_refs, refs = refs[: sum(pieces)], refs[sum(pieces) :]
    w_ref, local_ref, half_ref, send_ref, normed_ref = refs
    m = lax.axis_index("mp")
    depth = x_ref.shape[1]
    x = x_ref[...]
    square = None
    at = 0
    for k, n in enumerate(pieces):
        block = jnp.concatenate([r[...] for r in w_in_refs[at : at + n]], axis=0)
        at += n
        hidden = jnp.dot(x, block[:depth], preferred_element_type=F32)
        part = jnp.sum(hidden * hidden, axis=1, keepdims=True)
        square = part if square is None else square + part
        gain = block[depth:].astype(F32)[:1]
        cols = hidden.shape[1]
        normed_ref[:, pl.ds(pl.multiple_of((m ^ k) * cols, cols), cols)] = (hidden * gain).astype(BF16)
        if k == 0:
            local_ref[...] = hidden
    normed = normed_ref[...]
    wide = w_ref.shape[1]
    each = wide // chunks
    for c in range(chunks):
        at = slice(c * each, (c + 1) * each)
        half = jnp.dot(normed, w_ref[:, at], preferred_element_type=F32)
        half_ref[:, at] = half
        send_ref[:, at] = half.astype(BF16)
    half_ref[:, wide:] = jnp.broadcast_to(square, (x.shape[0], 128))
    send_ref[:, wide:] = two_terms(square)


def down_kernel(chunks, sections, mps, take, half_ref, other_ref, local_ref, w_ref, _, own_ref, *refs):
    *send_refs, part_ref = refs
    units, wide = w_ref.shape
    each = wide // chunks
    square = half_ref[:, units : units + 1] + jnp.sum(other_ref[:, units:].astype(F32), axis=1, keepdims=True)
    inv = lax.rsqrt(square / DM + EPSILON)
    up = (half_ref[:, :units] + other_ref[:, :units].astype(F32)) * inv
    hidden = jax.nn.gelu(up, approximate=True).astype(BF16)
    for c in range(chunks):
        at = slice(c * each, (c + 1) * each)
        part_ref[:, at] = jnp.dot(hidden, w_ref[:, at], preferred_element_type=F32)
    m = lax.axis_index("mp")
    cols = local_ref.shape[1]
    own = pl.ds(pl.multiple_of(m * cols, cols), cols)
    part_ref[:, own] = part_ref[:, own] + local_ref[...]
    for k, ref in enumerate([own_ref, *send_refs]):
        starts = [pl.multiple_of((s * mps + (m ^ k)) * take, take) for s in range(sections)]
        mine = [part_ref[pl.ds(start, take), :] for start in starts]
        ref[...] = jnp.concatenate(mine, axis=0).astype(ref.dtype)


def add_kernel(own_ref, *refs):
    *got_refs, _, keep_ref, send_ref, total_ref = refs
    total = own_ref[...]
    for ref in got_refs:
        total = total + ref[...].astype(F32)
    total_ref[...] = total
    sec = lax.axis_index("section")
    take = keep_ref.shape[0]
    keep_ref[...] = total_ref[pl.ds(pl.multiple_of(sec * take, take), take), :]
    send_ref[...] = total_ref[pl.ds(pl.multiple_of((1 - sec) * take, take), take), :]


def finish_kernel(keep_ref, got_ref, out_ref):
    sec = lax.axis_index("section")
    wide = keep_ref.shape[1]
    out_ref[:, pl.ds(pl.multiple_of(sec * wide, wide), wide)] = keep_ref[...].astype(BF16)
    out_ref[:, pl.ds(pl.multiple_of((1 - sec) * wide, wide), wide)] = got_ref[...].astype(BF16)


def per_device(sections, dps, mps, events, hist_len, sess_len, w_uvqk, w_out, attn_gain, w_in, ffn_gain, w_up, w_down):
    events = events[0]
    length, width = events.shape
    sess = sess_len.shape[1]
    take = sess // MICRO
    peers = sections * mps
    rows = take * peers
    cols = w_in.shape[1]
    units = w_up.shape[1]
    half_width = w_down.shape[1]
    group = ("section", "mp")
    first = take * SESS_MAX
    rest = length - first

    gain = jnp.broadcast_to(attn_gain, (8, width))
    ends = jnp.sum(jnp.where(jnp.tri(sess, dtype=jnp.bool_), sess_len, 0), axis=1)
    bounds = jnp.stack([ends - sess_len[0], jnp.minimum(ends, hist_len), jnp.broadcast_to(hist_len, ends.shape)])
    bounds = jnp.broadcast_to(bounds.astype(F32)[:, :, None], (3, sess, 128))
    place, parts, w_in_blocks, dps = gather_weights(w_uvqk, w_out, w_in, ffn_gain, sections, dps, mps)

    micro_rows, full_w, full_wout, kv_first, sums_ev, sums_g = call(
        functools.partial(first_kernel, place, dps, (peers, take), len(parts)),
        "encode_first",
        [bounds, events[:first], gain, *parts],
        [
            ((rows, width), BF16),
            ((width, 4 * width), BF16),
            ((width, width), BF16),
            ((first, 2 * width), BF16),
            ((sess, width), F32),
            ((sess, width), F32),
        ],
        [
            pltpu.VMEM((first, width), BF16),
            pltpu.VMEM((first, width), F32),
            pltpu.VMEM((first, width), F32),
        ],
        16,
        8 * first * width * width + 2 * first * first * width,
        6 * 1024 * 1024,
        4 * first * width + HEADS * first * first,
    )
    arrived = lax.all_to_all(
        micro_rows.reshape(peers, take, width), group, split_axis=0, concat_axis=0, tiled=True
    ).reshape(rows, width)
    blocks = [piece for block in w_in_blocks for piece in block]
    local, half, half_send = call(
        functools.partial(up_kernel, 4, [len(block) for block in w_in_blocks]),
        "up_half",
        [arrived, *blocks, w_up],
        [((rows, cols), F32), ((rows, units + 128), F32), ((rows, units + 128), BF16)],
        [pltpu.VMEM((rows, w_up.shape[0]), BF16)],
        10,
        2 * rows * w_up.size,
        2 * w_up.size,
    )
    other = swap(half_send, "section", sections, 1)
    queries_gate, kv_rest, sums_ev = call(
        functools.partial(project_kernel, dps, first),
        "project_rest",
        [bounds, events[first:], full_w, sums_ev, local],
        [((rest, 2 * width), BF16), ((rest, 2 * width), BF16), ((sess, width), F32)],
        [],
        10,
        8 * rest * width * width,
        6 * 1024 * 1024,
        4 * rest * width,
    )
    pair = sections * take
    own, *sends = call(
        functools.partial(down_kernel, 4, sections, mps, take),
        "down_part",
        [half, other, local, w_down, sums_ev],
        [((pair, half_width), F32)] + [((pair, half_width), BF16)] * (mps - 1),
        [pltpu.VMEM((rows, half_width), F32)],
        8,
        2 * rows * w_down.size,
        2 * w_down.size,
        rows * units,
    )

    got = [swap(x, "mp", mps, k + 1) for k, x in enumerate(sends)]
    pairs = all_pairs(rest)
    late = pairs[-1:]
    pairs = pairs[: -len(late)]
    (att,) = call(
        functools.partial(attend_kernel, pairs),
        "attend_most",
        [queries_gate, kv_first, kv_rest, own],
        [((rest, width), F32)],
        [],
        10,
        3 * rest * length * width,
        4 * 1024 * 1024,
        HEADS * rest * length,
    )
    keep, send = call(
        add_kernel,
        "add_parts",
        [own, *got, att],
        [((take, half_width), F32)] * 2,
        [pltpu.VMEM((pair, half_width), F32)],
        8,
        mps * pair * half_width,
        2 * mps * pair * half_width,
    )
    got = swap(send, "section", sections, 1)
    (pooled,) = call(
        functools.partial(attend_rest_kernel, first, late, dps),
        "attend_last",
        [bounds, gain, queries_gate, kv_first, kv_rest, sums_g, sums_ev, full_wout, att, keep],
        [((sess, width), BF16)],
        [pltpu.VMEM((rest, width), F32), pltpu.VMEM((sess, width), F32)],
        10,
        rest * length * width // 2,
        4 * 1024 * 1024,
        HEADS * rest * length // 8,
    )
    (cross_out,) = call(
        finish_kernel,
        "finish",
        [keep, got],
        [((take, half_width * sections), BF16)],
        [],
        8,
        0,
        16 * take * half_width,
    )
    return (pooled, cross_out)


def solution(mesh):
    sizes = [mesh.shape[name] for name in ("section", "dp", "mp")]
    return jax.shard_map(
        functools.partial(per_device, *sizes),
        mesh=mesh,
        in_specs=(
            P(("section", "dp", "mp"), None, None),
            P(("section", "dp", "mp")),
            P(("section", "dp", "mp"), None),
            P("dp", None),
            P("dp", None),
            P(),
            P(None, ("section", "mp")),
            P(None, ("section", "mp")),
            P("section", "mp"),
            P("mp", "section"),
        ),
        out_specs=(P(("section", "dp", "mp"), None), P(("section", "dp", "mp"), None)),
        check_vma=False,
    )
```

```python
import functools

import jax
import jax.numpy as jnp
from jax import lax
from jax.experimental import pallas as pl
from jax.experimental.pallas import tpu as pltpu
from jax.sharding import PartitionSpec as P

HEADS = 4
DM = 4096
MICRO = 4
SESS_MAX = 64
EPSILON = 1e-06
F32 = jnp.float32
BF16 = jnp.bfloat16

VMEM = pl.BlockSpec(memory_space=pltpu.VMEM)


def swap(x, axis, size, flip):
    return lax.ppermute(x, axis, [(i, i ^ flip) for i in range(size)])


def silu_half(h):
    return h + h * jnp.tanh(h)


def order_of(dps):
    return [0, *range(2, dps), 1]


def in_order(ref, at, dps):
    if dps == 1:
        return ref[at, :]
    z = lax.axis_index("dp")
    cols = ref.shape[1] // dps
    return jnp.concatenate([ref[at, pl.ds(pl.multiple_of((z ^ k) * cols, cols), cols)] for k in order_of(dps)], axis=1)


def project(dps, row0, hist, ev_ref, w_ref, gate_ref, q_ref, kv_ref):
    rows, width = ev_ref.shape
    step = min(rows, 512)
    for r in range(0, rows, step):
        at = slice(r, r + step)
        x = in_order(ev_ref, at, dps)
        row_pos = lax.broadcasted_iota(jnp.int32, (step, 1), 0).astype(F32) + (row0 + r)

        def act(n):
            part = jnp.dot(x, w_ref[:, n * width : (n + 1) * width], preferred_element_type=F32)
            return silu_half(part * 0.5)

        gate_ref[at, :] = act(0).astype(gate_ref.dtype)
        kv_ref[at, :width] = jnp.where(row_pos < hist, act(1), 0.0).astype(BF16)
        q_ref[at, :] = act(2).astype(BF16)
        kv_ref[at, width:] = act(3).astype(BF16)


STEP = 256


def attend(q_ref, kv_refs, att_ref):
    rows, width = q_ref.shape
    head = width // HEADS
    step = min(rows, STEP)
    *earlier, own = kv_refs
    for i in range(rows // step):
        at = slice(i * step, (i + 1) * step)
        upto = slice(0, (i + 1) * step)
        row = lax.broadcasted_iota(jnp.int32, (step, (i + 1) * step), 0) + i * step
        seen = lax.broadcasted_iota(jnp.int32, (step, (i + 1) * step), 1) <= row
        for h in range(HEADS):
            q = q_ref[at, h * head : (h + 1) * head]
            total = None
            for ref, keys in [*[(ref, slice(0, ref.shape[0])) for ref in earlier], (own, upto)]:
                k = ref[keys, width + h * head : width + (h + 1) * head]
                v = ref[keys, h * head : (h + 1) * head]
                s = lax.dot_general(q, k, (((1,), (1,)), ((), ())), preferred_element_type=F32)
                wts = silu_half(s * (0.5 * head**-0.5))
                if ref is own:
                    wts = jnp.where(seen, wts, 0.0)
                mixed = jnp.dot(wts.astype(BF16), v, preferred_element_type=F32)
                total = mixed if total is None else total + mixed
            att_ref[at, h * head : (h + 1) * head] = total


def gated_rows(att, gain_ref, gate):
    inv = lax.rsqrt(jnp.mean(att * att, axis=1, keepdims=True) + EPSILON)
    return (att * inv * gain_ref[:1] * gate.astype(F32)).astype(BF16)


def membership(bounds_ref, row0, rows):
    starts, ends = bounds_ref[0, :, :1], bounds_ref[1, :, :1]
    pos = (lax.broadcasted_iota(jnp.int32, (starts.shape[0], rows), 1) + row0).astype(F32)
    return jnp.where((pos >= starts) & (pos < ends), 1.0, 0.0).astype(BF16)


def pool(dps, bounds_ref, sums_ev, sums_ref, wout_ref):
    n_valid = jnp.maximum(bounds_ref[1, :, :1] - bounds_ref[0, :, :1], 1.0)
    sess = sums_ev.shape[0]
    sums_g = in_order(sums_ref, slice(None), dps)
    hi = sums_g.astype(BF16)
    rest = sums_g - hi.astype(F32)
    mid = rest.astype(BF16)
    low = (rest - mid.astype(F32)).astype(BF16)
    terms = jnp.dot(jnp.concatenate([low, mid, hi], axis=0), wout_ref[...], preferred_element_type=F32)
    return (terms[:sess] + terms[sess : 2 * sess] + terms[2 * sess :] + sums_ev) / n_valid


def first_kernel(place, dps, copies_out, n_parts, bounds_ref, ev_ref, gain_ref, *refs):
    parts, refs = refs[:n_parts], refs[n_parts:]
    pooled_ref, w_ref, wout_ref, kv_ref, sums_ev_ref, sums_g_ref, q_ref, gate_ref, att_ref = refs
    place(parts, w_ref, wout_ref)
    member = membership(bounds_ref, 0, ev_ref.shape[0])
    sums_ev = jnp.dot(member, ev_ref[...], preferred_element_type=F32)
    sums_ev_ref[...] = sums_ev
    project(dps, 0, bounds_ref[2, :1, :1], ev_ref, w_ref, gate_ref, q_ref, kv_ref)
    attend(q_ref, [kv_ref], att_ref)
    gated = gated_rows(att_ref[...], gain_ref, gate_ref[...])
    sums_g_ref[...] = jnp.dot(member, gated, preferred_element_type=F32)
    out = pool(dps, bounds_ref, sums_ev, sums_g_ref, wout_ref)
    peers, take = copies_out
    pooled_ref[...] = jnp.concatenate([out[:take]] * peers, axis=0).astype(BF16)


def halves(ref):
    cols = ref.shape[1] // 2
    return ref.at[:, :cols], ref.at[:, cols:]


def project_kernel(dps, row0, bounds_ref, ev_ref, w_ref, sums_ev_ref, _, qg_ref, kv_ref, out_ref):
    q_ref, gate_ref = halves(qg_ref)
    project(dps, row0, bounds_ref[2, :1, :1], ev_ref, w_ref, gate_ref, q_ref, kv_ref)
    member = membership(bounds_ref, row0, ev_ref.shape[0])
    out_ref[...] = sums_ev_ref[...] + jnp.dot(member, ev_ref[...], preferred_element_type=F32)


def attend_kernel(row0, bounds_ref, gain_ref, qg_ref, kv_first, kv_ref, sums_ref, _, out_ref, att_ref):
    q_ref, gate_ref = halves(qg_ref)
    attend(q_ref, [kv_first, kv_ref], att_ref)
    gated = gated_rows(att_ref[...], gain_ref, gate_ref[...])
    member = membership(bounds_ref, row0, q_ref.shape[0])
    out_ref[...] = sums_ref[...] + jnp.dot(member, gated, preferred_element_type=F32)


def pool_kernel(dps, bounds_ref, sums_ev_ref, sums_ref, wout_ref, _, out_ref):
    out_ref[...] = pool(dps, bounds_ref, sums_ev_ref[...], sums_ref, wout_ref).astype(BF16)


def call(kernel, name, operands, out_shape, scratch, mib, flops, size, transcendentals=0):
    return pl.pallas_call(
        kernel,
        in_specs=[VMEM] * len(operands),
        out_specs=[VMEM] * len(out_shape),
        out_shape=[jax.ShapeDtypeStruct(shape, kind) for shape, kind in out_shape],
        scratch_shapes=scratch,
        compiler_params=pltpu.CompilerParams(vmem_limit_bytes=mib * 1024 * 1024),
        cost_estimate=pl.CostEstimate(flops=flops, bytes_accessed=size, transcendentals=transcendentals),
        name=name,
    )(*operands)


def parity(m):
    return (m & 1) ^ ((m >> 1) & 1)


def split_kernel(*refs):
    *parts, left_ref, right_ref, both_ref = refs
    half = left_ref.shape[2]
    for k, part in enumerate(parts):
        for i, ref in enumerate((left_ref, right_ref)):
            piece = part[:, i * half : (i + 1) * half]
            ref[k] = piece
            both_ref[i, k] = piece


def gather_weights(w_uvqk, w_out, w_in, ffn_gain, sections, dps, mps):
    depth, wide = w_uvqk.shape
    width = w_out.shape[1]
    w_in = jnp.concatenate([w_in, ffn_gain, jnp.zeros((15, w_in.shape[1]), BF16)], axis=0)
    if (sections, mps) != (2, 4) or wide != 4 * width or depth % 128:
        ws = [lax.all_gather(x, "dp", axis=0, tiled=True) for x in (w_uvqk, w_out)]
        blocks = [[w_in]] + [[swap(w_in, "mp", mps, k)] for k in range(1, mps)]

        def place_whole(parts, w_ref, wout_ref):
            w_ref[...] = parts[0][...]
            wout_ref[...] = parts[1][...]

        return place_whole, ws, blocks, 1

    part = depth // 4
    cut = width // 2
    sec, m = lax.axis_index("section"), lax.axis_index("mp")
    share = sec * 2 + parity(m)
    mine = jnp.concatenate(
        [
            lax.dynamic_slice_in_dim(w_uvqk, share * width, width, 1),
            lax.dynamic_slice_in_dim(w_out, share * part, part, 0),
        ],
        axis=0,
    )
    got = [swap(mine, "dp", dps, k) for k in order_of(dps)[1:]]
    size = (len(got), depth + part, cut)
    left, right, both = call(
        split_kernel, "split", got, [(size, BF16), (size, BF16), ((2, *size), BF16)], [], 8, 0, 16 * 1024 * 1024
    )
    others = [swap(left, "mp", mps, 1), swap(right, "mp", mps, 2)]
    parts = [w_uvqk[:, : wide // 2], w_uvqk[:, wide // 2 :], w_out[: depth // 2], w_out[depth // 2 :]]
    parts = parts + [both, *others] + [swap(p, "section", sections, 1) for p in (both, *others)]

    from_x, from_y = swap(w_in, "mp", mps, 1), swap(w_in, "mp", mps, 2)
    middle = w_in.shape[0] // 32 * 16
    diagonal = [swap(from_x[:middle], "mp", mps, 2), swap(from_y[middle:], "mp", mps, 1)]
    blocks = [[w_in], [from_x], [from_y], diagonal]

    def place(parts, w_ref, wout_ref):
        sec, m = lax.axis_index("section"), lax.axis_index("mp")
        for i in range(2):
            w_ref[:depth, i * (wide // 2) : (i + 1) * (wide // 2)] = parts[i][...]
            wout_ref[i * (depth // 2) : (i + 1) * (depth // 2)] = parts[2 + i][...]
        for i, ref in enumerate(parts[4:]):
            other_sec, what = i // 3, i % 3
            owner = (sec ^ other_sec) * 2 + (parity(m) ^ (what > 0))
            for side in (0, 1) if what == 0 else (what - 1,):
                at = side * cut
                cols = pl.ds(pl.multiple_of(owner * width + at, cut), cut)
                for k in range(dps - 1):
                    piece = ref[side, k] if what == 0 else ref[k]
                    row = (k + 1) * depth
                    w_ref[row : row + depth, cols] = piece[:depth]
                    rows = pl.ds(pl.multiple_of(row + owner * part, part), part)
                    wout_ref[rows, at : at + cut] = piece[depth:]

    return place, parts, blocks, dps


def two_terms(square):
    hi = square.astype(BF16).astype(F32)
    lane = lax.broadcasted_iota(jnp.int32, (square.shape[0], 128), 1)
    return jnp.where(lane == 0, hi, jnp.where(lane == 1, square - hi, 0.0)).astype(BF16)


def up_kernel(chunks, pieces, x_ref, *refs):
    w_in_refs, refs = refs[: sum(pieces)], refs[sum(pieces) :]
    w_ref, local_ref, half_ref, send_ref, normed_ref = refs
    m = lax.axis_index("mp")
    depth = x_ref.shape[1]
    x = x_ref[...]
    square = None
    at = 0
    for k, n in enumerate(pieces):
        block = jnp.concatenate([r[...] for r in w_in_refs[at : at + n]], axis=0)
        at += n
        hidden = jnp.dot(x, block[:depth], preferred_element_type=F32)
        part = jnp.sum(hidden * hidden, axis=1, keepdims=True)
        square = part if square is None else square + part
        gain = block[depth:].astype(F32)[:1]
        cols = hidden.shape[1]
        normed_ref[:, pl.ds(pl.multiple_of((m ^ k) * cols, cols), cols)] = (hidden * gain).astype(BF16)
        if k == 0:
            local_ref[...] = hidden
    normed = normed_ref[...]
    wide = w_ref.shape[1]
    each = wide // chunks
    for c in range(chunks):
        at = slice(c * each, (c + 1) * each)
        half = jnp.dot(normed, w_ref[:, at], preferred_element_type=F32)
        half_ref[:, at] = half
        send_ref[:, at] = half.astype(BF16)
    half_ref[:, wide:] = jnp.broadcast_to(square, (x.shape[0], 128))
    send_ref[:, wide:] = two_terms(square)


def down_kernel(chunks, sections, mps, take, half_ref, other_ref, local_ref, w_ref, _, own_ref, *refs):
    *send_refs, part_ref = refs
    units, wide = w_ref.shape
    each = wide // chunks
    square = half_ref[:, units : units + 1] + jnp.sum(other_ref[:, units:].astype(F32), axis=1, keepdims=True)
    inv = lax.rsqrt(square / DM + EPSILON)
    up = (half_ref[:, :units] + other_ref[:, :units].astype(F32)) * inv
    hidden = jax.nn.gelu(up, approximate=True).astype(BF16)
    for c in range(chunks):
        at = slice(c * each, (c + 1) * each)
        part_ref[:, at] = jnp.dot(hidden, w_ref[:, at], preferred_element_type=F32)
    m = lax.axis_index("mp")
    cols = local_ref.shape[1]
    own = pl.ds(pl.multiple_of(m * cols, cols), cols)
    part_ref[:, own] = part_ref[:, own] + local_ref[...]
    for k, ref in enumerate([own_ref, *send_refs]):
        starts = [pl.multiple_of((s * mps + (m ^ k)) * take, take) for s in range(sections)]
        mine = [part_ref[pl.ds(start, take), :] for start in starts]
        ref[...] = jnp.concatenate(mine, axis=0).astype(ref.dtype)


def add_kernel(own_ref, *refs):
    *got_refs, _, keep_ref, send_ref, total_ref = refs
    total = own_ref[...]
    for ref in got_refs:
        total = total + ref[...].astype(F32)
    total_ref[...] = total
    sec = lax.axis_index("section")
    take = keep_ref.shape[0]
    keep_ref[...] = total_ref[pl.ds(pl.multiple_of(sec * take, take), take), :]
    send_ref[...] = total_ref[pl.ds(pl.multiple_of((1 - sec) * take, take), take), :]


def finish_kernel(keep_ref, got_ref, out_ref):
    sec = lax.axis_index("section")
    wide = keep_ref.shape[1]
    out_ref[:, pl.ds(pl.multiple_of(sec * wide, wide), wide)] = keep_ref[...].astype(BF16)
    out_ref[:, pl.ds(pl.multiple_of((1 - sec) * wide, wide), wide)] = got_ref[...].astype(BF16)


def per_device(sections, dps, mps, events, hist_len, sess_len, w_uvqk, w_out, attn_gain, w_in, ffn_gain, w_up, w_down):
    events = events[0]
    length, width = events.shape
    sess = sess_len.shape[1]
    take = sess // MICRO
    peers = sections * mps
    rows = take * peers
    cols = w_in.shape[1]
    units = w_up.shape[1]
    half_width = w_down.shape[1]
    group = ("section", "mp")
    first = take * SESS_MAX
    rest = length - first

    gain = jnp.broadcast_to(attn_gain, (8, width))
    ends = jnp.sum(jnp.where(jnp.tri(sess, dtype=jnp.bool_), sess_len, 0), axis=1)
    bounds = jnp.stack([ends - sess_len[0], jnp.minimum(ends, hist_len), jnp.broadcast_to(hist_len, ends.shape)])
    bounds = jnp.broadcast_to(bounds.astype(F32)[:, :, None], (3, sess, 128))
    place, parts, w_in_blocks, dps = gather_weights(w_uvqk, w_out, w_in, ffn_gain, sections, dps, mps)

    micro_rows, full_w, full_wout, kv_first, sums_ev, sums_g = call(
        functools.partial(first_kernel, place, dps, (peers, take), len(parts)),
        "encode_first",
        [bounds, events[:first], gain, *parts],
        [
            ((rows, width), BF16),
            ((width, 4 * width), BF16),
            ((width, width), BF16),
            ((first, 2 * width), BF16),
            ((sess, width), F32),
            ((sess, width), F32),
        ],
        [
            pltpu.VMEM((first, width), BF16),
            pltpu.VMEM((first, width), F32),
            pltpu.VMEM((first, width), F32),
        ],
        16,
        8 * first * width * width + 2 * first * first * width,
        6 * 1024 * 1024,
        4 * first * width + HEADS * first * first,
    )
    arrived = lax.all_to_all(
        micro_rows.reshape(peers, take, width), group, split_axis=0, concat_axis=0, tiled=True
    ).reshape(rows, width)
    blocks = [piece for block in w_in_blocks for piece in block]
    local, half, half_send = call(
        functools.partial(up_kernel, 4, [len(block) for block in w_in_blocks]),
        "up_half",
        [arrived, *blocks, w_up],
        [((rows, cols), F32), ((rows, units + 128), F32), ((rows, units + 128), BF16)],
        [pltpu.VMEM((rows, w_up.shape[0]), BF16)],
        10,
        2 * rows * w_up.size,
        2 * w_up.size,
    )
    other = swap(half_send, "section", sections, 1)
    queries_gate, kv_rest, sums_ev = call(
        functools.partial(project_kernel, dps, first),
        "project_rest",
        [bounds, events[first:], full_w, sums_ev, local],
        [((rest, 2 * width), BF16), ((rest, 2 * width), BF16), ((sess, width), F32)],
        [],
        10,
        8 * rest * width * width,
        6 * 1024 * 1024,
        4 * rest * width,
    )
    pair = sections * take
    own, *sends = call(
        functools.partial(down_kernel, 4, sections, mps, take),
        "down_part",
        [half, other, local, w_down, sums_ev],
        [((pair, half_width), F32)] + [((pair, half_width), BF16)] * (mps - 1),
        [pltpu.VMEM((rows, half_width), F32)],
        8,
        2 * rows * w_down.size,
        2 * w_down.size,
        rows * units,
    )

    got = [swap(x, "mp", mps, k + 1) for k, x in enumerate(sends)]
    (sums_g,) = call(
        functools.partial(attend_kernel, first),
        "attend_rest",
        [bounds, gain, queries_gate, kv_first, kv_rest, sums_g, own],
        [((sess, width), F32)],
        [pltpu.VMEM((rest, width), F32)],
        10,
        4 * rest * length * width,
        4 * 1024 * 1024,
        HEADS * rest * length,
    )
    keep, send = call(
        add_kernel,
        "add_parts",
        [own, *got, sums_g],
        [((take, half_width), F32)] * 2,
        [pltpu.VMEM((pair, half_width), F32)],
        8,
        mps * pair * half_width,
        2 * mps * pair * half_width,
    )
    got = swap(send, "section", sections, 1)
    (pooled,) = call(
        functools.partial(pool_kernel, dps),
        "pool_rows",
        [bounds, sums_ev, sums_g, full_wout, keep],
        [((sess, width), BF16)],
        [],
        8,
        6 * sess * width * width,
        1024 * 1024,
    )
    (cross_out,) = call(
        finish_kernel,
        "finish",
        [keep, got],
        [((take, half_width * sections), BF16)],
        [],
        8,
        0,
        16 * take * half_width,
    )
    return (pooled, cross_out)


def solution(mesh):
    sizes = [mesh.shape[name] for name in ("section", "dp", "mp")]
    return jax.shard_map(
        functools.partial(per_device, *sizes),
        mesh=mesh,
        in_specs=(
            P(("section", "dp", "mp"), None, None),
            P(("section", "dp", "mp")),
            P(("section", "dp", "mp"), None),
            P("dp", None),
            P("dp", None),
            P(),
            P(None, ("section", "mp")),
            P(None, ("section", "mp")),
            P("section", "mp"),
            P("mp", "section"),
        ),
        out_specs=(P(("section", "dp", "mp"), None), P(("section", "dp", "mp"), None)),
        check_vma=False,
    )
```

```python
import functools

import jax
import jax.numpy as jnp
from jax import lax
from jax.experimental import pallas as pl
from jax.experimental.pallas import tpu as pltpu
from jax.sharding import PartitionSpec as P

HEADS = 4
DM = 4096
MICRO = 4
SESS_MAX = 64
EPSILON = 1e-06
STEP = 256
F32 = jnp.float32
BF16 = jnp.bfloat16

VMEM = pl.BlockSpec(memory_space=pltpu.VMEM)


def swap(x, axis, size, flip):
    return lax.ppermute(x, axis, [(i, i ^ flip) for i in range(size)])


def silu_half(h):
    return h + h * jnp.tanh(h)


def order_of(dps):
    return [0, *range(2, dps), 1]


def in_order(ref, at, dps):
    if dps == 1:
        return ref[at, :]
    z = lax.axis_index("dp")
    cols = ref.shape[1] // dps
    return jnp.concatenate([ref[at, pl.ds(pl.multiple_of((z ^ k) * cols, cols), cols)] for k in order_of(dps)], axis=1)


def project(dps, row0, hist, ev_ref, w_ref, gate_ref, q_ref, kv_ref):
    rows, width = ev_ref.shape
    step = min(rows, STEP)
    for r in range(0, rows, step):
        at = slice(r, r + step)
        x = in_order(ev_ref, at, dps)
        row_pos = lax.broadcasted_iota(jnp.int32, (step, 1), 0).astype(F32) + (row0 + r)

        def act(n):
            part = jnp.dot(x, w_ref[:, n * width : (n + 1) * width], preferred_element_type=F32)
            return silu_half(part * 0.5)

        gate_ref[at, :] = act(0).astype(gate_ref.dtype)
        kv_ref[at, :width] = jnp.where(row_pos < hist, act(1), 0.0).astype(BF16)
        q_ref[at, :] = act(2).astype(BF16)
        kv_ref[at, width:] = act(3).astype(BF16)


def attend(q_ref, kv_refs, att_ref):
    rows, width = q_ref.shape
    head = width // HEADS
    step = min(rows, STEP)
    *earlier, own = kv_refs
    for i in range(rows // step):
        at = slice(i * step, (i + 1) * step)
        upto = slice(0, (i + 1) * step)
        row = lax.broadcasted_iota(jnp.int32, (step, (i + 1) * step), 0) + i * step
        seen = lax.broadcasted_iota(jnp.int32, (step, (i + 1) * step), 1) <= row
        for h in range(HEADS):
            q = q_ref[at, h * head : (h + 1) * head]
            total = None
            for ref, keys in [*[(ref, slice(0, ref.shape[0])) for ref in earlier], (own, upto)]:
                k = ref[keys, width + h * head : width + (h + 1) * head]
                v = ref[keys, h * head : (h + 1) * head]
                s = lax.dot_general(q, k, (((1,), (1,)), ((), ())), preferred_element_type=F32)
                wts = silu_half(s * (0.5 * head**-0.5))
                if ref is own:
                    wts = jnp.where(seen, wts, 0.0)
                mixed = jnp.dot(wts.astype(BF16), v, preferred_element_type=F32)
                total = mixed if total is None else total + mixed
            att_ref[at, h * head : (h + 1) * head] = total


def gated_rows(att, gain_ref, gate):
    inv = lax.rsqrt(jnp.mean(att * att, axis=1, keepdims=True) + EPSILON)
    return (att * inv * gain_ref[:1] * gate.astype(F32)).astype(BF16)


def membership(bounds_ref, row0, rows):
    starts, ends = bounds_ref[0, :, :1], bounds_ref[1, :, :1]
    pos = (lax.broadcasted_iota(jnp.int32, (starts.shape[0], rows), 1) + row0).astype(F32)
    return jnp.where((pos >= starts) & (pos < ends), 1.0, 0.0).astype(BF16)


def pool(dps, bounds_ref, sums_ev, sums_ref, wout_ref):
    n_valid = jnp.maximum(bounds_ref[1, :, :1] - bounds_ref[0, :, :1], 1.0)
    sess = sums_ev.shape[0]
    sums_g = in_order(sums_ref, slice(None), dps)
    hi = sums_g.astype(BF16)
    rest = sums_g - hi.astype(F32)
    mid = rest.astype(BF16)
    low = (rest - mid.astype(F32)).astype(BF16)
    terms = jnp.dot(jnp.concatenate([low, mid, hi], axis=0), wout_ref[...], preferred_element_type=F32)
    return (terms[:sess] + terms[sess : 2 * sess] + terms[2 * sess :] + sums_ev) / n_valid


def first_kernel(place, dps, copies_out, n_parts, bounds_ref, ev_ref, gain_ref, *refs):
    parts, refs = refs[:n_parts], refs[n_parts:]
    pooled_ref, w_ref, wout_ref, kv_ref, sums_ev_ref, sums_g_ref, q_ref, gate_ref, att_ref = refs
    place(parts, w_ref, wout_ref)
    member = membership(bounds_ref, 0, ev_ref.shape[0])
    sums_ev = jnp.dot(member, ev_ref[...], preferred_element_type=F32)
    sums_ev_ref[...] = sums_ev
    project(dps, 0, bounds_ref[2, :1, :1], ev_ref, w_ref, gate_ref, q_ref, kv_ref)
    attend(q_ref, [kv_ref], att_ref)
    gated = gated_rows(att_ref[...], gain_ref, gate_ref[...])
    sums_g_ref[...] = jnp.dot(member, gated, preferred_element_type=F32)
    out = pool(dps, bounds_ref, sums_ev, sums_g_ref, wout_ref)
    peers, take = copies_out
    pooled_ref[...] = jnp.concatenate([out[:take]] * peers, axis=0).astype(BF16)


def halves(ref):
    cols = ref.shape[1] // 2
    return ref.at[:, :cols], ref.at[:, cols:]


def project_kernel(dps, row0, bounds_ref, ev_ref, w_ref, sums_ev_ref, _, qg_ref, kv_ref, out_ref):
    q_ref, gate_ref = halves(qg_ref)
    project(dps, row0, bounds_ref[2, :1, :1], ev_ref, w_ref, gate_ref, q_ref, kv_ref)
    member = membership(bounds_ref, row0, ev_ref.shape[0])
    out_ref[...] = sums_ev_ref[...] + jnp.dot(member, ev_ref[...], preferred_element_type=F32)


def attend_kernel(row0, bounds_ref, gain_ref, qg_ref, kv_first, kv_ref, sums_ref, _, out_ref, att_ref):
    q_ref, gate_ref = halves(qg_ref)
    attend(q_ref, [kv_first, kv_ref], att_ref)
    gated = gated_rows(att_ref[...], gain_ref, gate_ref[...])
    member = membership(bounds_ref, row0, q_ref.shape[0])
    out_ref[...] = sums_ref[...] + jnp.dot(member, gated, preferred_element_type=F32)


def pool_kernel(dps, bounds_ref, sums_ev_ref, sums_ref, wout_ref, _, out_ref):
    out_ref[...] = pool(dps, bounds_ref, sums_ev_ref[...], sums_ref, wout_ref).astype(BF16)


def call(kernel, name, operands, out_shape, scratch, mib, flops, size, transcendentals=0):
    return pl.pallas_call(
        kernel,
        in_specs=[VMEM] * len(operands),
        out_specs=[VMEM] * len(out_shape),
        out_shape=[jax.ShapeDtypeStruct(shape, kind) for shape, kind in out_shape],
        scratch_shapes=scratch,
        compiler_params=pltpu.CompilerParams(vmem_limit_bytes=mib * 1024 * 1024),
        cost_estimate=pl.CostEstimate(flops=flops, bytes_accessed=size, transcendentals=transcendentals),
        name=name,
    )(*operands)


def parity(m):
    return (m & 1) ^ ((m >> 1) & 1)


def split_kernel(*refs):
    *parts, left_ref, right_ref, both_ref = refs
    half = left_ref.shape[2]
    for k, part in enumerate(parts):
        for i, ref in enumerate((left_ref, right_ref)):
            piece = part[:, i * half : (i + 1) * half]
            ref[k] = piece
            both_ref[i, k] = piece


def gather_weights(w_uvqk, w_out, w_in, ffn_gain, sections, dps, mps):
    depth, wide = w_uvqk.shape
    width = w_out.shape[1]
    w_in = jnp.concatenate([w_in, ffn_gain, jnp.zeros((15, w_in.shape[1]), BF16)], axis=0)
    if (sections, mps) != (2, 4) or wide != 4 * width or depth % 128:
        ws = [lax.all_gather(x, "dp", axis=0, tiled=True) for x in (w_uvqk, w_out)]
        blocks = [[w_in]] + [[swap(w_in, "mp", mps, k)] for k in range(1, mps)]

        def place_whole(parts, w_ref, wout_ref):
            w_ref[...] = parts[0][...]
            wout_ref[...] = parts[1][...]

        return place_whole, ws, blocks, 1

    part = depth // 4
    cut = width // 2
    sec, m = lax.axis_index("section"), lax.axis_index("mp")
    share = sec * 2 + parity(m)
    mine = jnp.concatenate(
        [
            lax.dynamic_slice_in_dim(w_uvqk, share * width, width, 1),
            lax.dynamic_slice_in_dim(w_out, share * part, part, 0),
        ],
        axis=0,
    )
    got = [swap(mine, "dp", dps, k) for k in order_of(dps)[1:]]
    size = (len(got), depth + part, cut)
    left, right, both = call(
        split_kernel, "split", got, [(size, BF16), (size, BF16), ((2, *size), BF16)], [], 8, 0, 16 * 1024 * 1024
    )
    others = [swap(left, "mp", mps, 1), swap(right, "mp", mps, 2)]
    parts = [w_uvqk[:, : wide // 2], w_uvqk[:, wide // 2 :], w_out[: depth // 2], w_out[depth // 2 :]]
    parts = parts + [both, *others] + [swap(p, "section", sections, 1) for p in (both, *others)]

    from_x, from_y = swap(w_in, "mp", mps, 1), swap(w_in, "mp", mps, 2)
    middle = w_in.shape[0] // 32 * 16
    diagonal = [swap(from_x[:middle], "mp", mps, 2), swap(from_y[middle:], "mp", mps, 1)]
    blocks = [[w_in], [from_x], [from_y], diagonal]

    def place(parts, w_ref, wout_ref):
        sec, m = lax.axis_index("section"), lax.axis_index("mp")
        for i in range(2):
            w_ref[:depth, i * (wide // 2) : (i + 1) * (wide // 2)] = parts[i][...]
            wout_ref[i * (depth // 2) : (i + 1) * (depth // 2)] = parts[2 + i][...]
        for i, ref in enumerate(parts[4:]):
            other_sec, what = i // 3, i % 3
            owner = (sec ^ other_sec) * 2 + (parity(m) ^ (what > 0))
            for side in (0, 1) if what == 0 else (what - 1,):
                at = side * cut
                cols = pl.ds(pl.multiple_of(owner * width + at, cut), cut)
                for k in range(dps - 1):
                    piece = ref[side, k] if what == 0 else ref[k]
                    row = (k + 1) * depth
                    w_ref[row : row + depth, cols] = piece[:depth]
                    rows = pl.ds(pl.multiple_of(row + owner * part, part), part)
                    wout_ref[rows, at : at + cut] = piece[depth:]

    return place, parts, blocks, dps


def two_terms(square):
    hi = square.astype(BF16).astype(F32)
    lane = lax.broadcasted_iota(jnp.int32, (square.shape[0], 128), 1)
    return jnp.where(lane == 0, hi, jnp.where(lane == 1, square - hi, 0.0)).astype(BF16)


def up_kernel(chunks, pieces, x_ref, *refs):
    w_in_refs, refs = refs[: sum(pieces)], refs[sum(pieces) :]
    w_ref, local_ref, half_ref, send_ref, normed_ref = refs
    m = lax.axis_index("mp")
    depth = x_ref.shape[1]
    x = x_ref[...]
    square = None
    at = 0
    for k, n in enumerate(pieces):
        block = jnp.concatenate([r[...] for r in w_in_refs[at : at + n]], axis=0)
        at += n
        hidden = jnp.dot(x, block[:depth], preferred_element_type=F32)
        part = jnp.sum(hidden * hidden, axis=1, keepdims=True)
        square = part if square is None else square + part
        gain = block[depth:].astype(F32)[:1]
        cols = hidden.shape[1]
        normed_ref[:, pl.ds(pl.multiple_of((m ^ k) * cols, cols), cols)] = (hidden * gain).astype(BF16)
        if k == 0:
            local_ref[...] = hidden
    normed = normed_ref[...]
    wide = w_ref.shape[1]
    each = wide // chunks
    for c in range(chunks):
        at = slice(c * each, (c + 1) * each)
        half = jnp.dot(normed, w_ref[:, at], preferred_element_type=F32)
        half_ref[:, at] = half
        send_ref[:, at] = half.astype(BF16)
    half_ref[:, wide:] = jnp.broadcast_to(square, (x.shape[0], 128))
    send_ref[:, wide:] = two_terms(square)


def down_kernel(chunks, sections, mps, take, half_ref, other_ref, local_ref, w_ref, _, own_ref, *refs):
    *send_refs, part_ref = refs
    units, wide = w_ref.shape
    each = wide // chunks
    square = half_ref[:, units : units + 1] + jnp.sum(other_ref[:, units:].astype(F32), axis=1, keepdims=True)
    inv = lax.rsqrt(square / DM + EPSILON)
    up = (half_ref[:, :units] + other_ref[:, :units].astype(F32)) * inv
    hidden = jax.nn.gelu(up, approximate=True).astype(BF16)
    for c in range(chunks):
        at = slice(c * each, (c + 1) * each)
        part_ref[:, at] = jnp.dot(hidden, w_ref[:, at], preferred_element_type=F32)
    m = lax.axis_index("mp")
    cols = local_ref.shape[1]
    own = pl.ds(pl.multiple_of(m * cols, cols), cols)
    part_ref[:, own] = part_ref[:, own] + local_ref[...]
    for k, ref in enumerate([own_ref, *send_refs]):
        starts = [pl.multiple_of((s * mps + (m ^ k)) * take, take) for s in range(sections)]
        mine = [part_ref[pl.ds(start, take), :] for start in starts]
        ref[...] = jnp.concatenate(mine, axis=0).astype(ref.dtype)


def add_kernel(own_ref, *refs):
    *got_refs, _, keep_ref, send_ref, total_ref = refs
    total = own_ref[...]
    for ref in got_refs:
        total = total + ref[...].astype(F32)
    total_ref[...] = total
    sec = lax.axis_index("section")
    take = keep_ref.shape[0]
    keep_ref[...] = total_ref[pl.ds(pl.multiple_of(sec * take, take), take), :]
    send_ref[...] = total_ref[pl.ds(pl.multiple_of((1 - sec) * take, take), take), :]


def finish_kernel(keep_ref, got_ref, out_ref):
    sec = lax.axis_index("section")
    wide = keep_ref.shape[1]
    out_ref[:, pl.ds(pl.multiple_of(sec * wide, wide), wide)] = keep_ref[...].astype(BF16)
    out_ref[:, pl.ds(pl.multiple_of((1 - sec) * wide, wide), wide)] = got_ref[...].astype(BF16)


def per_device(sections, dps, mps, events, hist_len, sess_len, w_uvqk, w_out, attn_gain, w_in, ffn_gain, w_up, w_down):
    events = events[0]
    length, width = events.shape
    sess = sess_len.shape[1]
    take = sess // MICRO
    peers = sections * mps
    rows = take * peers
    cols = w_in.shape[1]
    units = w_up.shape[1]
    half_width = w_down.shape[1]
    group = ("section", "mp")
    first = take * SESS_MAX
    rest = length - first

    gain = jnp.broadcast_to(attn_gain, (8, width))
    ends = jnp.sum(jnp.where(jnp.tri(sess, dtype=jnp.bool_), sess_len, 0), axis=1)
    bounds = jnp.stack([ends - sess_len[0], jnp.minimum(ends, hist_len), jnp.broadcast_to(hist_len, ends.shape)])
    bounds = jnp.broadcast_to(bounds.astype(F32)[:, :, None], (3, sess, 128))
    place, parts, w_in_blocks, dps = gather_weights(w_uvqk, w_out, w_in, ffn_gain, sections, dps, mps)

    micro_rows, full_w, full_wout, kv_first, sums_ev, sums_g = call(
        functools.partial(first_kernel, place, dps, (peers, take), len(parts)),
        "encode_first",
        [bounds, events[:first], gain, *parts],
        [
            ((rows, width), BF16),
            ((width, 4 * width), BF16),
            ((width, width), BF16),
            ((first, 2 * width), BF16),
            ((sess, width), F32),
            ((sess, width), F32),
        ],
        [
            pltpu.VMEM((first, width), BF16),
            pltpu.VMEM((first, width), F32),
            pltpu.VMEM((first, width), F32),
        ],
        16,
        8 * first * width * width + 2 * first * first * width,
        6 * 1024 * 1024,
        4 * first * width + HEADS * first * first,
    )
    arrived = lax.all_to_all(
        micro_rows.reshape(peers, take, width), group, split_axis=0, concat_axis=0, tiled=True
    ).reshape(rows, width)
    blocks = [piece for block in w_in_blocks for piece in block]
    local, half, half_send = call(
        functools.partial(up_kernel, 4, [len(block) for block in w_in_blocks]),
        "up_half",
        [arrived, *blocks, w_up],
        [((rows, cols), F32), ((rows, units + 128), F32), ((rows, units + 128), BF16)],
        [pltpu.VMEM((rows, w_up.shape[0]), BF16)],
        10,
        2 * rows * w_up.size,
        2 * w_up.size,
    )
    other = swap(half_send, "section", sections, 1)
    queries_gate, kv_rest, sums_ev = call(
        functools.partial(project_kernel, dps, first),
        "project_rest",
        [bounds, events[first:], full_w, sums_ev, local],
        [((rest, 2 * width), BF16), ((rest, 2 * width), BF16), ((sess, width), F32)],
        [],
        10,
        8 * rest * width * width,
        6 * 1024 * 1024,
        4 * rest * width,
    )
    pair = sections * take
    own, *sends = call(
        functools.partial(down_kernel, 4, sections, mps, take),
        "down_part",
        [half, other, local, w_down, sums_ev],
        [((pair, half_width), F32)] + [((pair, half_width), BF16)] * (mps - 1),
        [pltpu.VMEM((rows, half_width), F32)],
        8,
        2 * rows * w_down.size,
        2 * w_down.size,
        rows * units,
    )

    got = [swap(sends[k - 1], "mp", mps, k) for k in range(mps - 1, 0, -1)]
    (sums_g,) = call(
        functools.partial(attend_kernel, first),
        "attend_rest",
        [bounds, gain, queries_gate, kv_first, kv_rest, sums_g, own],
        [((sess, width), F32)],
        [pltpu.VMEM((rest, width), F32)],
        10,
        4 * rest * length * width,
        4 * 1024 * 1024,
        HEADS * rest * length,
    )
    keep, send = call(
        add_kernel,
        "add_parts",
        [own, *got, sums_g],
        [((take, half_width), F32)] * 2,
        [pltpu.VMEM((pair, half_width), F32)],
        8,
        mps * pair * half_width,
        2 * mps * pair * half_width,
    )
    got = swap(send, "section", sections, 1)
    (pooled,) = call(
        functools.partial(pool_kernel, dps),
        "pool_rows",
        [bounds, sums_ev, sums_g, full_wout, keep],
        [((sess, width), BF16)],
        [],
        8,
        6 * sess * width * width,
        1024 * 1024,
    )
    (cross_out,) = call(
        finish_kernel,
        "finish",
        [keep, got],
        [((take, half_width * sections), BF16)],
        [],
        8,
        0,
        16 * take * half_width,
    )
    return (pooled, cross_out)


def solution(mesh):
    sizes = [mesh.shape[name] for name in ("section", "dp", "mp")]
    return jax.shard_map(
        functools.partial(per_device, *sizes),
        mesh=mesh,
        in_specs=(
            P(("section", "dp", "mp"), None, None),
            P(("section", "dp", "mp")),
            P(("section", "dp", "mp"), None),
            P("dp", None),
            P("dp", None),
            P(),
            P(None, ("section", "mp")),
            P(None, ("section", "mp")),
            P("section", "mp"),
            P("mp", "section"),
        ),
        out_specs=(P(("section", "dp", "mp"), None), P(("section", "dp", "mp"), None)),
        check_vma=False,
    )
```

```python
import functools

import jax
import jax.numpy as jnp
from jax import lax
from jax.experimental import pallas as pl
from jax.experimental.pallas import tpu as pltpu
from jax.sharding import PartitionSpec as P

HEADS = 4
DM = 4096
MICRO = 4
SESS_MAX = 64
EPSILON = 1e-06
STEP = 256
F32 = jnp.float32
BF16 = jnp.bfloat16

VMEM = pl.BlockSpec(memory_space=pltpu.VMEM)


def swap(x, axis, size, flip):
    return lax.ppermute(x, axis, [(i, i ^ flip) for i in range(size)])


def silu_half(h):
    return h + h * jnp.tanh(h)


def order_of(dps):
    return [0, *range(2, dps), 1]


def in_order(ref, at, dps):
    if dps == 1:
        return ref[at, :]
    z = lax.axis_index("dp")
    cols = ref.shape[1] // dps
    return jnp.concatenate([ref[at, pl.ds(pl.multiple_of((z ^ k) * cols, cols), cols)] for k in order_of(dps)], axis=1)


def project(dps, row0, hist, ev_ref, w_ref, gate_ref, q_ref, kv_ref):
    rows, width = ev_ref.shape
    step = min(rows, STEP)
    for r in range(0, rows, step):
        at = slice(r, r + step)
        x = in_order(ev_ref, at, dps)
        row_pos = lax.broadcasted_iota(jnp.int32, (step, 1), 0).astype(F32) + (row0 + r)

        def act(n):
            part = jnp.dot(x, w_ref[:, n * width : (n + 1) * width], preferred_element_type=F32)
            return silu_half(part * 0.5)

        gate_ref[at, :] = act(0).astype(gate_ref.dtype)
        kv_ref[at, :width] = jnp.where(row_pos < hist, act(1), 0.0).astype(BF16)
        q_ref[at, :] = act(2).astype(BF16)
        kv_ref[at, width:] = act(3).astype(BF16)


def attend(q_ref, kv_refs, att_ref):
    rows, width = q_ref.shape
    head = width // HEADS
    step = min(rows, STEP)
    *earlier, own = kv_refs
    for i in range(rows // step):
        at = slice(i * step, (i + 1) * step)
        upto = slice(0, (i + 1) * step)
        row = lax.broadcasted_iota(jnp.int32, (step, (i + 1) * step), 0) + i * step
        seen = lax.broadcasted_iota(jnp.int32, (step, (i + 1) * step), 1) <= row
        for h in range(HEADS):
            q = q_ref[at, h * head : (h + 1) * head]
            total = None
            for ref, keys in [*[(ref, slice(0, ref.shape[0])) for ref in earlier], (own, upto)]:
                k = ref[keys, width + h * head : width + (h + 1) * head]
                v = ref[keys, h * head : (h + 1) * head]
                s = lax.dot_general(q, k, (((1,), (1,)), ((), ())), preferred_element_type=F32)
                wts = silu_half(s * (0.5 * head**-0.5))
                if ref is own:
                    wts = jnp.where(seen, wts, 0.0)
                mixed = jnp.dot(wts.astype(BF16), v, preferred_element_type=F32)
                total = mixed if total is None else total + mixed
            att_ref[at, h * head : (h + 1) * head] = total


def gated_rows(att, gain_ref, gate):
    inv = lax.rsqrt(jnp.mean(att * att, axis=1, keepdims=True) + EPSILON)
    return (att * inv * gain_ref[:1] * gate.astype(F32)).astype(BF16)


def membership(bounds_ref, row0, rows):
    starts, ends = bounds_ref[0, :, :1], bounds_ref[1, :, :1]
    pos = (lax.broadcasted_iota(jnp.int32, (starts.shape[0], rows), 1) + row0).astype(F32)
    return jnp.where((pos >= starts) & (pos < ends), 1.0, 0.0).astype(BF16)


def pool(dps, bounds_ref, sums_ev, sums_ref, wout_ref):
    n_valid = jnp.maximum(bounds_ref[1, :, :1] - bounds_ref[0, :, :1], 1.0)
    sess = sums_ev.shape[0]
    sums_g = in_order(sums_ref, slice(None), dps)
    hi = sums_g.astype(BF16)
    rest = sums_g - hi.astype(F32)
    mid = rest.astype(BF16)
    low = (rest - mid.astype(F32)).astype(BF16)
    terms = jnp.dot(jnp.concatenate([low, mid, hi], axis=0), wout_ref[...], preferred_element_type=F32)
    return (terms[:sess] + terms[sess : 2 * sess] + terms[2 * sess :] + sums_ev) / n_valid


def first_kernel(place, dps, copies_out, n_parts, bounds_ref, ev_ref, gain_ref, *refs):
    parts, refs = refs[:n_parts], refs[n_parts:]
    pooled_ref, w_ref, wout_ref, kv_ref, sums_ev_ref, sums_g_ref, q_ref, gate_ref, att_ref = refs
    place(parts, w_ref, wout_ref)
    member = membership(bounds_ref, 0, ev_ref.shape[0])
    sums_ev = jnp.dot(member, ev_ref[...], preferred_element_type=F32)
    sums_ev_ref[...] = sums_ev
    project(dps, 0, bounds_ref[2, :1, :1], ev_ref, w_ref, gate_ref, q_ref, kv_ref)
    attend(q_ref, [kv_ref], att_ref)
    gated = gated_rows(att_ref[...], gain_ref, gate_ref[...])
    sums_g_ref[...] = jnp.dot(member, gated, preferred_element_type=F32)
    out = pool(dps, bounds_ref, sums_ev, sums_g_ref, wout_ref)
    peers, take = copies_out
    pooled_ref[...] = jnp.concatenate([out[:take]] * peers, axis=0).astype(BF16)


def halves(ref):
    cols = ref.shape[1] // 2
    return ref.at[:, :cols], ref.at[:, cols:]


def project_kernel(dps, row0, bounds_ref, ev_ref, w_ref, sums_ev_ref, _, qg_ref, kv_ref, out_ref):
    q_ref, gate_ref = halves(qg_ref)
    project(dps, row0, bounds_ref[2, :1, :1], ev_ref, w_ref, gate_ref, q_ref, kv_ref)
    member = membership(bounds_ref, row0, ev_ref.shape[0])
    out_ref[...] = sums_ev_ref[...] + jnp.dot(member, ev_ref[...], preferred_element_type=F32)


def attend_kernel(row0, bounds_ref, gain_ref, qg_ref, kv_first, kv_ref, sums_ref, _, out_ref, att_ref):
    q_ref, gate_ref = halves(qg_ref)
    attend(q_ref, [kv_first, kv_ref], att_ref)
    gated = gated_rows(att_ref[...], gain_ref, gate_ref[...])
    member = membership(bounds_ref, row0, q_ref.shape[0])
    out_ref[...] = sums_ref[...] + jnp.dot(member, gated, preferred_element_type=F32)


def pool_kernel(dps, bounds_ref, sums_ev_ref, sums_ref, wout_ref, _, out_ref):
    out_ref[...] = pool(dps, bounds_ref, sums_ev_ref[...], sums_ref, wout_ref).astype(BF16)


def call(kernel, name, operands, out_shape, scratch, mib, flops, size, transcendentals=0):
    return pl.pallas_call(
        kernel,
        in_specs=[VMEM] * len(operands),
        out_specs=[VMEM] * len(out_shape),
        out_shape=[jax.ShapeDtypeStruct(shape, kind) for shape, kind in out_shape],
        scratch_shapes=scratch,
        compiler_params=pltpu.CompilerParams(vmem_limit_bytes=mib * 1024 * 1024),
        cost_estimate=pl.CostEstimate(flops=flops, bytes_accessed=size, transcendentals=transcendentals),
        name=name,
    )(*operands)


def parity(m):
    return (m & 1) ^ ((m >> 1) & 1)


def split_kernel(*refs):
    *parts, left_ref, right_ref, both_ref = refs
    half = left_ref.shape[2]
    for k, part in enumerate(parts):
        for i, ref in enumerate((left_ref, right_ref)):
            piece = part[:, i * half : (i + 1) * half]
            ref[k] = piece
            both_ref[i, k] = piece


def gather_weights(w_uvqk, w_out, w_in, ffn_gain, sections, dps, mps):
    depth, wide = w_uvqk.shape
    width = w_out.shape[1]
    w_in = jnp.concatenate([w_in, ffn_gain, jnp.zeros((15, w_in.shape[1]), BF16)], axis=0)
    if (sections, mps) != (2, 4) or wide != 4 * width or depth % 128:
        ws = [lax.all_gather(x, "dp", axis=0, tiled=True) for x in (w_uvqk, w_out)]
        blocks = [[w_in]] + [[swap(w_in, "mp", mps, k)] for k in range(1, mps)]

        def place_whole(parts, w_ref, wout_ref):
            w_ref[...] = parts[0][...]
            wout_ref[...] = parts[1][...]

        return place_whole, ws, blocks, 1

    part = depth // 4
    cut = width // 2
    sec, m = lax.axis_index("section"), lax.axis_index("mp")
    share = sec * 2 + parity(m)
    mine = jnp.concatenate(
        [
            lax.dynamic_slice_in_dim(w_uvqk, share * width, width, 1),
            lax.dynamic_slice_in_dim(w_out, share * part, part, 0),
        ],
        axis=0,
    )
    got = [swap(mine, "dp", dps, k) for k in order_of(dps)[1:]]
    size = (len(got), depth + part, cut)
    left, right, both = call(
        split_kernel, "split", got, [(size, BF16), (size, BF16), ((2, *size), BF16)], [], 8, 0, 16 * 1024 * 1024
    )
    others = [swap(left, "mp", mps, 1), swap(right, "mp", mps, 2)]
    parts = [w_uvqk[:, : wide // 2], w_uvqk[:, wide // 2 :], w_out[: depth // 2], w_out[depth // 2 :]]
    parts = parts + [both, *others] + [swap(p, "section", sections, 1) for p in (both, *others)]

    from_x, from_y = swap(w_in, "mp", mps, 1), swap(w_in, "mp", mps, 2)
    middle = w_in.shape[0] // 32 * 16
    diagonal = [swap(from_x[:middle], "mp", mps, 2), swap(from_y[middle:], "mp", mps, 1)]
    blocks = [[w_in], [from_x], [from_y], diagonal]

    def place(parts, w_ref, wout_ref):
        sec, m = lax.axis_index("section"), lax.axis_index("mp")
        for i in range(2):
            w_ref[:depth, i * (wide // 2) : (i + 1) * (wide // 2)] = parts[i][...]
            wout_ref[i * (depth // 2) : (i + 1) * (depth // 2)] = parts[2 + i][...]
        for i, ref in enumerate(parts[4:]):
            other_sec, what = i // 3, i % 3
            owner = (sec ^ other_sec) * 2 + (parity(m) ^ (what > 0))
            for side in (0, 1) if what == 0 else (what - 1,):
                at = side * cut
                cols = pl.ds(pl.multiple_of(owner * width + at, cut), cut)
                for k in range(dps - 1):
                    piece = ref[side, k] if what == 0 else ref[k]
                    row = (k + 1) * depth
                    w_ref[row : row + depth, cols] = piece[:depth]
                    rows = pl.ds(pl.multiple_of(row + owner * part, part), part)
                    wout_ref[rows, at : at + cut] = piece[depth:]

    return place, parts, blocks, dps


def two_terms(square):
    hi = square.astype(BF16).astype(F32)
    lane = lax.broadcasted_iota(jnp.int32, (square.shape[0], 128), 1)
    return jnp.where(lane == 0, hi, jnp.where(lane == 1, square - hi, 0.0)).astype(BF16)


def up_kernel(chunks, pieces, x_ref, *refs):
    w_in_refs, refs = refs[: sum(pieces)], refs[sum(pieces) :]
    w_ref, local_ref, half_ref, send_ref, normed_ref = refs
    m = lax.axis_index("mp")
    depth = x_ref.shape[1]
    x = x_ref[...]
    square = None
    at = 0
    for k, n in enumerate(pieces):
        block = jnp.concatenate([r[...] for r in w_in_refs[at : at + n]], axis=0)
        at += n
        hidden = jnp.dot(x, block[:depth], preferred_element_type=F32)
        part = jnp.sum(hidden * hidden, axis=1, keepdims=True)
        square = part if square is None else square + part
        gain = block[depth:].astype(F32)[:1]
        cols = hidden.shape[1]
        normed_ref[:, pl.ds(pl.multiple_of((m ^ k) * cols, cols), cols)] = (hidden * gain).astype(BF16)
        if k == 0:
            local_ref[...] = hidden
    normed = normed_ref[...]
    wide = w_ref.shape[1]
    each = wide // chunks
    for c in range(chunks):
        at = slice(c * each, (c + 1) * each)
        half = jnp.dot(normed, w_ref[:, at], preferred_element_type=F32)
        half_ref[:, at] = half
        send_ref[:, at] = half.astype(BF16)
    half_ref[:, wide:] = jnp.broadcast_to(square, (x.shape[0], 128))
    send_ref[:, wide:] = two_terms(square)


def down_kernel(chunks, sections, mps, take, half_ref, other_ref, local_ref, w_ref, _, own_ref, *refs):
    *send_refs, part_ref = refs
    units, wide = w_ref.shape
    each = wide // chunks
    square = half_ref[:, units : units + 1] + jnp.sum(other_ref[:, units:].astype(F32), axis=1, keepdims=True)
    inv = lax.rsqrt(square / DM + EPSILON)
    up = (half_ref[:, :units] + other_ref[:, :units].astype(F32)) * inv
    hidden = jax.nn.gelu(up, approximate=True).astype(BF16)
    for c in range(chunks):
        at = slice(c * each, (c + 1) * each)
        part_ref[:, at] = jnp.dot(hidden, w_ref[:, at], preferred_element_type=F32)
    m = lax.axis_index("mp")
    cols = local_ref.shape[1]
    own = pl.ds(pl.multiple_of(m * cols, cols), cols)
    part_ref[:, own] = part_ref[:, own] + local_ref[...]
    for k, ref in enumerate([own_ref, *send_refs]):
        starts = [pl.multiple_of((s * mps + (m ^ k)) * take, take) for s in range(sections)]
        mine = [part_ref[pl.ds(start, take), :] for start in starts]
        ref[...] = jnp.concatenate(mine, axis=0).astype(ref.dtype)


def add_kernel(own_ref, *refs):
    *got_refs, _, keep_ref, send_ref, total_ref = refs
    total = own_ref[...]
    for ref in got_refs:
        total = total + ref[...].astype(F32)
    total_ref[...] = total
    sec = lax.axis_index("section")
    take = keep_ref.shape[0]
    keep_ref[...] = total_ref[pl.ds(pl.multiple_of(sec * take, take), take), :]
    send_ref[...] = total_ref[pl.ds(pl.multiple_of((1 - sec) * take, take), take), :]


def finish_kernel(keep_ref, got_ref, out_ref):
    sec = lax.axis_index("section")
    wide = keep_ref.shape[1]
    out_ref[:, pl.ds(pl.multiple_of(sec * wide, wide), wide)] = keep_ref[...].astype(BF16)
    out_ref[:, pl.ds(pl.multiple_of((1 - sec) * wide, wide), wide)] = got_ref[...].astype(BF16)


def per_device(sections, dps, mps, events, hist_len, sess_len, w_uvqk, w_out, attn_gain, w_in, ffn_gain, w_up, w_down):
    events = events[0]
    length, width = events.shape
    sess = sess_len.shape[1]
    take = sess // MICRO
    peers = sections * mps
    rows = take * peers
    cols = w_in.shape[1]
    units = w_up.shape[1]
    half_width = w_down.shape[1]
    group = ("section", "mp")
    first = take * SESS_MAX
    rest = length - first

    gain = jnp.broadcast_to(attn_gain, (8, width))
    ends = jnp.sum(jnp.where(jnp.tri(sess, dtype=jnp.bool_), sess_len, 0), axis=1)
    bounds = jnp.stack([ends - sess_len[0], jnp.minimum(ends, hist_len), jnp.broadcast_to(hist_len, ends.shape)])
    bounds = jnp.broadcast_to(bounds.astype(F32)[:, :, None], (3, sess, 128))
    place, parts, w_in_blocks, dps = gather_weights(w_uvqk, w_out, w_in, ffn_gain, sections, dps, mps)

    micro_rows, full_w, full_wout, kv_first, sums_ev, sums_g = call(
        functools.partial(first_kernel, place, dps, (peers, take), len(parts)),
        "encode_first",
        [bounds, events[:first], gain, *parts],
        [
            ((rows, width), BF16),
            ((width, 4 * width), BF16),
            ((width, width), BF16),
            ((first, 2 * width), BF16),
            ((sess, width), F32),
            ((sess, width), F32),
        ],
        [
            pltpu.VMEM((first, width), BF16),
            pltpu.VMEM((first, width), F32),
            pltpu.VMEM((first, width), F32),
        ],
        16,
        8 * first * width * width + 2 * first * first * width,
        6 * 1024 * 1024,
        4 * first * width + HEADS * first * first,
    )
    arrived = lax.all_to_all(
        micro_rows.reshape(peers, take, width), group, split_axis=0, concat_axis=0, tiled=True
    ).reshape(rows, width)
    blocks = [piece for block in w_in_blocks for piece in block]
    local, half, half_send = call(
        functools.partial(up_kernel, 1, [len(block) for block in w_in_blocks]),
        "up_half",
        [arrived, *blocks, w_up],
        [((rows, cols), F32), ((rows, units + 128), F32), ((rows, units + 128), BF16)],
        [pltpu.VMEM((rows, w_up.shape[0]), BF16)],
        10,
        2 * rows * w_up.size,
        2 * w_up.size,
    )
    other = swap(half_send, "section", sections, 1)
    queries_gate, kv_rest, sums_ev = call(
        functools.partial(project_kernel, dps, first),
        "project_rest",
        [bounds, events[first:], full_w, sums_ev, local],
        [((rest, 2 * width), BF16), ((rest, 2 * width), BF16), ((sess, width), F32)],
        [],
        10,
        8 * rest * width * width,
        6 * 1024 * 1024,
        4 * rest * width,
    )
    pair = sections * take
    own, *sends = call(
        functools.partial(down_kernel, 4, sections, mps, take),
        "down_part",
        [half, other, local, w_down, sums_ev],
        [((pair, half_width), F32)] + [((pair, half_width), BF16)] * (mps - 1),
        [pltpu.VMEM((rows, half_width), F32)],
        8,
        2 * rows * w_down.size,
        2 * w_down.size,
        rows * units,
    )

    got = [swap(sends[k - 1], "mp", mps, k) for k in range(mps - 1, 0, -1)]
    (sums_g,) = call(
        functools.partial(attend_kernel, first),
        "attend_rest",
        [bounds, gain, queries_gate, kv_first, kv_rest, sums_g, own],
        [((sess, width), F32)],
        [pltpu.VMEM((rest, width), F32)],
        10,
        4 * rest * length * width,
        4 * 1024 * 1024,
        HEADS * rest * length,
    )
    keep, send = call(
        add_kernel,
        "add_parts",
        [own, *got, sums_g],
        [((take, half_width), F32)] * 2,
        [pltpu.VMEM((pair, half_width), F32)],
        8,
        mps * pair * half_width,
        2 * mps * pair * half_width,
    )
    got = swap(send, "section", sections, 1)
    (pooled,) = call(
        functools.partial(pool_kernel, dps),
        "pool_rows",
        [bounds, sums_ev, sums_g, full_wout, keep],
        [((sess, width), BF16)],
        [],
        8,
        6 * sess * width * width,
        1024 * 1024,
    )
    (cross_out,) = call(
        finish_kernel,
        "finish",
        [keep, got],
        [((take, half_width * sections), BF16)],
        [],
        8,
        0,
        16 * take * half_width,
    )
    return (pooled, cross_out)


def solution(mesh):
    sizes = [mesh.shape[name] for name in ("section", "dp", "mp")]
    return jax.shard_map(
        functools.partial(per_device, *sizes),
        mesh=mesh,
        in_specs=(
            P(("section", "dp", "mp"), None, None),
            P(("section", "dp", "mp")),
            P(("section", "dp", "mp"), None),
            P("dp", None),
            P("dp", None),
            P(),
            P(None, ("section", "mp")),
            P(None, ("section", "mp")),
            P("section", "mp"),
            P("mp", "section"),
        ),
        out_specs=(P(("section", "dp", "mp"), None), P(("section", "dp", "mp"), None)),
        check_vma=False,
    )
```
